128 devices in a mesh: dp: 4 (over y_hi, core), fsdp: 32 (over z, y_lo, x).
Axes of the slice: x: 4, y: 4 (y_hi: 2, y_lo: 2; y = y_hi * 2 + y_lo), z: 4, core: 2. Of those that a mesh axis runs over, the one named last changes fastest.
Arguments:
- images: bfloat16 [512, 16, 16, 512], P(('dp', 'fsdp')), may hold values from -6 to 6
- routes: int32 [512, 1], P(('dp', 'fsdp')), may hold values from 0 to 3; in each aligned block of 4 rows (0 to 3, 4 to 7, ...) at most 2 rows name the same one
- bucket: int32 [512], P(('dp', 'fsdp')), may hold values from 0 to 7
- heights: int32 [8], replicated, may hold values from 8 to 16, as said below
- widths: int32 [8], replicated, may hold values from 8 to 16, as said below
- w_conv: bfloat16 [512, 9, 512], P('fsdp'), may hold values from -0.09375 to 0.09375
- w_down: bfloat16 [2048, 512], P('fsdp'), may hold values from -0.125 to 0.125
- w_up: bfloat16 [512, 2048], P('fsdp'), may hold values from -0.25 to 0.25
- norm_gain: float32 [512], replicated, may hold values from 0.1 to 1.9
- norm_shift: float32 [512], replicated, may hold values from -3 to 3
- cotangent: bfloat16 [1024, 16, 16, 512], P(('dp', 'fsdp')), may hold values from -6 to 6
Outputs:
- block_out: float32 [1024, 16, 16, 512], P(('dp', 'fsdp'))
- grad_conv: float32 [512, 9, 512], P('fsdp')
- grad_down: float32 [2048, 512], P('fsdp')
- grad_up: float32 [512, 2048], P('fsdp')
The draws below stay inside these ranges and needn't reach their ends.
Inputs may be any that keep to these rules, and one draw needn't show every extreme that they name: Even heights; one bucket is 16 high and one is 8 high. Even widths; one bucket is 16 wide and one is 8 wide. `routes`: the rows of one device name one owner at most 2 times.
All inputs are finite; a program needn't handle non-finite values.
Results may differ from the reference program's by a relative error of at most 0.0052.
Values may be sent and summed in bfloat16 or wider, within the bound.
No kernel may reach another device: no remote copies, remote signals or barrier semaphores. Data moves between devices by JAX's collectives and lax.ppermute only.
A program may use at most 128 MiB of HBM per device.

```python
import math
import jax
import jax.numpy as jnp
import numpy as np
from jax import lax

C = 512
GROUPS = 32
S = 16
NB = 8
IMG_DEV = 4
MOST = 2
SLOTS = 8
IMGS = 512
RECV = 1024
N_DP = 4
N_FSDP = 32


def draw_heights(key, part):
    key = jax.random.fold_in(key, 11)
    offsets = jax.random.randint(key, (NB,), 0, S // 4 + 1)
    values = S // 2 + 2 * offsets
    values = values.at[0].set(S).at[1].set(S // 2)
    return values.astype(jnp.int32)


def draw_widths(key, part):
    key = jax.random.fold_in(key, 12)
    offsets = jax.random.randint(key, (NB,), 0, S // 4 + 1)
    values = S // 2 + 2 * offsets
    values = values.at[0].set(S // 2).at[1].set(S)
    return values.astype(jnp.int32)


def place_ends(entries, own_key, low, top_value):
    place = [jax.random.randint(jax.random.fold_in(own_key, axis), (), 0, length) for axis, length in enumerate(entries.shape)]
    widest = entries.shape.index(max(entries.shape))
    neighbour = place[:widest] + [(place[widest] + 1) % entries.shape[widest]] + place[widest + 1:]
    return entries.at[tuple(place)].set(low).at[tuple(neighbour)].set(top_value)


def steps_of(rng, shape, pieces, least, high):
    level = 1.0
    for dim, shards_of in pieces:
        draws = jax.random.uniform(jax.random.fold_in(jax.random.fold_in(rng, 6), dim), (shards_of,), jnp.float32, least / len(pieces), high / len(pieces))
        level = level * jnp.repeat(jnp.exp(draws), shape[dim] // shards_of).reshape((-1,) + (1,) * (len(shape) - 1 - dim))
    return level


def assign_block(key, own, number, rows, amount, top, bound, lean):
    ranking = jax.random.permutation(key, amount)
    heavy_load, common = load_shares(amount, rows * top, bound, lean, True), load_shares(amount, rows * top, bound, lean, False)
    places = jnp.arange(amount)

    def named(lengths, turn):
        used = int((lengths > 0).sum())
        fixed = max(1, used // 4)
        passed = fixed + (places - fixed + turn * (used - fixed)) % max(1, amount - fixed)
        return jnp.zeros((amount,), jnp.int32).at[ranking[jnp.where(places < fixed, places, passed)]].set(jnp.asarray(lengths, jnp.int32))

    lengths = jnp.where(number % 4 == 0, named(heavy_load, number // 4), named(common, number - number // 4 - 1))
    mixed = jax.random.permutation(jax.random.fold_in(own, 3), amount)
    donor, receiver = mixed[0:amount // 2 * 2:2], mixed[1:amount // 2 * 2:2]
    slack = jnp.minimum(lengths[donor] - 1, bound - lengths[receiver]) // 2
    slack = jnp.where((donor == ranking[0]) | (receiver == ranking[0]) | (lengths[receiver] == 0), 0, jnp.maximum(slack, 0))
    passed = jax.random.randint(jax.random.fold_in(own, 4), (amount // 2,), 0, 1 << 20) % (slack + 1)
    lengths = lengths.at[donor].add(-passed).at[receiver].add(passed)
    labels = jnp.searchsorted(jnp.cumsum(lengths), jnp.arange(rows * top), side="right").astype(jnp.int32)
    grid = labels.reshape(top, rows).T
    grid = grid[jax.random.permutation(jax.random.fold_in(own, 1), rows)]
    turn = jax.random.randint(jax.random.fold_in(own, 2), (rows, 1), 0, top)
    return jnp.take_along_axis(grid, (jnp.arange(top)[None, :] + turn) % top, axis=1)


def load_shares(count, total, limit, lean, full):
    weights = [(1 << 20) // math.isqrt(standing ** lean) + 1 for standing in range(1, count + 1)]
    largest = limit if full else min(limit, max(-(-total // count), total * weights[0] // sum(weights)))
    least = 1 if total - largest >= count - 1 else 0
    given, rest = [largest] + [least] * (count - 1), total - largest - least * (count - 1)
    while rest > 0:
        free = [i for i in range(1, count) if given[i] < largest] or [i for i in range(1, count) if given[i] < limit]
        pool, remaining = sum([weights[i] for i in free]), rest
        for i in free:
            addition = min(limit - given[i], max(1, remaining * weights[i] // pool), rest)
            given[i] = given[i] + addition
            rest = rest - addition
    return np.array(given)


def gaussian(stream_key, dims, scale, reach, split=(), kind=jnp.bfloat16):
    drawn = scale * jax.random.normal(stream_key, dims, jnp.float32)
    if split:
        drawn = drawn * steps_of(stream_key, dims, split, -0.22, 0.18)
    return jnp.clip(drawn, -reach, reach).astype(kind)


def setup_inputs(seed: int = 0) -> dict:
    keys = jax.random.split(jax.random.key(seed), 12)
    images = gaussian(keys[0], (IMGS, S, S, C), 1.0, 6.0, ((0, 128),))
    routes_keys = jax.random.split(jax.random.fold_in(keys[1], 1), IMGS // IMG_DEV)
    routes_turns = jax.random.permutation(jax.random.fold_in(keys[1], 3), IMGS // IMG_DEV)
    routes = jax.vmap(lambda own, number: assign_block(jax.random.fold_in(keys[1], 2), own, number, IMG_DEV, N_DP, 1, MOST, 1))(routes_keys, routes_turns).reshape((IMGS, 1))
    bucket = place_ends(jax.random.randint(keys[2], (IMGS,), 0, NB), jax.random.fold_in(keys[2], 1), 0, NB - 1).astype(jnp.int32)
    heights = draw_heights(jax.random.fold_in(keys[11], 71), 0)
    widths = draw_widths(jax.random.fold_in(keys[11], 71), 0)
    w_conv = gaussian(keys[5], (C, 9, C), (9 * C) ** -0.5, 0.09375, ((0, 32),))
    w_down = gaussian(keys[6], (4 * C, C), (4 * C) ** -0.5, 0.125, ((0, 32),))
    w_up = gaussian(keys[7], (C, 4 * C), C ** -0.5, 0.25, ((0, 32),))
    norm_gain = jnp.clip(1.0 + 0.18 * jax.random.normal(keys[8], (C,), jnp.float32), 0.1, 1.9)
    norm_shift = gaussian(keys[9], (C,), 0.5, 3.0, (), jnp.float32)
    cotangent = gaussian(keys[10], (RECV, S, S, C), 1.0, 6.0, ((0, 128),))
    return {"images": images, "routes": routes, "bucket": bucket, "heights": heights, "widths": widths, "w_conv": w_conv, "w_down": w_down, "w_up": w_up, "norm_gain": norm_gain, "norm_shift": norm_shift, "cotangent": cotangent}


epsilon = 1e-05

def make_masks(slot_ids, heights, widths, extent):
    bucket_ids = jnp.arange(heights.shape[0], dtype=jnp.int32)
    chosen = (slot_ids[:, None] == bucket_ids[None, :]).astype(jnp.int32)
    heights_of = lax.optimization_barrier(jnp.sum(chosen * heights[None, :], axis=1))
    widths_of = lax.optimization_barrier(jnp.sum(chosen * widths[None, :], axis=1))
    position = jnp.arange(extent, dtype=jnp.int32)
    inside = (position[None, :, None] < heights_of[:, None, None]) & (position[None, None, :] < widths_of[:, None, None])
    return inside.astype(jnp.float32)[..., None]

def space_to_depth(values):
    batch, extent, _, channels = values.shape
    values = values.reshape(batch, extent // 2, 2, extent // 2, 2, channels).transpose(0, 1, 3, 2, 4, 5)
    return values.reshape(batch, extent // 2, extent // 2, 4 * channels)

def depth_to_space(values):
    batch, half, _, folded = values.shape
    channels = folded // 4
    values = values.reshape(batch, half, half, 2, 2, channels).transpose(0, 1, 3, 2, 4, 5)
    return values.reshape(batch, 2 * half, 2 * half, channels)

def group_stats(values, masks):
    batch = values.shape[0]
    channels = values.shape[-1]
    group_width = channels // GROUPS
    counted = jnp.maximum(lax.optimization_barrier(jnp.sum(masks, axis=(1, 2, 3))) * group_width, 1.0)
    per_chan = lax.optimization_barrier(jnp.sum(values * masks, axis=(1, 2)))
    centre = lax.optimization_barrier(jnp.sum(per_chan.reshape(batch, GROUPS, group_width), axis=2)) / counted[:, None]
    mean_chan = jnp.repeat(centre, group_width, axis=1)
    centred = (values - mean_chan[:, None, None, :]) * masks
    squares = lax.optimization_barrier(jnp.sum(centred * centred, axis=(1, 2))).reshape(batch, GROUPS, group_width)
    variance = lax.optimization_barrier(jnp.sum(squares, axis=2)) / counted[:, None]
    inverse = lax.rsqrt(variance + epsilon)
    return (mean_chan, jnp.repeat(inverse, group_width, axis=1))

def contract_rows(left, right):
    return lax.dot_general(left, right, (((0,), (0,)), ((), ())), preferred_element_type=jnp.float32)

def block_pass(slabs, masks, cot_slabs, w_conv, w_down, w_up, norm_gain, norm_shift, loss_scale):
    batch, extent, _, channels = slabs.shape
    half = extent // 2
    inputs = slabs.astype(jnp.float32)
    mean_chan, inv_chan = group_stats(inputs, masks)
    normed = (inputs - mean_chan[:, None, None, :]) * inv_chan[:, None, None, :] * norm_gain + norm_shift
    activated = (jax.nn.silu(normed) * masks).astype(jnp.bfloat16)
    padded = jnp.pad(activated, ((0, 0), (1, 1), (1, 1), (0, 0)))
    windows = [padded[:, row_off:row_off + extent, col_off:col_off + extent, :].reshape(-1, channels) for row_off in range(3) for col_off in range(3)]
    convolved = jnp.zeros((batch * extent * extent, channels), jnp.float32)
    for tap in range(9):
        convolved = convolved + jnp.dot(windows[tap], w_conv[:, tap, :], preferred_element_type=jnp.float32)
    convolved = convolved.reshape(batch, extent, extent, channels)
    skip_wide = (inputs + convolved) * masks
    skipped = skip_wide.astype(jnp.bfloat16)
    folded = space_to_depth(skipped).reshape(-1, 4 * channels)
    lowered = jnp.dot(folded, w_down, preferred_element_type=jnp.float32).astype(jnp.bfloat16)
    raised = jnp.dot(lowered, w_up, preferred_element_type=jnp.float32).reshape(batch, half, half, 4 * channels)
    outputs = (skip_wide + depth_to_space(raised)) * masks
    grad_out = cot_slabs.astype(jnp.float32) * masks * loss_scale
    grad_rounded = grad_out.astype(jnp.bfloat16)
    grad_folded = space_to_depth(grad_rounded).reshape(-1, 4 * channels)
    grad_up = contract_rows(lowered, grad_folded)
    grad_low = lax.dot_general(grad_folded, w_up, (((1,), (1,)), ((), ())), preferred_element_type=jnp.float32).astype(jnp.bfloat16)
    grad_down = contract_rows(folded, grad_low)
    returned_grad = lax.dot_general(grad_low, w_down, (((1,), (1,)), ((), ())), preferred_element_type=jnp.float32).reshape(batch, half, half, 4 * channels)
    grad_skip = ((grad_out + depth_to_space(returned_grad)) * masks).astype(jnp.bfloat16).reshape(-1, channels)
    grad_conv = jnp.stack([contract_rows(windows[tap], grad_skip) for tap in range(9)], axis=1)
    return (outputs, grad_conv, grad_down, grad_up)

def reference(images, routes, bucket, heights, widths, w_conv, w_down, w_up, norm_gain, norm_shift, cotangent):
    devices_all = N_DP * N_FSDP
    target = routes[:, 0].reshape(devices_all, IMG_DEV)
    position = jnp.arange(IMG_DEV, dtype=jnp.int32)
    earlier = position[None, :] < position[:, None]
    same_owner = target[:, :, None] == target[:, None, :]
    order_in = lax.optimization_barrier(jnp.sum((same_owner & earlier[None]).astype(jnp.int32), axis=2))
    device_ids = jnp.arange(devices_all, dtype=jnp.int32)
    source_dp = device_ids // N_FSDP
    source_fsdp = device_ids % N_FSDP
    destination = (target * N_FSDP + source_fsdp[:, None]) * SLOTS + source_dp[:, None] * MOST + order_in
    destination = destination.reshape(-1).astype(jnp.int32)
    own_cot = cotangent[destination]
    loss_scale = 1.0 / math.sqrt(IMGS * S * S)

    def step_fn(carry, block):
        slabs, slot_ids, cot_block = block
        masks = make_masks(slot_ids, heights, widths, S)
        produced, part_conv, part_down, part_up = block_pass(slabs, masks, cot_block, w_conv, w_down, w_up, norm_gain, norm_shift, loss_scale)
        return ((carry[0] + part_conv, carry[1] + part_down, carry[2] + part_up), produced)
    initial = (jnp.zeros((C, 9, C), jnp.float32), jnp.zeros((4 * C, C), jnp.float32), jnp.zeros((C, 4 * C), jnp.float32))
    blocks = (images.reshape(devices_all, IMG_DEV, S, S, C), bucket.reshape(devices_all, IMG_DEV), own_cot.reshape(devices_all, IMG_DEV, S, S, C))
    totals, produced = lax.scan(step_fn, initial, blocks)
    block_out = jnp.zeros((RECV, S, S, C), jnp.float32).at[destination].set(produced.reshape(IMGS, S, S, C))
    return (block_out, totals[0], totals[1], totals[2])
```

```python
import functools
import math

import jax
import jax.numpy as jnp
from jax import lax
from jax.experimental import pallas as pl
from jax.experimental.pallas import tpu as pltpu
from jax.sharding import PartitionSpec as P

GROUPS = 32
epsilon = 1e-05
BF = jnp.bfloat16
F32 = jnp.float32
I32 = jnp.int32
AXES = ("dp", "fsdp")
VMEM_BYTES = 56 * 1024 * 1024


def moved(fn):
    pairs = []
    for index in range(128):
        dp, fsdp = index // 32, index % 32
        place = (dp // 2, dp % 2, fsdp // 8, fsdp // 4 % 2, fsdp % 4)
        h, c, z, y, x = fn(*place)
        pairs.append((index, (h * 2 + c) * 32 + z * 8 + y * 4 + x))
    return pairs


STEP = {
    "y": moved(lambda h, c, z, y, x: (h, c, z, 1 - y, x)),
    "hy": moved(lambda h, c, z, y, x: (1 - h, c, z, 1 - y, x)),
    "c": moved(lambda h, c, z, y, x: (h, 1 - c, z, y, x)),
    "h": moved(lambda h, c, z, y, x: (1 - h, c, z, y, x)),
    "hc": moved(lambda h, c, z, y, x: (1 - h, 1 - c, z, y, x)),
}
PLANES = [[z * 8 + y * 4 + x for z in range(4) for x in range(4)] for y in range(2)]


def send(value, move):
    return lax.ppermute(value, AXES, STEP[move])


def over_dp(blocks):
    own, beside, across, both = blocks
    return (own, send(beside, "c"), send(across, "h"), send(both, "hc"))


def over_column(parts, y):
    kept = lax.dynamic_index_in_dim(parts, y, axis=0, keepdims=False)
    given = lax.dynamic_index_in_dim(parts, 1 - y, axis=0, keepdims=False)
    sent = given.astype(BF)
    got = (send(sent, "y"), send(kept.astype(BF), "h"), send(sent, "hy"))
    total = kept + got[0].astype(F32) + got[1].astype(F32) + got[2].astype(F32)
    return total, send(total, "c")


def over_plane(blocks):
    return lax.all_to_all(
        blocks, "fsdp", split_axis=0, concat_axis=0, axis_index_groups=PLANES, tiled=True
    )


def dot(left, right, left_dim, right_dim):
    return lax.dot_general(
        left, right, (((left_dim,), (right_dim,)), ((), ())), preferred_element_type=F32
    )


def kernel_call(body, out_shape, flops, moved_bytes, scratch=(), **more):
    return pl.pallas_call(
        body,
        out_shape=out_shape,
        scratch_shapes=list(scratch),
        compiler_params=pltpu.CompilerParams(vmem_limit_bytes=VMEM_BYTES),
        cost_estimate=pl.CostEstimate(
            flops=int(flops), bytes_accessed=int(moved_bytes), transcendentals=0
        ),
        **more,
    )


def laned(extent_rows, extent_columns, lanes):
    block = min(128, lanes)
    return pltpu.VMEM((lanes // block, extent_rows, extent_columns, block), F32)


def put_line(ref, row, first, values):
    block = ref.shape[3]
    for b in range(ref.shape[0]):
        ref[b, row, first : first + values.shape[0], :] = values[:, b * block : (b + 1) * block]


def get_line(ref, row):
    return jnp.concatenate([ref[b, row] for b in range(ref.shape[0])], axis=1)


def every_second(ref, row, first, side):
    places = [
        ref[pl.ds(b, 1), pl.ds(row, 1), pl.ds(first, side, stride=2), :].reshape(side, ref.shape[3])
        for b in range(ref.shape[0])
    ]
    return jnp.concatenate(places, axis=1)


def put_every_second(ref, row, first, values):
    side, block = values.shape[0], ref.shape[3]
    for b in range(ref.shape[0]):
        ref[pl.ds(b, 1), pl.ds(row, 1), pl.ds(first, side, stride=2), :] = values[
            :, b * block : (b + 1) * block
        ].reshape(1, 1, side, block)


WHOLE = pl.BlockSpec(memory_space=pltpu.VMEM)
SCALARS = pl.BlockSpec(memory_space=pltpu.SMEM)


def over_group(sums, width):
    lane = lax.broadcasted_iota(I32, sums.shape, 1)
    step = width // 2
    while step:
        lower = (lane & step) == 0
        lanes = sums.shape[1]
        sums = sums + jnp.where(
            lower, pltpu.roll(sums, lanes - step, 1), pltpu.roll(sums, step, 1)
        )
        step //= 2
    return sums


def norm_kernel(extent, meta, image, gain, shift, windows, residual, padded, raw):
    place = pl.program_id(0)
    channels = image.shape[2]
    half = channels // 2
    height, width = meta[place], meta[8 + place]
    core = meta[24]

    @pl.when(place == 0)
    def _():
        padded[...] = jnp.zeros_like(padded)

    inside = lax.broadcasted_iota(I32, (extent, channels), 0) < width

    def line(row):
        return image[0, row * extent : (row + 1) * extent, :].astype(F32)

    def mask(row):
        return (inside & (row < height)).astype(F32)

    group = channels // GROUPS
    counted = jnp.maximum((height * width * group).astype(F32), 1.0)
    total = jnp.zeros((extent, channels), F32)
    for row in range(extent):
        total = total + line(row) * mask(row)
    total = jnp.broadcast_to(jnp.sum(total, axis=0, keepdims=True), (8, channels))
    mean = (over_group(total, group) / counted)[:1]
    total = jnp.zeros((extent, channels), F32)
    for row in range(extent):
        centred = (line(row) - mean) * mask(row)
        total = total + centred * centred
    total = jnp.broadcast_to(jnp.sum(total, axis=0, keepdims=True), (8, channels))
    variance = (over_group(total, group) / counted)[:1]
    scale = lax.rsqrt(variance + epsilon) * gain[...]
    for row in range(extent):
        normed = (line(row) - mean) * scale + shift[...]
        put_line(padded, row + 1, 8, normed / (1.0 + jnp.exp(-normed)) * mask(row))
        residue = image[
            0, row * extent : (row + 1) * extent, pl.ds(pl.multiple_of(core * half, half), half)
        ]
        put_line(raw, row, 0, residue.astype(F32))
    side = extent // 2
    for p in range(4):
        for q in range(4):
            for i in range(0, side, 2):
                pair = [every_second(padded, 2 * n + p, 7 + q, side) for n in (i, i + 1)]
                windows[p * 4 + q, i * side : (i + 2) * side, :] = jnp.concatenate(pair).astype(BF)
    for k in range(4):
        for i in range(0, side, 2):
            pair = [every_second(raw, 2 * n + k // 2, k % 2, side) for n in (i, i + 1)]
            residual[k, i * side : (i + 2) * side, :] = jnp.concatenate(pair).astype(BF)


def normed_windows(meta, images, gain, shift):
    count, extent, _, channels = images.shape
    pixels, half = extent * extent, channels // 2
    quarter = pixels // 4
    return kernel_call(
        functools.partial(norm_kernel, extent),
        (
            jax.ShapeDtypeStruct((16, count * quarter, channels), BF),
            jax.ShapeDtypeStruct((4, count * quarter, half), BF),
        ),
        flops=40 * images.size,
        moved_bytes=12 * images.size,
        scratch=(
            laned(extent + 2, extent + 16, channels),
            laned(extent, extent, half),
        ),
        grid=(count,),
        in_specs=[
            SCALARS,
            pl.BlockSpec((1, pixels, channels), lambda g: (g, 0, 0)),
            pl.BlockSpec((1, channels), lambda g: (0, 0)),
            pl.BlockSpec((1, channels), lambda g: (0, 0)),
        ],
        out_specs=(
            pl.BlockSpec((16, quarter, channels), lambda g: (0, g, 0)),
            pl.BlockSpec((4, quarter, half), lambda g: (0, g, 0)),
        ),
    )(meta, images.reshape(count, pixels, channels), gain[None, :], shift[None, :])


def gather_up(pieces, up):
    rows = pieces.shape[2]
    for f in range(32):
        z, y, x = f // 8, f // 4 % 2, f % 4
        for k in range(4):
            up[k, f * rows : (f + 1) * rows, :] = pieces[z * 4 + x, y * 4 + k]


def gather_down(pieces, down):
    rows, half = pieces.shape[2:]
    for z in range(4):
        for x in range(4):
            for unit in range(8):
                side, step = unit // 4, unit % 4
                first = (x * 4 + step) * rows
                down[z, first : first + rows, side * half : (side + 1) * half] = pieces[
                    z * 4 + x, 8 + unit
                ]


def swapped_sum(own, got):
    middle = own.shape[0] // 2
    return jnp.concatenate(
        [own[:middle] + got[middle:], own[middle:] + got[:middle]], axis=0
    ).astype(BF)


def glow_kernel(
    extent, loss_scale, meta, cot0, cot1, cot2, cot3, pieces, folded, part, raw, up, cot, sem
):
    side = extent // 2
    quarter = side * side
    half = cot.shape[2]
    slots = cot0.shape[0]
    copies = [
        pltpu.make_async_copy(ref, cot.at[pl.ds(r * slots, slots)], sem.at[r])
        for r, ref in enumerate((cot0, cot1, cot2, cot3))
    ]
    for copy in copies:
        copy.start()
    gather_up(pieces, up)
    for copy in copies:
        copy.wait()
    images = folded.shape[1] // quarter
    inside = lax.broadcasted_iota(I32, (extent, half), 0)

    def one(g, carry):
        height, width, slot = meta[g], meta[8 + g], meta[16 + g]
        for row in range(extent):
            kept = ((inside < width) & (row < height)).astype(F32)
            line = cot[slot, row * extent : (row + 1) * extent, :].astype(F32)
            put_line(raw, row, 0, line * kept)
        for k in range(4):
            for i in range(0, side, 2):
                pair = [every_second(raw, 2 * n + k // 2, k % 2, side) for n in (i, i + 1)]
                first = pl.multiple_of(g * quarter + i * side, 2 * side)
                folded[k, pl.ds(first, 2 * side), :] = jnp.concatenate(pair).astype(BF)
        return carry

    lax.fori_loop(0, images, one, 0)
    total = None
    for k in range(4):
        scaled = (folded[k].astype(F32) * loss_scale).astype(BF)
        term = dot(scaled, up[k], 1, 1)
        total = term if total is None else total + term
    part[...] = total


def grad_conv_kernel(
    loss_scale, mask, own, got, folded, pieces, windows_own, windows_pair, glow, grads, down, turned
):
    half = folded.shape[2]
    rows = grads.shape[2]
    middle = folded.shape[1] // 2
    gather_down(pieces, down)
    glow[...] = swapped_sum(own, got)
    kept = jnp.concatenate([mask[...]] * (half // mask.shape[1]), axis=1)
    for k in range(4):
        grad = folded[k].astype(F32) * loss_scale + dot(glow[...], down[k], 1, 1)
        turned[k] = (grad * kept).T.astype(BF)
    for t in range(9):
        total = None
        for k in range(4):
            v = (k // 2 + t // 3) * 4 + k % 2 + t % 3
            for columns, windows in ((slice(0, middle), windows_own), (slice(middle, None), windows_pair)):
                term = dot(turned[k, :, columns], windows[v], 1, 0)
                total = term if total is None else total + term
        total = total.T.astype(BF)
        for f in range(32):
            z, y, x = f // 8, f // 4 % 2, f % 4
            grads[z * 4 + x, y * 9 + t] = total[f * rows : (f + 1) * rows, :]


def conv_kernel(
    mask,
    conv_pieces,
    pieces,
    windows_own,
    windows_pair,
    residual_own,
    residual_pair,
    wide,
    skip,
    part,
    conv,
    down,
):
    half = wide.shape[2]
    rows = conv_pieces.shape[2]
    middle = wide.shape[1] // 2
    for f in range(32):
        z, y, x = f // 8, f // 4 % 2, f % 4
        for t in range(9):
            conv[t, f * rows : (f + 1) * rows, :] = conv_pieces[z * 4 + x, y * 9 + t]
    gather_down(pieces, down)
    total = None
    for k in range(4):
        for first, windows, residual in (
            (0, windows_own, residual_own),
            (middle, windows_pair, residual_pair),
        ):
            convolved = None
            for t in range(9):
                v = (k // 2 + t // 3) * 4 + k % 2 + t % 3
                term = dot(windows[v], conv[t], 1, 0)
                convolved = term if convolved is None else convolved + term
            kept = mask[first : first + middle, :]
            kept = jnp.concatenate([kept] * (half // mask.shape[1]), axis=1)
            masked = (residual[k].astype(F32) + convolved) * kept
            wide[k, first : first + middle, :] = masked
            skip[k, first : first + middle, :] = masked.astype(BF)
        term = dot(skip[k], down[k], 1, 0)
        total = term if total is None else total + term
    part[...] = total


def output_kernel(
    extent,
    loss_scale,
    meta,
    mask,
    own,
    got,
    wide,
    skip,
    glow,
    folded,
    pieces,
    back0,
    back1,
    back2,
    back3,
    grads,
    low,
    up,
    outputs,
    raw,
    returning,
):
    side = extent // 2
    quarter = side * side
    half = wide.shape[2]
    rows = grads.shape[2]
    images = wide.shape[1] // quarter
    gather_up(pieces, up)
    low[...] = swapped_sum(own, got)
    kept = jnp.concatenate([mask[...]] * (half // mask.shape[1]), axis=1)
    for k in range(4):
        outputs[k] = (wide[k] + dot(low[...], up[k], 1, 0)) * kept
    returning[...] = jnp.zeros_like(returning)

    def one(g, carry):
        slot = meta[16 + g]
        for k in range(4):
            for i in range(side):
                first = pl.multiple_of(g * quarter + i * side, side)
                put_every_second(raw, 2 * i + k // 2, k % 2, outputs[k, pl.ds(first, side), :])
        for row in range(extent):
            returning[slot, row * extent : (row + 1) * extent, :] = get_line(raw, row).astype(BF)
        return carry

    lax.fori_loop(0, images, one, 0)
    slots = back0.shape[0]
    for r, back in enumerate((back0, back1, back2, back3)):
        back[...] = returning[r * slots : (r + 1) * slots]
    turned = low[...].astype(F32).T.astype(BF)
    for k in range(4):
        scaled = (folded[k].astype(F32) * loss_scale).astype(BF)
        grad = dot(turned, scaled, 1, 0).astype(BF)
        for f in range(32):
            z, y, x = f // 8, f // 4 % 2, f % 4
            grads[z * 4 + x, y * 4 + k] = grad[f * rows : (f + 1) * rows, :]
        grad = dot(skip[k].astype(F32).T.astype(BF), glow[...], 1, 0).astype(BF)
        for x in range(4):
            for unit in range(8):
                side_of, step = unit // 4, unit % 4
                first = (x * 4 + step) * rows
                grads[k * 4 + x, 8 + unit] = grad[
                    first : first + rows, side_of * half : (side_of + 1) * half
                ]


def replicas(number, half):
    for r in range(4):
        chip, core = number // 2, number % 2
        chip = 1 - chip if r // 2 else chip
        core = 1 - core if r % 2 else core
        yield r, chip, pl.ds(pl.multiple_of(core * half, half), half)


def split_kernel(number, cot, out0, out1, out2, out3):
    outs = (out0, out1, out2, out3)
    slots, _, half = out0.shape
    for r, chip, lanes in replicas(number[0], half):
        outs[r][...] = cot[pl.ds(chip * slots, slots), :, lanes]


def join_kernel(number, back0, back1, back2, back3, out, wide, sem):
    backs = (back0, back1, back2, back3)
    slots, _, half = back0.shape
    copies = []
    for r, chip, lanes in replicas(number[0], half):
        wide[r] = backs[r][...].astype(F32)
        target = out.at[pl.ds(chip * slots, slots), :, lanes]
        copies.append(pltpu.make_async_copy(wide.at[r], target, sem.at[r]))
        copies[-1].start()
    for copy in copies:
        copy.wait()


def per_device(
    images, routes, bucket, heights, widths, w_conv, w_down, w_up, norm_gain, norm_shift, cotangent
):
    count, extent, _, channels = images.shape
    half = channels // 2
    pixels = extent * extent
    quarter = pixels // 4
    most = cotangent.shape[0] // 4
    rows = w_conv.shape[0]
    low_rows = 2 * count * quarter
    loss_scale = 1.0 / math.sqrt(count * 128 * pixels)
    dp, fsdp = lax.axis_index("dp"), lax.axis_index("fsdp")
    core, y = dp % 2, fsdp // 4 % 2

    conv_own = lax.dynamic_slice_in_dim(w_conv, core * half, half, axis=2).transpose(1, 0, 2)
    up_own = lax.dynamic_slice_in_dim(
        w_up.reshape(rows, 4, channels), core * half, half, axis=2
    ).transpose(1, 0, 2)
    down_own = w_down.reshape(4 * rows, 2, half).transpose(1, 0, 2).reshape(8, rows, half)
    packed = jnp.concatenate([up_own, down_own, conv_own])
    other = send(packed, "y")

    block = jax.ShapeDtypeStruct((2 * most, pixels, half), BF)
    number = dp.astype(I32).reshape(1)
    outgoing = kernel_call(
        split_kernel,
        (block,) * 4,
        flops=0,
        moved_bytes=4 * cotangent.size,
        in_specs=[SCALARS, WHOLE],
        out_specs=(WHOLE,) * 4,
    )(number, cotangent.reshape(4 * most, pixels, channels))
    outgoing, other = lax.optimization_barrier((outgoing, other))
    arrived = over_dp(outgoing)
    first = jnp.where(y == 0, packed, other)
    second = jnp.where(y == 0, other, packed)
    down_kept = jnp.where(core == 0, first[4:12], second[4:12])
    up_down = jnp.concatenate([first[:4], second[:4], down_kept])
    conv_two = jnp.concatenate([first[12:], second[12:]])
    up_down = over_plane(jnp.broadcast_to(up_down, (16, *up_down.shape)))
    conv_two = lax.all_gather(conv_two, "fsdp", axis_index_groups=PLANES)

    images_pair = send(images, "c")
    ids = jnp.concatenate([routes, bucket[:, None]], axis=1)
    ids_pair = send(ids, "c")

    def described(table, side):
        target = table[:, 0]
        position = jnp.arange(count, dtype=I32)
        earlier = position[None, :] < position[:, None]
        same_owner = target[:, None] == target[None, :]
        order_in = jnp.sum((same_owner & earlier).astype(I32), axis=1)
        slot = (target ^ dp) * 2 * most + side * most + order_in
        chosen = table[:, 1][:, None] == jnp.arange(heights.shape[0], dtype=I32)[None, :]
        height = jnp.sum(jnp.where(chosen, heights[None, :], 0), axis=1)
        width = jnp.sum(jnp.where(chosen, widths[None, :], 0), axis=1)
        return jnp.stack([height, width, slot])

    def numbers(first, second):
        parts = jnp.concatenate([first, second], axis=1).reshape(-1)
        return jnp.concatenate([parts, jnp.broadcast_to(core, (8,)).astype(I32)])

    own_facts, pair_facts = described(ids, core), described(ids_pair, 1 - core)
    own_meta = numbers(own_facts, own_facts)
    pair_meta = numbers(pair_facts, pair_facts)
    meta = numbers(own_facts, pair_facts)
    height, width = meta[:8], meta[8:16]
    place = jnp.arange(extent // 2, dtype=I32) * 2
    mask = (place[None, :, None] < height[:, None, None]) & (
        place[None, None, :] < width[:, None, None]
    )
    mask = jnp.broadcast_to(mask.astype(F32).reshape(low_rows, 1), (low_rows, min(128, half)))

    windows_own, residual_own = normed_windows(own_meta, images, norm_gain, norm_shift)
    windows_pair, residual_pair = normed_windows(pair_meta, images_pair, norm_gain, norm_shift)

    ready, windows_own, windows_pair = lax.optimization_barrier((meta, windows_own, windows_pair))
    folded, glow_part = kernel_call(
        functools.partial(glow_kernel, extent, loss_scale),
        (
            jax.ShapeDtypeStruct((4, low_rows, half), BF),
            jax.ShapeDtypeStruct((low_rows, channels), F32),
        ),
        flops=8 * low_rows * channels * half,
        moved_bytes=5 << 20,
        scratch=(
            laned(extent, extent, half),
            pltpu.VMEM((4, channels, half), BF),
            pltpu.VMEM((8 * most, pixels, half), BF),
            pltpu.SemaphoreType.DMA((4,)),
        ),
        in_specs=[SCALARS] + [pl.BlockSpec(memory_space=pl.ANY)] * 4 + [WHOLE],
        out_specs=(WHOLE, WHOLE),
    )(ready, *arrived, up_down)
    glow_got = send(glow_part, "c")

    glow, conv_grads = kernel_call(
        functools.partial(grad_conv_kernel, loss_scale),
        (
            jax.ShapeDtypeStruct((low_rows, channels), BF),
            jax.ShapeDtypeStruct((16, 18, rows, half), BF),
        ),
        flops=80 * low_rows * channels * half,
        moved_bytes=15 << 20,
        scratch=(pltpu.VMEM((4, half, channels), BF), pltpu.VMEM((4, half, low_rows), BF)),
        in_specs=[WHOLE] * 7,
        out_specs=(WHOLE, WHOLE),
    )(mask, glow_part, glow_got, folded, up_down, windows_own, windows_pair)
    conv_grads = over_plane(conv_grads)
    glow, windows_own, windows_pair = lax.optimization_barrier((glow, windows_own, windows_pair))

    wide, skip, low_part = kernel_call(
        conv_kernel,
        (
            jax.ShapeDtypeStruct((4, low_rows, half), F32),
            jax.ShapeDtypeStruct((4, low_rows, half), BF),
            jax.ShapeDtypeStruct((low_rows, channels), F32),
        ),
        flops=80 * low_rows * channels * half,
        moved_bytes=18 << 20,
        scratch=(pltpu.VMEM((9, channels, half), BF), pltpu.VMEM((4, half, channels), BF)),
        in_specs=[WHOLE] * 7,
        out_specs=(WHOLE,) * 3,
    )(mask, conv_two, up_down, windows_own, windows_pair, residual_own, residual_pair)
    low_got = send(low_part, "c")

    *returning, grads = kernel_call(
        functools.partial(output_kernel, extent, loss_scale),
        (
            *(block,) * 4,
            jax.ShapeDtypeStruct((16, 16, rows, half), BF),
        ),
        flops=24 * low_rows * channels * half,
        moved_bytes=14 << 20,
        scratch=(
            pltpu.VMEM((low_rows, channels), BF),
            pltpu.VMEM((4, channels, half), BF),
            pltpu.VMEM((4, low_rows, half), F32),
            laned(extent, extent, half),
            pltpu.VMEM((8 * most, pixels, half), BF),
        ),
        in_specs=[SCALARS] + [WHOLE] * 8,
        out_specs=(WHOLE,) * 5,
    )(meta, mask, low_part, low_got, wide, skip, glow, folded, up_down)
    returned = over_dp(returning)
    grads = over_plane(grads)

    conv_sum = jnp.sum(conv_grads.astype(F32), axis=0).reshape(2, 9, rows, half)
    conv_sum, returned = lax.optimization_barrier((conv_sum, returned))

    def by_core(own, pair):
        return jnp.where(core == 0, jnp.stack([own, pair]), jnp.stack([pair, own]))

    out_conv = by_core(*over_column(conv_sum, y)).transpose(2, 1, 0, 3)
    out_conv = out_conv.reshape(rows, 9, channels)
    grads_sum = jnp.sum(grads.astype(F32), axis=0)
    up_sum, down_sum = grads_sum[:8].reshape(2, 4, rows, half), grads_sum[8:]
    shares = jnp.concatenate([up_sum, jnp.broadcast_to(down_sum, (2, *down_sum.shape))], axis=1)
    shares, out_conv = lax.optimization_barrier((shares, out_conv))
    own, pair = over_column(shares, y)
    out_up = by_core(own[:4], pair[:4]).transpose(2, 1, 0, 3).reshape(rows, 4 * channels)
    out_down = jnp.where(y == core, own[4:], pair[4:])
    out_down = out_down.reshape(2, 4 * rows, half).transpose(1, 0, 2).reshape(4 * rows, channels)

    block_out = kernel_call(
        join_kernel,
        jax.ShapeDtypeStruct((4 * most, pixels, channels), F32),
        flops=0,
        moved_bytes=6 * cotangent.size,
        scratch=(pltpu.VMEM((4, 2 * most, pixels, half), F32), pltpu.SemaphoreType.DMA((4,))),
        in_specs=[SCALARS] + [WHOLE] * 4,
        out_specs=pl.BlockSpec(memory_space=pl.ANY),
    )(number, *returned)
    return (block_out.reshape(cotangent.shape), out_conv, out_down, out_up)


def solution(mesh):
    return jax.shard_map(
        per_device,
        mesh=mesh,
        in_specs=(
            P(("dp", "fsdp"), None, None, None),
            P(("dp", "fsdp"), None),
            P(("dp", "fsdp")),
            P(),
            P(),
            P("fsdp", None, None),
            P("fsdp", None),
            P("fsdp", None),
            P(),
            P(),
            P(("dp", "fsdp"), None, None, None),
        ),
        out_specs=(
            P(("dp", "fsdp"), None, None, None),
            P("fsdp", None, None),
            P("fsdp", None),
            P("fsdp", None),
        ),
        check_vma=False,
    )
```

```python
import functools
import math

import jax
import jax.numpy as jnp
from jax import lax
from jax.experimental import pallas as pl
from jax.experimental.pallas import tpu as pltpu
from jax.sharding import PartitionSpec as P

GROUPS = 32
epsilon = 1e-05
BF = jnp.bfloat16
F32 = jnp.float32
I32 = jnp.int32
AXES = ("dp", "fsdp")
SENT = 5
VMEM_BYTES = 56 * 1024 * 1024


def moved(fn):
    pairs = []
    for index in range(128):
        dp, fsdp = index // 32, index % 32
        place = (dp // 2, dp % 2, fsdp // 8, fsdp // 4 % 2, fsdp % 4)
        h, c, z, y, x = fn(*place)
        pairs.append((index, (h * 2 + c) * 32 + z * 8 + y * 4 + x))
    return pairs


STEP = {
    "y": moved(lambda h, c, z, y, x: (h, c, z, 1 - y, x)),
    "hy": moved(lambda h, c, z, y, x: (1 - h, c, z, 1 - y, x)),
    "c": moved(lambda h, c, z, y, x: (h, 1 - c, z, y, x)),
    "h": moved(lambda h, c, z, y, x: (1 - h, c, z, y, x)),
    "hc": moved(lambda h, c, z, y, x: (1 - h, 1 - c, z, y, x)),
}
PLANES = [[z * 8 + y * 4 + x for z in range(4) for x in range(4)] for y in range(2)]


def send(value, move):
    return lax.ppermute(value, AXES, STEP[move])


def over_dp(blocks):
    own, beside, across, both = blocks
    return (own, send(beside, "c"), send(across, "h"), send(both, "hc"))


def over_column(parts, y):
    kept = lax.dynamic_index_in_dim(parts, y, axis=0, keepdims=False)
    given = lax.dynamic_index_in_dim(parts, 1 - y, axis=0, keepdims=False)
    sent = given.astype(BF)
    got = (send(sent, "y"), send(kept.astype(BF), "h"), send(sent, "hy"))
    total = kept + got[0].astype(F32) + got[1].astype(F32) + got[2].astype(F32)
    return total, send(total, "c")


def over_plane(blocks):
    return lax.all_to_all(
        blocks, "fsdp", split_axis=0, concat_axis=0, axis_index_groups=PLANES, tiled=True
    )


def dot(left, right, left_dim, right_dim):
    return lax.dot_general(
        left, right, (((left_dim,), (right_dim,)), ((), ())), preferred_element_type=F32
    )


def kernel_call(body, out_shape, flops, moved_bytes, scratch=(), **more):
    return pl.pallas_call(
        body,
        out_shape=out_shape,
        scratch_shapes=list(scratch),
        compiler_params=pltpu.CompilerParams(vmem_limit_bytes=VMEM_BYTES),
        cost_estimate=pl.CostEstimate(
            flops=int(flops), bytes_accessed=int(moved_bytes), transcendentals=0
        ),
        **more,
    )


def laned(extent_rows, extent_columns, lanes):
    block = min(128, lanes)
    return pltpu.VMEM((lanes // block, extent_rows, extent_columns, block), F32)


def put_line(ref, row, first, values):
    block = ref.shape[3]
    for b in range(ref.shape[0]):
        ref[b, row, first : first + values.shape[0], :] = values[:, b * block : (b + 1) * block]


def get_line(ref, row):
    return jnp.concatenate([ref[b, row] for b in range(ref.shape[0])], axis=1)


def every_second(ref, row, first, side):
    places = [
        ref[pl.ds(b, 1), pl.ds(row, 1), pl.ds(first, side, stride=2), :].reshape(side, ref.shape[3])
        for b in range(ref.shape[0])
    ]
    return jnp.concatenate(places, axis=1)


def put_every_second(ref, row, first, values):
    side, block = values.shape[0], ref.shape[3]
    for b in range(ref.shape[0]):
        ref[pl.ds(b, 1), pl.ds(row, 1), pl.ds(first, side, stride=2), :] = values[
            :, b * block : (b + 1) * block
        ].reshape(1, 1, side, block)


WHOLE = pl.BlockSpec(memory_space=pltpu.VMEM)
SCALARS = pl.BlockSpec(memory_space=pltpu.SMEM)


def over_group(sums, width):
    lane = lax.broadcasted_iota(I32, sums.shape, 1)
    step = width // 2
    while step:
        lower = (lane & step) == 0
        lanes = sums.shape[1]
        sums = sums + jnp.where(
            lower, pltpu.roll(sums, lanes - step, 1), pltpu.roll(sums, step, 1)
        )
        step //= 2
    return sums


def norm_kernel(extent, meta, image, gain, shift, windows, residual, padded, raw):
    place = pl.program_id(0)
    channels = image.shape[2]
    half = channels // 2
    height, width = meta[place], meta[8 + place]
    core = meta[24]

    @pl.when(place == 0)
    def _():
        padded[...] = jnp.zeros_like(padded)

    inside = lax.broadcasted_iota(I32, (extent, channels), 0) < width

    def line(row):
        return image[0, row * extent : (row + 1) * extent, :].astype(F32)

    def mask(row):
        return (inside & (row < height)).astype(F32)

    group = channels // GROUPS
    counted = jnp.maximum((height * width * group).astype(F32), 1.0)
    total = jnp.zeros((extent, channels), F32)
    for row in range(extent):
        total = total + line(row) * mask(row)
    total = jnp.broadcast_to(jnp.sum(total, axis=0, keepdims=True), (8, channels))
    mean = (over_group(total, group) / counted)[:1]
    total = jnp.zeros((extent, channels), F32)
    for row in range(extent):
        centred = (line(row) - mean) * mask(row)
        total = total + centred * centred
    total = jnp.broadcast_to(jnp.sum(total, axis=0, keepdims=True), (8, channels))
    variance = (over_group(total, group) / counted)[:1]
    scale = lax.rsqrt(variance + epsilon) * gain[...]
    for row in range(extent):
        normed = (line(row) - mean) * scale + shift[...]
        put_line(padded, row + 1, 8, normed / (1.0 + jnp.exp(-normed)) * mask(row))
        residue = image[
            0, row * extent : (row + 1) * extent, pl.ds(pl.multiple_of(core * half, half), half)
        ]
        put_line(raw, row, 0, residue.astype(F32))
    side = extent // 2
    for p in range(4):
        for q in range(4):
            for i in range(0, side, 2):
                pair = [every_second(padded, 2 * n + p, 7 + q, side) for n in (i, i + 1)]
                windows[p * 4 + q, i * side : (i + 2) * side, :] = jnp.concatenate(pair).astype(BF)
    for k in range(4):
        for i in range(0, side, 2):
            pair = [every_second(raw, 2 * n + k // 2, k % 2, side) for n in (i, i + 1)]
            residual[k, i * side : (i + 2) * side, :] = jnp.concatenate(pair).astype(BF)


def normed_windows(meta, images, gain, shift):
    count, extent, _, channels = images.shape
    pixels, half = extent * extent, channels // 2
    quarter = pixels // 4
    return kernel_call(
        functools.partial(norm_kernel, extent),
        (
            jax.ShapeDtypeStruct((16, count * quarter, channels), BF),
            jax.ShapeDtypeStruct((4, count * quarter, half), BF),
        ),
        flops=40 * images.size,
        moved_bytes=12 * images.size,
        scratch=(
            laned(extent + 2, extent + 16, channels),
            laned(extent, extent, half),
        ),
        grid=(count,),
        in_specs=[
            SCALARS,
            pl.BlockSpec((1, pixels, channels), lambda g: (g, 0, 0)),
            pl.BlockSpec((1, channels), lambda g: (0, 0)),
            pl.BlockSpec((1, channels), lambda g: (0, 0)),
        ],
        out_specs=(
            pl.BlockSpec((16, quarter, channels), lambda g: (0, g, 0)),
            pl.BlockSpec((4, quarter, half), lambda g: (0, g, 0)),
        ),
    )(meta, images.reshape(count, pixels, channels), gain[None, :], shift[None, :])


def gather_up(pieces, up):
    rows = pieces.shape[2]
    for f in range(32):
        z, y, x = f // 8, f // 4 % 2, f % 4
        for k in range(4):
            up[k, f * rows : (f + 1) * rows, :] = pieces[z * 4 + x, y * 4 + k]


def gather_down(pieces, down):
    rows, half = pieces.shape[2:]
    for z in range(4):
        for x in range(4):
            for unit in range(8):
                side, step = unit // 4, unit % 4
                first = (x * 4 + step) * rows
                down[z, first : first + rows, side * half : (side + 1) * half] = pieces[
                    z * 4 + x, 8 + unit
                ]


def swapped_sum(own, got):
    middle = own.shape[0] // 2
    return jnp.concatenate(
        [own[:middle] + got[middle:], own[middle:] + got[:middle]], axis=0
    ).astype(BF)


def glow_kernel(
    extent, loss_scale, meta, cot0, cot1, cot2, cot3, pieces, folded, part, raw, up, cot, sem
):
    side = extent // 2
    quarter = side * side
    half = cot.shape[2]
    slots = cot0.shape[0]
    copies = [
        pltpu.make_async_copy(ref, cot.at[pl.ds(r * slots, slots)], sem.at[r])
        for r, ref in enumerate((cot0, cot1, cot2, cot3))
    ]
    for copy in copies:
        copy.start()
    gather_up(pieces, up)
    for copy in copies:
        copy.wait()
    images = folded.shape[1] // quarter
    inside = lax.broadcasted_iota(I32, (extent, half), 0)

    def one(g, carry):
        height, width, slot = meta[g], meta[8 + g], meta[16 + g]
        for row in range(extent):
            kept = ((inside < width) & (row < height)).astype(F32)
            line = cot[slot, row * extent : (row + 1) * extent, :].astype(F32)
            put_line(raw, row, 0, line * kept)
        for k in range(4):
            for i in range(0, side, 2):
                pair = [every_second(raw, 2 * n + k // 2, k % 2, side) for n in (i, i + 1)]
                first = pl.multiple_of(g * quarter + i * side, 2 * side)
                folded[k, pl.ds(first, 2 * side), :] = jnp.concatenate(pair).astype(BF)
        return carry

    lax.fori_loop(0, images, one, 0)
    total = None
    for k in range(4):
        scaled = (folded[k].astype(F32) * loss_scale).astype(BF)
        term = dot(scaled, up[k], 1, 1)
        total = term if total is None else total + term
    part[...] = total


def grad_conv_kernel(
    loss_scale,
    mask,
    own,
    got,
    folded,
    pieces,
    windows_own,
    windows_pair,
    glow,
    grads,
    rest,
    down,
    turned,
):
    half = folded.shape[2]
    rows = grads.shape[2]
    middle = folded.shape[1] // 2
    gather_down(pieces, down)
    glow[...] = swapped_sum(own, got)
    kept = jnp.concatenate([mask[...]] * (half // mask.shape[1]), axis=1)
    for k in range(4):
        grad = folded[k].astype(F32) * loss_scale + dot(glow[...], down[k], 1, 1)
        turned[k] = (grad * kept).T.astype(BF)
    for t in range(9):
        total = None
        for k in range(4):
            v = (k // 2 + t // 3) * 4 + k % 2 + t % 3
            for columns, windows in ((slice(0, middle), windows_own), (slice(middle, None), windows_pair)):
                term = dot(turned[k, :, columns], windows[v], 1, 0)
                total = term if total is None else total + term
        total = total.T
        for f in range(32):
            z, y, x = f // 8, f // 4 % 2, f % 4
            piece = total[f * rows : (f + 1) * rows, :]
            if t < SENT:
                grads[z * 4 + x, y * SENT + t] = piece.astype(BF)
            else:
                rest[z * 4 + x, y * (9 - SENT) + t - SENT] = piece


def conv_kernel(
    mask,
    conv_pieces,
    pieces,
    windows_own,
    windows_pair,
    residual_own,
    residual_pair,
    wide,
    skip,
    part,
    conv,
    down,
):
    half = wide.shape[2]
    rows = conv_pieces.shape[2]
    middle = wide.shape[1] // 2
    for f in range(32):
        z, y, x = f // 8, f // 4 % 2, f % 4
        for t in range(9):
            conv[t, f * rows : (f + 1) * rows, :] = conv_pieces[z * 4 + x, y * 9 + t]
    gather_down(pieces, down)
    total = None
    for k in range(4):
        for first, windows, residual in (
            (0, windows_own, residual_own),
            (middle, windows_pair, residual_pair),
        ):
            convolved = None
            for t in range(9):
                v = (k // 2 + t // 3) * 4 + k % 2 + t % 3
                term = dot(windows[v], conv[t], 1, 0)
                convolved = term if convolved is None else convolved + term
            kept = mask[first : first + middle, :]
            kept = jnp.concatenate([kept] * (half // mask.shape[1]), axis=1)
            masked = (residual[k].astype(F32) + convolved) * kept
            wide[k, first : first + middle, :] = masked
            skip[k, first : first + middle, :] = masked.astype(BF)
        term = dot(skip[k], down[k], 1, 0)
        total = term if total is None else total + term
    part[...] = total


def output_kernel(
    extent,
    loss_scale,
    meta,
    mask,
    own,
    got,
    wide,
    skip,
    glow,
    folded,
    pieces,
    back0,
    back1,
    back2,
    back3,
    grads,
    low,
    up,
    outputs,
    raw,
    returning,
):
    side = extent // 2
    quarter = side * side
    half = wide.shape[2]
    rows = grads.shape[2]
    images = wide.shape[1] // quarter
    gather_up(pieces, up)
    low[...] = swapped_sum(own, got)
    kept = jnp.concatenate([mask[...]] * (half // mask.shape[1]), axis=1)
    for k in range(4):
        outputs[k] = (wide[k] + dot(low[...], up[k], 1, 0)) * kept
    returning[...] = jnp.zeros_like(returning)

    def one(g, carry):
        slot = meta[16 + g]
        for k in range(4):
            for i in range(side):
                first = pl.multiple_of(g * quarter + i * side, side)
                put_every_second(raw, 2 * i + k // 2, k % 2, outputs[k, pl.ds(first, side), :])
        for row in range(extent):
            returning[slot, row * extent : (row + 1) * extent, :] = get_line(raw, row).astype(BF)
        return carry

    lax.fori_loop(0, images, one, 0)
    slots = back0.shape[0]
    for r, back in enumerate((back0, back1, back2, back3)):
        back[...] = returning[r * slots : (r + 1) * slots]
    turned = low[...].astype(F32).T.astype(BF)
    for k in range(4):
        scaled = (folded[k].astype(F32) * loss_scale).astype(BF)
        grad = dot(turned, scaled, 1, 0).astype(BF)
        for f in range(32):
            z, y, x = f // 8, f // 4 % 2, f % 4
            grads[z * 4 + x, y * 4 + k] = grad[f * rows : (f + 1) * rows, :]
        grad = dot(skip[k].astype(F32).T.astype(BF), glow[...], 1, 0).astype(BF)
        for x in range(4):
            for unit in range(8):
                side_of, step = unit // 4, unit % 4
                first = (x * 4 + step) * rows
                grads[k * 4 + x, 8 + unit] = grad[
                    first : first + rows, side_of * half : (side_of + 1) * half
                ]


def replicas(number, half):
    for r in range(4):
        chip, core = number // 2, number % 2
        chip = 1 - chip if r // 2 else chip
        core = 1 - core if r % 2 else core
        yield r, chip, pl.ds(pl.multiple_of(core * half, half), half)


def split_kernel(number, cot, out0, out1, out2, out3):
    outs = (out0, out1, out2, out3)
    slots, _, half = out0.shape
    for r, chip, lanes in replicas(number[0], half):
        outs[r][...] = cot[pl.ds(chip * slots, slots), :, lanes]


def join_kernel(number, back0, back1, back2, back3, out, wide, sem):
    backs = (back0, back1, back2, back3)
    slots, _, half = back0.shape
    copies = []
    for r, chip, lanes in replicas(number[0], half):
        wide[r] = backs[r][...].astype(F32)
        target = out.at[pl.ds(chip * slots, slots), :, lanes]
        copies.append(pltpu.make_async_copy(wide.at[r], target, sem.at[r]))
        copies[-1].start()
    for copy in copies:
        copy.wait()


def per_device(
    images, routes, bucket, heights, widths, w_conv, w_down, w_up, norm_gain, norm_shift, cotangent
):
    count, extent, _, channels = images.shape
    half = channels // 2
    pixels = extent * extent
    quarter = pixels // 4
    most = cotangent.shape[0] // 4
    rows = w_conv.shape[0]
    low_rows = 2 * count * quarter
    loss_scale = 1.0 / math.sqrt(count * 128 * pixels)
    dp, fsdp = lax.axis_index("dp"), lax.axis_index("fsdp")
    core, y = dp % 2, fsdp // 4 % 2

    conv_own = lax.dynamic_slice_in_dim(w_conv, core * half, half, axis=2).transpose(1, 0, 2)
    up_own = lax.dynamic_slice_in_dim(
        w_up.reshape(rows, 4, channels), core * half, half, axis=2
    ).transpose(1, 0, 2)
    down_own = w_down.reshape(4 * rows, 2, half).transpose(1, 0, 2).reshape(8, rows, half)
    packed = jnp.concatenate([up_own, down_own, conv_own])
    other = send(packed, "y")

    block = jax.ShapeDtypeStruct((2 * most, pixels, half), BF)
    number = dp.astype(I32).reshape(1)
    outgoing = kernel_call(
        split_kernel,
        (block,) * 4,
        flops=0,
        moved_bytes=4 * cotangent.size,
        in_specs=[SCALARS, WHOLE],
        out_specs=(WHOLE,) * 4,
    )(number, cotangent.reshape(4 * most, pixels, channels))
    outgoing, other = lax.optimization_barrier((outgoing, other))
    arrived = over_dp(outgoing)
    first = jnp.where(y == 0, packed, other)
    second = jnp.where(y == 0, other, packed)
    down_kept = jnp.where(core == 0, first[4:12], second[4:12])
    up_down = jnp.concatenate([first[:4], second[:4], down_kept])
    conv_two = jnp.concatenate([first[12:], second[12:]])
    up_down = over_plane(jnp.broadcast_to(up_down, (16, *up_down.shape)))
    conv_two = lax.all_gather(conv_two, "fsdp", axis_index_groups=PLANES)

    images_pair = send(images, "c")
    ids = jnp.concatenate([routes, bucket[:, None]], axis=1)
    ids_pair = send(ids, "c")

    def described(table, side):
        target = table[:, 0]
        position = jnp.arange(count, dtype=I32)
        earlier = position[None, :] < position[:, None]
        same_owner = target[:, None] == target[None, :]
        order_in = jnp.sum((same_owner & earlier).astype(I32), axis=1)
        slot = (target ^ dp) * 2 * most + side * most + order_in
        chosen = table[:, 1][:, None] == jnp.arange(heights.shape[0], dtype=I32)[None, :]
        height = jnp.sum(jnp.where(chosen, heights[None, :], 0), axis=1)
        width = jnp.sum(jnp.where(chosen, widths[None, :], 0), axis=1)
        return jnp.stack([height, width, slot])

    def numbers(first, second):
        parts = jnp.concatenate([first, second], axis=1).reshape(-1)
        return jnp.concatenate([parts, jnp.broadcast_to(core, (8,)).astype(I32)])

    own_facts, pair_facts = described(ids, core), described(ids_pair, 1 - core)
    own_meta = numbers(own_facts, own_facts)
    pair_meta = numbers(pair_facts, pair_facts)
    meta = numbers(own_facts, pair_facts)
    height, width = meta[:8], meta[8:16]
    place = jnp.arange(extent // 2, dtype=I32) * 2
    mask = (place[None, :, None] < height[:, None, None]) & (
        place[None, None, :] < width[:, None, None]
    )
    mask = jnp.broadcast_to(mask.astype(F32).reshape(low_rows, 1), (low_rows, min(128, half)))

    windows_own, residual_own = normed_windows(own_meta, images, norm_gain, norm_shift)
    windows_pair, residual_pair = normed_windows(pair_meta, images_pair, norm_gain, norm_shift)

    ready, windows_own, windows_pair = lax.optimization_barrier((meta, windows_own, windows_pair))
    folded, glow_part = kernel_call(
        functools.partial(glow_kernel, extent, loss_scale),
        (
            jax.ShapeDtypeStruct((4, low_rows, half), BF),
            jax.ShapeDtypeStruct((low_rows, channels), F32),
        ),
        flops=8 * low_rows * channels * half,
        moved_bytes=5 << 20,
        scratch=(
            laned(extent, extent, half),
            pltpu.VMEM((4, channels, half), BF),
            pltpu.VMEM((8 * most, pixels, half), BF),
            pltpu.SemaphoreType.DMA((4,)),
        ),
        in_specs=[SCALARS] + [pl.BlockSpec(memory_space=pl.ANY)] * 4 + [WHOLE],
        out_specs=(WHOLE, WHOLE),
    )(ready, *arrived, up_down)
    glow_got = send(glow_part, "c")

    glow, conv_grads, conv_rest = kernel_call(
        functools.partial(grad_conv_kernel, loss_scale),
        (
            jax.ShapeDtypeStruct((low_rows, channels), BF),
            jax.ShapeDtypeStruct((16, 2 * SENT, rows, half), BF),
            jax.ShapeDtypeStruct((16, 18 - 2 * SENT, rows, half), F32),
        ),
        flops=80 * low_rows * channels * half,
        moved_bytes=15 << 20,
        scratch=(pltpu.VMEM((4, half, channels), BF), pltpu.VMEM((4, half, low_rows), BF)),
        in_specs=[WHOLE] * 7,
        out_specs=(WHOLE,) * 3,
    )(mask, glow_part, glow_got, folded, up_down, windows_own, windows_pair)
    conv_grads = over_plane(conv_grads)
    conv_rest = lax.psum_scatter(
        conv_rest, "fsdp", scatter_dimension=0, axis_index_groups=PLANES, tiled=True
    )
    glow, windows_own, windows_pair = lax.optimization_barrier((glow, windows_own, windows_pair))

    wide, skip, low_part = kernel_call(
        conv_kernel,
        (
            jax.ShapeDtypeStruct((4, low_rows, half), F32),
            jax.ShapeDtypeStruct((4, low_rows, half), BF),
            jax.ShapeDtypeStruct((low_rows, channels), F32),
        ),
        flops=80 * low_rows * channels * half,
        moved_bytes=18 << 20,
        scratch=(pltpu.VMEM((9, channels, half), BF), pltpu.VMEM((4, half, channels), BF)),
        in_specs=[WHOLE] * 7,
        out_specs=(WHOLE,) * 3,
    )(mask, conv_two, up_down, windows_own, windows_pair, residual_own, residual_pair)
    low_got = send(low_part, "c")

    *returning, grads = kernel_call(
        functools.partial(output_kernel, extent, loss_scale),
        (
            *(block,) * 4,
            jax.ShapeDtypeStruct((16, 16, rows, half), BF),
        ),
        flops=24 * low_rows * channels * half,
        moved_bytes=14 << 20,
        scratch=(
            pltpu.VMEM((low_rows, channels), BF),
            pltpu.VMEM((4, channels, half), BF),
            pltpu.VMEM((4, low_rows, half), F32),
            laned(extent, extent, half),
            pltpu.VMEM((8 * most, pixels, half), BF),
        ),
        in_specs=[SCALARS] + [WHOLE] * 8,
        out_specs=(WHOLE,) * 5,
    )(meta, mask, low_part, low_got, wide, skip, glow, folded, up_down)
    returned = over_dp(returning)
    grads = over_plane(grads)

    conv_sum = jnp.sum(conv_grads.astype(F32), axis=0).reshape(2, SENT, rows, half)
    conv_rest = conv_rest.reshape(2, 9 - SENT, rows, half)
    grads_sum = jnp.sum(grads.astype(F32), axis=0)
    up_sum, down_sum = grads_sum[:8].reshape(2, 4, rows, half), grads_sum[8:]
    down_sum = jnp.broadcast_to(down_sum, (2, *down_sum.shape))
    shares = jnp.concatenate([conv_sum, conv_rest, up_sum, down_sum], axis=1)
    shares, returned = lax.optimization_barrier((shares, returned))
    own, pair = over_column(shares, y)

    def by_core(first, last):
        parts = (own[first:last], pair[first:last])
        both = jnp.where(core == 0, jnp.stack(parts), jnp.stack(parts[::-1]))
        return both.transpose(2, 1, 0, 3)

    out_conv = by_core(0, 9).reshape(rows, 9, channels)
    out_up = by_core(9, 13).reshape(rows, 4 * channels)
    out_down = jnp.where(y == core, own[13:], pair[13:])
    out_down = out_down.reshape(2, 4 * rows, half).transpose(1, 0, 2).reshape(4 * rows, channels)

    block_out = kernel_call(
        join_kernel,
        jax.ShapeDtypeStruct((4 * most, pixels, channels), F32),
        flops=0,
        moved_bytes=6 * cotangent.size,
        scratch=(pltpu.VMEM((4, 2 * most, pixels, half), F32), pltpu.SemaphoreType.DMA((4,))),
        in_specs=[SCALARS] + [WHOLE] * 4,
        out_specs=pl.BlockSpec(memory_space=pl.ANY),
    )(number, *returned)
    return (block_out.reshape(cotangent.shape), out_conv, out_down, out_up)


def solution(mesh):
    return jax.shard_map(
        per_device,
        mesh=mesh,
        in_specs=(
            P(("dp", "fsdp"), None, None, None),
            P(("dp", "fsdp"), None),
            P(("dp", "fsdp")),
            P(),
            P(),
            P("fsdp", None, None),
            P("fsdp", None),
            P("fsdp", None),
            P(),
            P(),
            P(("dp", "fsdp"), None, None, None),
        ),
        out_specs=(
            P(("dp", "fsdp"), None, None, None),
            P("fsdp", None, None),
            P("fsdp", None),
            P("fsdp", None),
        ),
        check_vma=False,
    )
```

```python
import functools
import math

import jax
import jax.numpy as jnp
from jax import lax
from jax.experimental import pallas as pl
from jax.experimental.pallas import tpu as pltpu
from jax.sharding import PartitionSpec as P

GROUPS = 32
epsilon = 1e-05
BF = jnp.bfloat16
F32 = jnp.float32
I32 = jnp.int32
AXES = ("dp", "fsdp")
VMEM_BYTES = 56 * 1024 * 1024


def moved(fn):
    pairs = []
    for index in range(128):
        dp, fsdp = index // 32, index % 32
        place = (dp // 2, dp % 2, fsdp // 8, fsdp // 4 % 2, fsdp % 4)
        h, c, z, y, x = fn(*place)
        pairs.append((index, (h * 2 + c) * 32 + z * 8 + y * 4 + x))
    return pairs


STEP = {
    "y": moved(lambda h, c, z, y, x: (h, c, z, 1 - y, x)),
    "hy": moved(lambda h, c, z, y, x: (1 - h, c, z, 1 - y, x)),
    "c": moved(lambda h, c, z, y, x: (h, 1 - c, z, y, x)),
    "h": moved(lambda h, c, z, y, x: (1 - h, c, z, y, x)),
    "hc": moved(lambda h, c, z, y, x: (1 - h, 1 - c, z, y, x)),
}
PLANES = [[z * 8 + y * 4 + x for z in range(4) for x in range(4)] for y in range(2)]


def send(value, move):
    return lax.ppermute(value, AXES, STEP[move])


def over_dp(blocks):
    own, beside, across, both = blocks
    return (own, send(beside, "c"), send(across, "h"), send(both, "hc"))


def over_column(parts, y):
    kept = lax.dynamic_index_in_dim(parts, y, axis=0, keepdims=False)
    given = lax.dynamic_index_in_dim(parts, 1 - y, axis=0, keepdims=False)
    sent = given.astype(BF)
    got = (send(sent, "y"), send(kept.astype(BF), "h"), send(sent, "hy"))
    total = kept + got[0].astype(F32) + got[1].astype(F32) + got[2].astype(F32)
    return total, send(total, "c")


def over_plane(blocks):
    return lax.all_to_all(
        blocks, "fsdp", split_axis=0, concat_axis=0, axis_index_groups=PLANES, tiled=True
    )


def dot(left, right, left_dim, right_dim):
    return lax.dot_general(
        left, right, (((left_dim,), (right_dim,)), ((), ())), preferred_element_type=F32
    )


def kernel_call(body, out_shape, flops, moved_bytes, scratch=(), **more):
    return pl.pallas_call(
        body,
        out_shape=out_shape,
        scratch_shapes=list(scratch),
        compiler_params=pltpu.CompilerParams(vmem_limit_bytes=VMEM_BYTES),
        cost_estimate=pl.CostEstimate(
            flops=int(flops), bytes_accessed=int(moved_bytes), transcendentals=0
        ),
        **more,
    )


def laned(extent_rows, extent_columns, lanes):
    block = min(128, lanes)
    return pltpu.VMEM((lanes // block, extent_rows, extent_columns, block), F32)


def put_line(ref, row, first, values):
    block = ref.shape[3]
    for b in range(ref.shape[0]):
        ref[b, row, first : first + values.shape[0], :] = values[:, b * block : (b + 1) * block]


def get_line(ref, row):
    return jnp.concatenate([ref[b, row] for b in range(ref.shape[0])], axis=1)


def every_second(ref, row, first, side):
    places = [
        ref[pl.ds(b, 1), pl.ds(row, 1), pl.ds(first, side, stride=2), :].reshape(side, ref.shape[3])
        for b in range(ref.shape[0])
    ]
    return jnp.concatenate(places, axis=1)


def put_every_second(ref, row, first, values):
    side, block = values.shape[0], ref.shape[3]
    for b in range(ref.shape[0]):
        ref[pl.ds(b, 1), pl.ds(row, 1), pl.ds(first, side, stride=2), :] = values[
            :, b * block : (b + 1) * block
        ].reshape(1, 1, side, block)


WHOLE = pl.BlockSpec(memory_space=pltpu.VMEM)
SCALARS = pl.BlockSpec(memory_space=pltpu.SMEM)


def over_group(sums, width):
    lane = lax.broadcasted_iota(I32, sums.shape, 1)
    step = width // 2
    while step:
        lower = (lane & step) == 0
        lanes = sums.shape[1]
        sums = sums + jnp.where(
            lower, pltpu.roll(sums, lanes - step, 1), pltpu.roll(sums, step, 1)
        )
        step //= 2
    return sums


def norm_kernel(extent, meta, image, gain, shift, windows, residual, padded, raw):
    place = pl.program_id(0)
    channels = image.shape[2]
    half = channels // 2
    height, width = meta[place], meta[8 + place]
    core = meta[24]

    @pl.when(place == 0)
    def _():
        padded[...] = jnp.zeros_like(padded)

    inside = lax.broadcasted_iota(I32, (extent, channels), 0) < width

    def line(row):
        return image[0, row * extent : (row + 1) * extent, :].astype(F32)

    def mask(row):
        return (inside & (row < height)).astype(F32)

    group = channels // GROUPS
    counted = jnp.maximum((height * width * group).astype(F32), 1.0)
    total = jnp.zeros((extent, channels), F32)
    for row in range(extent):
        total = total + line(row) * mask(row)
    total = jnp.broadcast_to(jnp.sum(total, axis=0, keepdims=True), (8, channels))
    mean = (over_group(total, group) / counted)[:1]
    total = jnp.zeros((extent, channels), F32)
    for row in range(extent):
        centred = (line(row) - mean) * mask(row)
        total = total + centred * centred
    total = jnp.broadcast_to(jnp.sum(total, axis=0, keepdims=True), (8, channels))
    variance = (over_group(total, group) / counted)[:1]
    scale = lax.rsqrt(variance + epsilon) * gain[...]
    for row in range(extent):
        normed = (line(row) - mean) * scale + shift[...]
        put_line(padded, row + 1, 8, normed / (1.0 + jnp.exp(-normed)) * mask(row))
        residue = image[
            0, row * extent : (row + 1) * extent, pl.ds(pl.multiple_of(core * half, half), half)
        ]
        put_line(raw, row, 0, residue.astype(F32))
    side = extent // 2
    for p in range(4):
        for q in range(4):
            for i in range(0, side, 2):
                pair = [every_second(padded, 2 * n + p, 7 + q, side) for n in (i, i + 1)]
                windows[p * 4 + q, i * side : (i + 2) * side, :] = jnp.concatenate(pair).astype(BF)
    for k in range(4):
        for i in range(0, side, 2):
            pair = [every_second(raw, 2 * n + k // 2, k % 2, side) for n in (i, i + 1)]
            residual[k, i * side : (i + 2) * side, :] = jnp.concatenate(pair).astype(BF)


def normed_windows(meta, images, gain, shift):
    count, extent, _, channels = images.shape
    pixels, half = extent * extent, channels // 2
    quarter = pixels // 4
    return kernel_call(
        functools.partial(norm_kernel, extent),
        (
            jax.ShapeDtypeStruct((16, count * quarter, channels), BF),
            jax.ShapeDtypeStruct((4, count * quarter, half), BF),
        ),
        flops=40 * images.size,
        moved_bytes=12 * images.size,
        scratch=(
            laned(extent + 2, extent + 16, channels),
            laned(extent, extent, half),
        ),
        grid=(count,),
        in_specs=[
            SCALARS,
            pl.BlockSpec((1, pixels, channels), lambda g: (g, 0, 0)),
            pl.BlockSpec((1, channels), lambda g: (0, 0)),
            pl.BlockSpec((1, channels), lambda g: (0, 0)),
        ],
        out_specs=(
            pl.BlockSpec((16, quarter, channels), lambda g: (0, g, 0)),
            pl.BlockSpec((4, quarter, half), lambda g: (0, g, 0)),
        ),
    )(meta, images.reshape(count, pixels, channels), gain[None, :], shift[None, :])


def gather_up(pieces, up):
    rows = pieces.shape[2]
    for f in range(32):
        z, y, x = f // 8, f // 4 % 2, f % 4
        for k in range(4):
            up[k, f * rows : (f + 1) * rows, :] = pieces[z * 4 + x, y * 4 + k]


def gather_down(pieces, down):
    rows, half = pieces.shape[2:]
    for z in range(4):
        for x in range(4):
            for unit in range(8):
                side, step = unit // 4, unit % 4
                first = (x * 4 + step) * rows
                down[z, first : first + rows, side * half : (side + 1) * half] = pieces[
                    z * 4 + x, unit
                ]


def swapped_sum(own, got):
    middle = own.shape[0] // 2
    return jnp.concatenate(
        [own[:middle] + got[middle:], own[middle:] + got[:middle]], axis=0
    ).astype(BF)


def glow_kernel(
    extent, loss_scale, meta, cot0, cot1, cot2, cot3, pieces, folded, part, raw, up, cot, sem
):
    side = extent // 2
    quarter = side * side
    half = cot.shape[2]
    slots = cot0.shape[0]
    copies = [
        pltpu.make_async_copy(ref, cot.at[pl.ds(r * slots, slots)], sem.at[r])
        for r, ref in enumerate((cot0, cot1, cot2, cot3))
    ]
    for copy in copies:
        copy.start()
    gather_up(pieces, up)
    for copy in copies:
        copy.wait()
    images = folded.shape[1] // quarter
    inside = lax.broadcasted_iota(I32, (extent, half), 0)

    def one(g, carry):
        height, width, slot = meta[g], meta[8 + g], meta[16 + g]
        for row in range(extent):
            kept = ((inside < width) & (row < height)).astype(F32)
            line = cot[slot, row * extent : (row + 1) * extent, :].astype(F32)
            put_line(raw, row, 0, line * kept)
        for k in range(4):
            for i in range(0, side, 2):
                pair = [every_second(raw, 2 * n + k // 2, k % 2, side) for n in (i, i + 1)]
                first = pl.multiple_of(g * quarter + i * side, 2 * side)
                folded[k, pl.ds(first, 2 * side), :] = jnp.concatenate(pair).astype(BF)
        return carry

    lax.fori_loop(0, images, one, 0)
    total = None
    for k in range(4):
        scaled = (folded[k].astype(F32) * loss_scale).astype(BF)
        term = dot(scaled, up[k], 1, 1)
        total = term if total is None else total + term
    part[...] = total


def grad_conv_kernel(
    loss_scale,
    mask,
    own,
    got,
    folded,
    pieces,
    windows_own,
    windows_pair,
    glow,
    grads,
    down,
    turned,
    windows,
    sem,
):
    half = folded.shape[2]
    copies = [
        pltpu.make_async_copy(ref, windows.at[part], sem.at[part])
        for part, ref in enumerate((windows_own, windows_pair))
    ]
    for copy in copies:
        copy.start()
    rows = grads.shape[2]
    middle = folded.shape[1] // 2
    gather_down(pieces, down)
    glow[...] = swapped_sum(own, got)
    kept = jnp.concatenate([mask[...]] * (half // mask.shape[1]), axis=1)
    for k in range(4):
        grad = folded[k].astype(F32) * loss_scale + dot(glow[...], down[k], 1, 1)
        turned[k] = (grad * kept).T.astype(BF)
    for copy in copies:
        copy.wait()
    for t in range(9):
        total = None
        for k in range(4):
            v = (k // 2 + t // 3) * 4 + k % 2 + t % 3
            for part in range(2):
                columns = slice(part * middle, (part + 1) * middle)
                term = dot(turned[k, :, columns], windows[part, v], 1, 0)
                total = term if total is None else total + term
        total = total.T.astype(BF)
        for f in range(32):
            z, y, x = f // 8, f // 4 % 2, f % 4
            grads[z * 4 + x, y * 9 + t] = total[f * rows : (f + 1) * rows, :]


def conv_kernel(
    mask,
    conv_pieces,
    pieces,
    windows_own,
    windows_pair,
    residual_own,
    residual_pair,
    wide,
    skip,
    part,
    conv,
    down,
):
    half = wide.shape[2]
    rows = conv_pieces.shape[2]
    middle = wide.shape[1] // 2
    for f in range(32):
        z, y, x = f // 8, f // 4 % 2, f % 4
        for t in range(9):
            conv[t, f * rows : (f + 1) * rows, :] = conv_pieces[z * 4 + x, y * 9 + t]
    gather_down(pieces, down)
    total = None
    for k in range(4):
        for first, windows, residual in (
            (0, windows_own, residual_own),
            (middle, windows_pair, residual_pair),
        ):
            convolved = None
            for t in range(9):
                v = (k // 2 + t // 3) * 4 + k % 2 + t % 3
                term = dot(windows[v], conv[t], 1, 0)
                convolved = term if convolved is None else convolved + term
            kept = mask[first : first + middle, :]
            kept = jnp.concatenate([kept] * (half // mask.shape[1]), axis=1)
            masked = (residual[k].astype(F32) + convolved) * kept
            wide[k, first : first + middle, :] = masked
            skip[k, first : first + middle, :] = masked.astype(BF)
        term = dot(skip[k], down[k], 1, 0)
        total = term if total is None else total + term
    part[...] = total


def output_kernel(
    extent,
    loss_scale,
    meta,
    mask,
    own,
    got,
    wide,
    skip,
    glow,
    folded,
    pieces,
    back0,
    back1,
    back2,
    back3,
    grads,
    low,
    up,
    outputs,
    raw,
    returning,
):
    side = extent // 2
    quarter = side * side
    half = wide.shape[2]
    rows = grads.shape[2]
    images = wide.shape[1] // quarter
    gather_up(pieces, up)
    low[...] = swapped_sum(own, got)
    kept = jnp.concatenate([mask[...]] * (half // mask.shape[1]), axis=1)
    for k in range(4):
        outputs[k] = (wide[k] + dot(low[...], up[k], 1, 0)) * kept
    returning[...] = jnp.zeros_like(returning)

    def one(g, carry):
        slot = meta[16 + g]
        for k in range(4):
            for i in range(side):
                first = pl.multiple_of(g * quarter + i * side, side)
                put_every_second(raw, 2 * i + k // 2, k % 2, outputs[k, pl.ds(first, side), :])
        for row in range(extent):
            returning[slot, row * extent : (row + 1) * extent, :] = get_line(raw, row).astype(BF)
        return carry

    lax.fori_loop(0, images, one, 0)
    slots = back0.shape[0]
    for r, back in enumerate((back0, back1, back2, back3)):
        back[...] = returning[r * slots : (r + 1) * slots]
    turned = low[...].astype(F32).T.astype(BF)
    for k in range(4):
        scaled = (folded[k].astype(F32) * loss_scale).astype(BF)
        grad = dot(turned, scaled, 1, 0).astype(BF)
        for f in range(32):
            z, y, x = f // 8, f // 4 % 2, f % 4
            grads[z * 4 + x, y * 4 + k] = grad[f * rows : (f + 1) * rows, :]
        grad = dot(skip[k].astype(F32).T.astype(BF), glow[...], 1, 0).astype(BF)
        for x in range(4):
            for unit in range(8):
                side_of, step = unit // 4, unit % 4
                first = (x * 4 + step) * rows
                grads[k * 4 + x, 8 + unit] = grad[
                    first : first + rows, side_of * half : (side_of + 1) * half
                ]


def replicas(number, half):
    for r in range(4):
        chip, core = number // 2, number % 2
        chip = 1 - chip if r // 2 else chip
        core = 1 - core if r % 2 else core
        yield r, chip, pl.ds(pl.multiple_of(core * half, half), half)


def split_kernel(number, cot, out0, out1, out2, out3):
    outs = (out0, out1, out2, out3)
    slots, _, half = out0.shape
    for r, chip, lanes in replicas(number[0], half):
        outs[r][...] = cot[pl.ds(chip * slots, slots), :, lanes]


def join_kernel(number, back0, back1, back2, back3, out, wide, sem):
    backs = (back0, back1, back2, back3)
    slots, _, half = back0.shape
    copies = []
    for r, chip, lanes in replicas(number[0], half):
        wide[r] = backs[r][...].astype(F32)
        target = out.at[pl.ds(chip * slots, slots), :, lanes]
        copies.append(pltpu.make_async_copy(wide.at[r], target, sem.at[r]))
        copies[-1].start()
    for copy in copies:
        copy.wait()


def per_device(
    images, routes, bucket, heights, widths, w_conv, w_down, w_up, norm_gain, norm_shift, cotangent
):
    count, extent, _, channels = images.shape
    half = channels // 2
    pixels = extent * extent
    quarter = pixels // 4
    most = cotangent.shape[0] // 4
    rows = w_conv.shape[0]
    low_rows = 2 * count * quarter
    loss_scale = 1.0 / math.sqrt(count * 128 * pixels)
    dp, fsdp = lax.axis_index("dp"), lax.axis_index("fsdp")
    core, y = dp % 2, fsdp // 4 % 2

    conv_own = lax.dynamic_slice_in_dim(w_conv, core * half, half, axis=2).transpose(1, 0, 2)
    up_own = lax.dynamic_slice_in_dim(
        w_up.reshape(rows, 4, channels), core * half, half, axis=2
    ).transpose(1, 0, 2)
    down_own = w_down.reshape(4 * rows, 2, half).transpose(1, 0, 2).reshape(8, rows, half)
    packed = jnp.concatenate([up_own, down_own, conv_own])
    other = send(packed, "y")

    block = jax.ShapeDtypeStruct((2 * most, pixels, half), BF)
    number = dp.astype(I32).reshape(1)
    outgoing = kernel_call(
        split_kernel,
        (block,) * 4,
        flops=0,
        moved_bytes=4 * cotangent.size,
        in_specs=[SCALARS, WHOLE],
        out_specs=(WHOLE,) * 4,
    )(number, cotangent.reshape(4 * most, pixels, channels))
    outgoing, other = lax.optimization_barrier((outgoing, other))
    arrived = over_dp(outgoing)
    first = jnp.where(y == 0, packed, other)
    second = jnp.where(y == 0, other, packed)
    down_kept = jnp.where(core == 0, first[4:12], second[4:12])
    up_two = jnp.concatenate([first[:4], second[:4]])
    conv_two = jnp.concatenate([first[12:], second[12:]])
    up_two = over_plane(jnp.broadcast_to(up_two, (16, *up_two.shape)))
    down_kept = over_plane(jnp.broadcast_to(down_kept, (16, *down_kept.shape)))
    conv_two = lax.all_gather(conv_two, "fsdp", axis_index_groups=PLANES)

    images_pair = send(images, "c")
    ids = jnp.concatenate([routes, bucket[:, None]], axis=1)
    ids_pair = send(ids, "c")

    def described(table, side):
        target = table[:, 0]
        position = jnp.arange(count, dtype=I32)
        earlier = position[None, :] < position[:, None]
        same_owner = target[:, None] == target[None, :]
        order_in = jnp.sum((same_owner & earlier).astype(I32), axis=1)
        slot = (target ^ dp) * 2 * most + side * most + order_in
        chosen = table[:, 1][:, None] == jnp.arange(heights.shape[0], dtype=I32)[None, :]
        height = jnp.sum(jnp.where(chosen, heights[None, :], 0), axis=1)
        width = jnp.sum(jnp.where(chosen, widths[None, :], 0), axis=1)
        return jnp.stack([height, width, slot])

    def numbers(first, second):
        parts = jnp.concatenate([first, second], axis=1).reshape(-1)
        return jnp.concatenate([parts, jnp.broadcast_to(core, (8,)).astype(I32)])

    own_facts, pair_facts = described(ids, core), described(ids_pair, 1 - core)
    own_meta = numbers(own_facts, own_facts)
    pair_meta = numbers(pair_facts, pair_facts)
    meta = numbers(own_facts, pair_facts)
    height, width = meta[:8], meta[8:16]
    place = jnp.arange(extent // 2, dtype=I32) * 2
    mask = (place[None, :, None] < height[:, None, None]) & (
        place[None, None, :] < width[:, None, None]
    )
    mask = jnp.broadcast_to(mask.astype(F32).reshape(low_rows, 1), (low_rows, min(128, half)))

    windows_own, residual_own = normed_windows(own_meta, images, norm_gain, norm_shift)
    windows_pair, residual_pair = normed_windows(pair_meta, images_pair, norm_gain, norm_shift)

    ready, mask, windows_own, windows_pair = lax.optimization_barrier(
        (meta, mask, windows_own, windows_pair)
    )
    folded, glow_part = kernel_call(
        functools.partial(glow_kernel, extent, loss_scale),
        (
            jax.ShapeDtypeStruct((4, low_rows, half), BF),
            jax.ShapeDtypeStruct((low_rows, channels), F32),
        ),
        flops=8 * low_rows * channels * half,
        moved_bytes=5 << 20,
        scratch=(
            laned(extent, extent, half),
            pltpu.VMEM((4, channels, half), BF),
            pltpu.VMEM((8 * most, pixels, half), BF),
            pltpu.SemaphoreType.DMA((4,)),
        ),
        in_specs=[SCALARS] + [pl.BlockSpec(memory_space=pl.ANY)] * 4 + [WHOLE],
        out_specs=(WHOLE, WHOLE),
    )(ready, *arrived, up_two)
    glow_got = send(glow_part, "c")

    glow, conv_grads = kernel_call(
        functools.partial(grad_conv_kernel, loss_scale),
        (
            jax.ShapeDtypeStruct((low_rows, channels), BF),
            jax.ShapeDtypeStruct((16, 18, rows, half), BF),
        ),
        flops=80 * low_rows * channels * half,
        moved_bytes=15 << 20,
        scratch=(
            pltpu.VMEM((4, half, channels), BF),
            pltpu.VMEM((4, half, low_rows), BF),
            pltpu.VMEM((2, *windows_own.shape), BF),
            pltpu.SemaphoreType.DMA((2,)),
        ),
        in_specs=[WHOLE] * 5 + [pl.BlockSpec(memory_space=pl.ANY)] * 2,
        out_specs=(WHOLE, WHOLE),
    )(mask, glow_part, glow_got, folded, down_kept, windows_own, windows_pair)
    conv_grads = over_plane(conv_grads)
    glow, windows_own, windows_pair = lax.optimization_barrier((glow, windows_own, windows_pair))

    wide, skip, low_part = kernel_call(
        conv_kernel,
        (
            jax.ShapeDtypeStruct((4, low_rows, half), F32),
            jax.ShapeDtypeStruct((4, low_rows, half), BF),
            jax.ShapeDtypeStruct((low_rows, channels), F32),
        ),
        flops=80 * low_rows * channels * half,
        moved_bytes=18 << 20,
        scratch=(pltpu.VMEM((9, channels, half), BF), pltpu.VMEM((4, half, channels), BF)),
        in_specs=[WHOLE] * 7,
        out_specs=(WHOLE,) * 3,
    )(mask, conv_two, down_kept, windows_own, windows_pair, residual_own, residual_pair)
    low_got = send(low_part, "c")

    *returning, grads = kernel_call(
        functools.partial(output_kernel, extent, loss_scale),
        (
            *(block,) * 4,
            jax.ShapeDtypeStruct((16, 16, rows, half), BF),
        ),
        flops=24 * low_rows * channels * half,
        moved_bytes=14 << 20,
        scratch=(
            pltpu.VMEM((low_rows, channels), BF),
            pltpu.VMEM((4, channels, half), BF),
            pltpu.VMEM((4, low_rows, half), F32),
            laned(extent, extent, half),
            pltpu.VMEM((8 * most, pixels, half), BF),
        ),
        in_specs=[SCALARS] + [WHOLE] * 8,
        out_specs=(WHOLE,) * 5,
    )(meta, mask, low_part, low_got, wide, skip, glow, folded, up_two)
    returned = over_dp(returning)
    grads = over_plane(grads)

    conv_sum = jnp.sum(conv_grads.astype(F32), axis=0).reshape(2, 9, rows, half)
    conv_sum, beside = lax.optimization_barrier((conv_sum, returned[1]))
    returned = (returned[0], beside, *returned[2:])

    def by_core(own, pair):
        return jnp.where(core == 0, jnp.stack([own, pair]), jnp.stack([pair, own]))

    out_conv = by_core(*over_column(conv_sum, y)).transpose(2, 1, 0, 3)
    out_conv = out_conv.reshape(rows, 9, channels)
    grads_sum = jnp.sum(grads.astype(F32), axis=0)
    up_sum, down_sum = grads_sum[:8].reshape(2, 4, rows, half), grads_sum[8:]
    shares = jnp.concatenate([up_sum, jnp.broadcast_to(down_sum, (2, *down_sum.shape))], axis=1)
    shares, out_conv = lax.optimization_barrier((shares, out_conv))
    own, pair = over_column(shares, y)
    out_up = by_core(own[:4], pair[:4]).transpose(2, 1, 0, 3).reshape(rows, 4 * channels)
    out_down = jnp.where(y == core, own[4:], pair[4:])
    out_down = out_down.reshape(2, 4 * rows, half).transpose(1, 0, 2).reshape(4 * rows, channels)

    block_out = kernel_call(
        join_kernel,
        jax.ShapeDtypeStruct((4 * most, pixels, channels), F32),
        flops=0,
        moved_bytes=6 * cotangent.size,
        scratch=(pltpu.VMEM((4, 2 * most, pixels, half), F32), pltpu.SemaphoreType.DMA((4,))),
        in_specs=[SCALARS] + [WHOLE] * 4,
        out_specs=pl.BlockSpec(memory_space=pl.ANY),
    )(number, *returned)
    return (block_out.reshape(cotangent.shape), out_conv, out_down, out_up)


def solution(mesh):
    return jax.shard_map(
        per_device,
        mesh=mesh,
        in_specs=(
            P(("dp", "fsdp"), None, None, None),
            P(("dp", "fsdp"), None),
            P(("dp", "fsdp")),
            P(),
            P(),
            P("fsdp", None, None),
            P("fsdp", None),
            P("fsdp", None),
            P(),
            P(),
            P(("dp", "fsdp"), None, None, None),
        ),
        out_specs=(
            P(("dp", "fsdp"), None, None, None),
            P("fsdp", None, None),
            P("fsdp", None),
            P("fsdp", None),
        ),
        check_vma=False,
    )
```

```python
import functools
import math

import jax
import jax.numpy as jnp
from jax import lax
from jax.experimental import pallas as pl
from jax.experimental.pallas import tpu as pltpu
from jax.sharding import PartitionSpec as P

GROUPS = 32
epsilon = 1e-05
BF = jnp.bfloat16
F32 = jnp.float32
I32 = jnp.int32
AXES = ("dp", "fsdp")
VMEM_BYTES = 56 * 1024 * 1024


def moved(fn):
    pairs = []
    for index in range(128):
        dp, fsdp = index // 32, index % 32
        place = (dp // 2, dp % 2, fsdp // 8, fsdp // 4 % 2, fsdp % 4)
        h, c, z, y, x = fn(*place)
        pairs.append((index, (h * 2 + c) * 32 + z * 8 + y * 4 + x))
    return pairs


STEP = {
    "y": moved(lambda h, c, z, y, x: (h, c, z, 1 - y, x)),
    "hy": moved(lambda h, c, z, y, x: (1 - h, c, z, 1 - y, x)),
    "c": moved(lambda h, c, z, y, x: (h, 1 - c, z, y, x)),
    "h": moved(lambda h, c, z, y, x: (1 - h, c, z, y, x)),
    "hc": moved(lambda h, c, z, y, x: (1 - h, 1 - c, z, y, x)),
}
PLANES = [[z * 8 + y * 4 + x for z in range(4) for x in range(4)] for y in range(2)]


def send(value, move):
    return lax.ppermute(value, AXES, STEP[move])


def over_dp(blocks):
    own, beside, across, both = blocks
    return (own, send(beside, "c"), send(across, "h"), send(both, "hc"))


def over_column(parts, y):
    kept = lax.dynamic_index_in_dim(parts, y, axis=0, keepdims=False)
    given = lax.dynamic_index_in_dim(parts, 1 - y, axis=0, keepdims=False)
    sent = given.astype(BF)
    got = (send(sent, "y"), send(kept.astype(BF), "h"), send(sent, "hy"))
    total = kept + got[0].astype(F32) + got[1].astype(F32) + got[2].astype(F32)
    return total, send(total, "c")


def over_plane(blocks):
    return lax.all_to_all(
        blocks, "fsdp", split_axis=0, concat_axis=0, axis_index_groups=PLANES, tiled=True
    )


def dot(left, right, left_dim, right_dim):
    return lax.dot_general(
        left, right, (((left_dim,), (right_dim,)), ((), ())), preferred_element_type=F32
    )


def kernel_call(body, out_shape, flops, moved_bytes, scratch=(), **more):
    return pl.pallas_call(
        body,
        out_shape=out_shape,
        scratch_shapes=list(scratch),
        compiler_params=pltpu.CompilerParams(vmem_limit_bytes=VMEM_BYTES),
        cost_estimate=pl.CostEstimate(
            flops=int(flops), bytes_accessed=int(moved_bytes), transcendentals=0
        ),
        **more,
    )


def laned(extent_rows, extent_columns, lanes):
    block = min(128, lanes)
    return pltpu.VMEM((lanes // block, extent_rows, extent_columns, block), F32)


def put_line(ref, row, first, values):
    block = ref.shape[3]
    for b in range(ref.shape[0]):
        ref[b, row, first : first + values.shape[0], :] = values[:, b * block : (b + 1) * block]


def get_line(ref, row):
    return jnp.concatenate([ref[b, row] for b in range(ref.shape[0])], axis=1)


def every_second(ref, row, first, side):
    places = [
        ref[pl.ds(b, 1), pl.ds(row, 1), pl.ds(first, side, stride=2), :].reshape(side, ref.shape[3])
        for b in range(ref.shape[0])
    ]
    return jnp.concatenate(places, axis=1)


def put_every_second(ref, row, first, values):
    side, block = values.shape[0], ref.shape[3]
    for b in range(ref.shape[0]):
        ref[pl.ds(b, 1), pl.ds(row, 1), pl.ds(first, side, stride=2), :] = values[
            :, b * block : (b + 1) * block
        ].reshape(1, 1, side, block)


WHOLE = pl.BlockSpec(memory_space=pltpu.VMEM)
SCALARS = pl.BlockSpec(memory_space=pltpu.SMEM)


def over_group(sums, width):
    lane = lax.broadcasted_iota(I32, sums.shape, 1)
    step = width // 2
    while step:
        lower = (lane & step) == 0
        lanes = sums.shape[1]
        sums = sums + jnp.where(
            lower, pltpu.roll(sums, lanes - step, 1), pltpu.roll(sums, step, 1)
        )
        step //= 2
    return sums


def norm_kernel(extent, meta, image, gain, shift, windows, residual, padded, raw):
    place = pl.program_id(0)
    channels = image.shape[2]
    half = channels // 2
    height, width = meta[place], meta[8 + place]
    core = meta[24]

    @pl.when(place == 0)
    def _():
        padded[...] = jnp.zeros_like(padded)

    inside = lax.broadcasted_iota(I32, (extent, channels), 0) < width

    def line(row):
        return image[0, row * extent : (row + 1) * extent, :].astype(F32)

    def mask(row):
        return (inside & (row < height)).astype(F32)

    group = channels // GROUPS
    counted = jnp.maximum((height * width * group).astype(F32), 1.0)
    total = jnp.zeros((extent, channels), F32)
    for row in range(extent):
        total = total + line(row) * mask(row)
    total = jnp.broadcast_to(jnp.sum(total, axis=0, keepdims=True), (8, channels))
    mean = (over_group(total, group) / counted)[:1]
    total = jnp.zeros((extent, channels), F32)
    for row in range(extent):
        centred = (line(row) - mean) * mask(row)
        total = total + centred * centred
    total = jnp.broadcast_to(jnp.sum(total, axis=0, keepdims=True), (8, channels))
    variance = (over_group(total, group) / counted)[:1]
    scale = lax.rsqrt(variance + epsilon) * gain[...]
    for row in range(extent):
        normed = (line(row) - mean) * scale + shift[...]
        put_line(padded, row + 1, 8, normed / (1.0 + jnp.exp(-normed)) * mask(row))
        residue = image[
            0, row * extent : (row + 1) * extent, pl.ds(pl.multiple_of(core * half, half), half)
        ]
        put_line(raw, row, 0, residue.astype(F32))
    side = extent // 2
    for p in range(4):
        for q in range(4):
            for i in range(0, side, 2):
                pair = [every_second(padded, 2 * n + p, 7 + q, side) for n in (i, i + 1)]
                windows[p * 4 + q, i * side : (i + 2) * side, :] = jnp.concatenate(pair).astype(BF)
    for k in range(4):
        for i in range(0, side, 2):
            pair = [every_second(raw, 2 * n + k // 2, k % 2, side) for n in (i, i + 1)]
            residual[k, i * side : (i + 2) * side, :] = jnp.concatenate(pair).astype(BF)


def normed_windows(meta, images, gain, shift):
    count, extent, _, channels = images.shape
    pixels, half = extent * extent, channels // 2
    quarter = pixels // 4
    return kernel_call(
        functools.partial(norm_kernel, extent),
        (
            jax.ShapeDtypeStruct((16, count * quarter, channels), BF),
            jax.ShapeDtypeStruct((4, count * quarter, half), BF),
        ),
        flops=40 * images.size,
        moved_bytes=12 * images.size,
        scratch=(
            laned(extent + 2, extent + 16, channels),
            laned(extent, extent, half),
        ),
        grid=(count,),
        in_specs=[
            SCALARS,
            pl.BlockSpec((1, pixels, channels), lambda g: (g, 0, 0)),
            pl.BlockSpec((1, channels), lambda g: (0, 0)),
            pl.BlockSpec((1, channels), lambda g: (0, 0)),
        ],
        out_specs=(
            pl.BlockSpec((16, quarter, channels), lambda g: (0, g, 0)),
            pl.BlockSpec((4, quarter, half), lambda g: (0, g, 0)),
        ),
    )(meta, images.reshape(count, pixels, channels), gain[None, :], shift[None, :])


def gather_up(pieces, up):
    rows = pieces.shape[2]
    for f in range(32):
        z, y, x = f // 8, f // 4 % 2, f % 4
        for k in range(4):
            up[k, f * rows : (f + 1) * rows, :] = pieces[z * 4 + x, y * 4 + k]


def gather_down(pieces, down):
    rows, half = pieces.shape[2:]
    for z in range(4):
        for x in range(4):
            for unit in range(8):
                side, step = unit // 4, unit % 4
                first = (x * 4 + step) * rows
                down[z, first : first + rows, side * half : (side + 1) * half] = pieces[
                    z * 4 + x, 8 + unit
                ]


def swapped_sum(own, got):
    middle = own.shape[0] // 2
    return jnp.concatenate(
        [own[:middle] + got[middle:], own[middle:] + got[:middle]], axis=0
    ).astype(BF)


def fold_kernel(extent, meta, cot0, cot1, cot2, cot3, folded, raw, cot, sem):
    side = extent // 2
    quarter = side * side
    half = cot.shape[2]
    slots = cot0.shape[0]
    copies = [
        pltpu.make_async_copy(ref, cot.at[pl.ds(r * slots, slots)], sem.at[r])
        for r, ref in enumerate((cot0, cot1, cot2, cot3))
    ]
    for copy in copies:
        copy.start()
    for copy in copies:
        copy.wait()
    images = folded.shape[1] // quarter
    inside = lax.broadcasted_iota(I32, (extent, half), 0)

    def one(g, carry):
        height, width, slot = meta[g], meta[8 + g], meta[16 + g]
        for row in range(extent):
            kept = ((inside < width) & (row < height)).astype(F32)
            line = cot[slot, row * extent : (row + 1) * extent, :].astype(F32)
            put_line(raw, row, 0, line * kept)
        for k in range(4):
            for i in range(0, side, 2):
                pair = [every_second(raw, 2 * n + k // 2, k % 2, side) for n in (i, i + 1)]
                first = pl.multiple_of(g * quarter + i * side, 2 * side)
                folded[k, pl.ds(first, 2 * side), :] = jnp.concatenate(pair).astype(BF)
        return carry

    lax.fori_loop(0, images, one, 0)


def glow_kernel(loss_scale, folded, pieces, part, up, held, sem):
    copy = pltpu.make_async_copy(pieces.at[:, pl.ds(0, 8)], held, sem)
    copy.start()
    copy.wait()
    gather_up(held, up)
    total = None
    for k in range(4):
        scaled = (folded[k].astype(F32) * loss_scale).astype(BF)
        term = dot(scaled, up[k], 1, 1)
        total = term if total is None else total + term
    part[...] = total


def grad_conv_kernel(
    loss_scale,
    mask,
    own,
    got,
    folded,
    pieces,
    windows_own,
    windows_pair,
    glow,
    grads,
    down,
    turned,
    sums,
    windows,
    sem,
):
    half = folded.shape[2]
    copies = [
        pltpu.make_async_copy(ref, windows.at[part], sem.at[part])
        for part, ref in enumerate((windows_own, windows_pair))
    ]
    for copy in copies:
        copy.start()
    rows = grads.shape[2]
    middle = folded.shape[1] // 2
    gather_down(pieces, down)
    glow[...] = swapped_sum(own, got)
    kept = jnp.concatenate([mask[...]] * (half // mask.shape[1]), axis=1)
    for k in range(4):
        grad = folded[k].astype(F32) * loss_scale + dot(glow[...], down[k], 1, 1)
        turned[k] = (grad * kept).T.astype(BF)
    for copy in copies:
        copy.wait()
    seen = set()
    for v in range(16):
        p, q = v // 4, v % 4
        users = [k for k in range(4) if 0 <= p - k // 2 < 3 and 0 <= q - k % 2 < 3]
        term = None
        for part in range(2):
            columns = slice(part * middle, (part + 1) * middle)
            left = jnp.concatenate([turned[k, :, columns] for k in users])
            piece = dot(left, windows[part, v], 1, 0)
            term = piece if term is None else term + piece
        for place, k in enumerate(users):
            t = (p - k // 2) * 3 + q - k % 2
            piece = term[place * half : (place + 1) * half]
            sums[t] = sums[t] + piece if t in seen else piece
            seen.add(t)
    for t in range(9):
        total = sums[t].T.astype(BF)
        for f in range(32):
            z, y, x = f // 8, f // 4 % 2, f % 4
            grads[z * 4 + x, y * 9 + t] = total[f * rows : (f + 1) * rows, :]


def conv_kernel(
    mask,
    conv_pieces,
    pieces,
    windows_own,
    windows_pair,
    residual_own,
    residual_pair,
    wide,
    skip,
    part,
    conv,
    down,
):
    half = wide.shape[2]
    rows = conv_pieces.shape[2]
    middle = wide.shape[1] // 2
    for f in range(32):
        z, y, x = f // 8, f // 4 % 2, f % 4
        for t in range(9):
            conv[t, f * rows : (f + 1) * rows, :] = conv_pieces[z * 4 + x, y * 9 + t]
    gather_down(pieces, down)
    total = None
    for k in range(4):
        for first, windows, residual in (
            (0, windows_own, residual_own),
            (middle, windows_pair, residual_pair),
        ):
            convolved = None
            for t in range(9):
                v = (k // 2 + t // 3) * 4 + k % 2 + t % 3
                term = dot(windows[v], conv[t], 1, 0)
                convolved = term if convolved is None else convolved + term
            kept = mask[first : first + middle, :]
            kept = jnp.concatenate([kept] * (half // mask.shape[1]), axis=1)
            masked = (residual[k].astype(F32) + convolved) * kept
            wide[k, first : first + middle, :] = masked
            skip[k, first : first + middle, :] = masked.astype(BF)
        term = dot(skip[k], down[k], 1, 0)
        total = term if total is None else total + term
    part[...] = total


def output_kernel(
    extent,
    loss_scale,
    meta,
    mask,
    own,
    got,
    wide,
    skip,
    glow,
    folded,
    pieces,
    back0,
    back1,
    back2,
    back3,
    grads,
    low,
    up,
    outputs,
    raw,
    returning,
):
    side = extent // 2
    quarter = side * side
    half = wide.shape[2]
    rows = grads.shape[2]
    images = wide.shape[1] // quarter
    gather_up(pieces, up)
    low[...] = swapped_sum(own, got)
    kept = jnp.concatenate([mask[...]] * (half // mask.shape[1]), axis=1)
    for k in range(4):
        outputs[k] = (wide[k] + dot(low[...], up[k], 1, 0)) * kept
    returning[...] = jnp.zeros_like(returning)

    def one(g, carry):
        slot = meta[16 + g]
        for k in range(4):
            for i in range(side):
                first = pl.multiple_of(g * quarter + i * side, side)
                put_every_second(raw, 2 * i + k // 2, k % 2, outputs[k, pl.ds(first, side), :])
        for row in range(extent):
            returning[slot, row * extent : (row + 1) * extent, :] = get_line(raw, row).astype(BF)
        return carry

    lax.fori_loop(0, images, one, 0)
    slots = back0.shape[0]
    for r, back in enumerate((back0, back1, back2, back3)):
        back[...] = returning[r * slots : (r + 1) * slots]
    turned = low[...].astype(F32).T.astype(BF)
    for k in range(4):
        scaled = (folded[k].astype(F32) * loss_scale).astype(BF)
        grad = dot(turned, scaled, 1, 0).astype(BF)
        for f in range(32):
            z, y, x = f // 8, f // 4 % 2, f % 4
            grads[z * 4 + x, y * 4 + k] = grad[f * rows : (f + 1) * rows, :]
        grad = dot(skip[k].astype(F32).T.astype(BF), glow[...], 1, 0).astype(BF)
        for x in range(4):
            for unit in range(8):
                side_of, step = unit // 4, unit % 4
                first = (x * 4 + step) * rows
                grads[k * 4 + x, 8 + unit] = grad[
                    first : first + rows, side_of * half : (side_of + 1) * half
                ]


def replicas(number, half):
    for r in range(4):
        chip, core = number // 2, number % 2
        chip = 1 - chip if r // 2 else chip
        core = 1 - core if r % 2 else core
        yield r, chip, pl.ds(pl.multiple_of(core * half, half), half)


def split_kernel(number, cot, out0, out1, out2, out3):
    outs = (out0, out1, out2, out3)
    slots, _, half = out0.shape
    for r, chip, lanes in replicas(number[0], half):
        outs[r][...] = cot[pl.ds(chip * slots, slots), :, lanes]


def join_kernel(number, back0, back1, back2, back3, out, wide, sem):
    backs = (back0, back1, back2, back3)
    slots, _, half = back0.shape
    copies = []
    for r, chip, lanes in replicas(number[0], half):
        wide[r] = backs[r][...].astype(F32)
        target = out.at[pl.ds(chip * slots, slots), :, lanes]
        copies.append(pltpu.make_async_copy(wide.at[r], target, sem.at[r]))
        copies[-1].start()
    for copy in copies:
        copy.wait()


def per_device(
    images, routes, bucket, heights, widths, w_conv, w_down, w_up, norm_gain, norm_shift, cotangent
):
    count, extent, _, channels = images.shape
    half = channels // 2
    pixels = extent * extent
    quarter = pixels // 4
    most = cotangent.shape[0] // 4
    rows = w_conv.shape[0]
    low_rows = 2 * count * quarter
    loss_scale = 1.0 / math.sqrt(count * 128 * pixels)
    dp, fsdp = lax.axis_index("dp"), lax.axis_index("fsdp")
    core, y = dp % 2, fsdp // 4 % 2

    conv_own = lax.dynamic_slice_in_dim(w_conv, core * half, half, axis=2).transpose(1, 0, 2)
    up_own = lax.dynamic_slice_in_dim(
        w_up.reshape(rows, 4, channels), core * half, half, axis=2
    ).transpose(1, 0, 2)
    down_own = w_down.reshape(4 * rows, 2, half).transpose(1, 0, 2).reshape(8, rows, half)
    packed = jnp.concatenate([up_own, down_own, conv_own])
    other = send(packed, "y")

    block = jax.ShapeDtypeStruct((2 * most, pixels, half), BF)
    number = dp.astype(I32).reshape(1)
    outgoing = kernel_call(
        split_kernel,
        (block,) * 4,
        flops=0,
        moved_bytes=4 * cotangent.size,
        in_specs=[SCALARS, WHOLE],
        out_specs=(WHOLE,) * 4,
    )(number, cotangent.reshape(4 * most, pixels, channels))
    outgoing, other = lax.optimization_barrier((outgoing, other))
    arrived = over_dp(outgoing)
    first = jnp.where(y == 0, packed, other)
    second = jnp.where(y == 0, other, packed)
    down_kept = jnp.where(core == 0, first[4:12], second[4:12])
    up_down = jnp.concatenate([first[:4], second[:4], down_kept])
    conv_two = jnp.concatenate([first[12:], second[12:]])
    up_down = over_plane(jnp.broadcast_to(up_down, (16, *up_down.shape)))
    conv_two = lax.all_gather(conv_two, "fsdp", axis_index_groups=PLANES)

    images_pair = send(images, "c")
    ids = jnp.concatenate([routes, bucket[:, None]], axis=1)
    ids_pair = send(ids, "c")

    def described(table, side):
        target = table[:, 0]
        position = jnp.arange(count, dtype=I32)
        earlier = position[None, :] < position[:, None]
        same_owner = target[:, None] == target[None, :]
        order_in = jnp.sum((same_owner & earlier).astype(I32), axis=1)
        slot = (target ^ dp) * 2 * most + side * most + order_in
        chosen = table[:, 1][:, None] == jnp.arange(heights.shape[0], dtype=I32)[None, :]
        height = jnp.sum(jnp.where(chosen, heights[None, :], 0), axis=1)
        width = jnp.sum(jnp.where(chosen, widths[None, :], 0), axis=1)
        return jnp.stack([height, width, slot])

    def numbers(first, second):
        parts = jnp.concatenate([first, second], axis=1).reshape(-1)
        return jnp.concatenate([parts, jnp.broadcast_to(core, (8,)).astype(I32)])

    own_facts, pair_facts = described(ids, core), described(ids_pair, 1 - core)
    own_meta = numbers(own_facts, own_facts)
    pair_meta = numbers(pair_facts, pair_facts)
    meta = numbers(own_facts, pair_facts)
    height, width = meta[:8], meta[8:16]
    place = jnp.arange(extent // 2, dtype=I32) * 2
    mask = (place[None, :, None] < height[:, None, None]) & (
        place[None, None, :] < width[:, None, None]
    )
    mask = jnp.broadcast_to(mask.astype(F32).reshape(low_rows, 1), (low_rows, min(128, half)))

    windows_own, residual_own = normed_windows(own_meta, images, norm_gain, norm_shift)
    windows_pair, residual_pair = normed_windows(pair_meta, images_pair, norm_gain, norm_shift)

    ready, mask, windows_own, windows_pair = lax.optimization_barrier(
        (meta, mask, windows_own, windows_pair)
    )
    folded = kernel_call(
        functools.partial(fold_kernel, extent),
        jax.ShapeDtypeStruct((4, low_rows, half), BF),
        flops=0,
        moved_bytes=3 << 20,
        scratch=(
            laned(extent, extent, half),
            pltpu.VMEM((8 * most, pixels, half), BF),
            pltpu.SemaphoreType.DMA((4,)),
        ),
        in_specs=[SCALARS] + [pl.BlockSpec(memory_space=pl.ANY)] * 4,
        out_specs=WHOLE,
    )(ready, *arrived)
    glow_part = kernel_call(
        functools.partial(glow_kernel, loss_scale),
        jax.ShapeDtypeStruct((low_rows, channels), F32),
        flops=8 * low_rows * channels * half,
        moved_bytes=3 << 20,
        scratch=(
            pltpu.VMEM((4, channels, half), BF),
            pltpu.VMEM((16, 8, rows, half), BF),
            pltpu.SemaphoreType.DMA,
        ),
        in_specs=[WHOLE, pl.BlockSpec(memory_space=pl.ANY)],
        out_specs=WHOLE,
    )(folded, up_down)
    glow_got = send(glow_part, "c")

    glow, conv_grads = kernel_call(
        functools.partial(grad_conv_kernel, loss_scale),
        (
            jax.ShapeDtypeStruct((low_rows, channels), BF),
            jax.ShapeDtypeStruct((16, 18, rows, half), BF),
        ),
        flops=80 * low_rows * channels * half,
        moved_bytes=15 << 20,
        scratch=(
            pltpu.VMEM((4, half, channels), BF),
            pltpu.VMEM((4, half, low_rows), BF),
            pltpu.VMEM((9, half, channels), F32),
            pltpu.VMEM((2, *windows_own.shape), BF),
            pltpu.SemaphoreType.DMA((2,)),
        ),
        in_specs=[WHOLE] * 5 + [pl.BlockSpec(memory_space=pl.ANY)] * 2,
        out_specs=(WHOLE, WHOLE),
    )(mask, glow_part, glow_got, folded, up_down, windows_own, windows_pair)
    conv_grads = over_plane(conv_grads)
    glow, windows_own, windows_pair = lax.optimization_barrier((glow, windows_own, windows_pair))

    wide, skip, low_part = kernel_call(
        conv_kernel,
        (
            jax.ShapeDtypeStruct((4, low_rows, half), F32),
            jax.ShapeDtypeStruct((4, low_rows, half), BF),
            jax.ShapeDtypeStruct((low_rows, channels), F32),
        ),
        flops=80 * low_rows * channels * half,
        moved_bytes=18 << 20,
        scratch=(pltpu.VMEM((9, channels, half), BF), pltpu.VMEM((4, half, channels), BF)),
        in_specs=[WHOLE] * 7,
        out_specs=(WHOLE,) * 3,
    )(mask, conv_two, up_down, windows_own, windows_pair, residual_own, residual_pair)
    low_got = send(low_part, "c")

    *returning, grads = kernel_call(
        functools.partial(output_kernel, extent, loss_scale),
        (
            *(block,) * 4,
            jax.ShapeDtypeStruct((16, 16, rows, half), BF),
        ),
        flops=24 * low_rows * channels * half,
        moved_bytes=14 << 20,
        scratch=(
            pltpu.VMEM((low_rows, channels), BF),
            pltpu.VMEM((4, channels, half), BF),
            pltpu.VMEM((4, low_rows, half), F32),
            laned(extent, extent, half),
            pltpu.VMEM((8 * most, pixels, half), BF),
        ),
        in_specs=[SCALARS] + [WHOLE] * 8,
        out_specs=(WHOLE,) * 5,
    )(meta, mask, low_part, low_got, wide, skip, glow, folded, up_down)
    returned = over_dp(returning)
    grads = over_plane(grads)

    conv_sum = jnp.sum(conv_grads.astype(F32), axis=0).reshape(2, 9, rows, half)
    grads_sum = jnp.sum(grads.astype(F32), axis=0)
    up_sum, down_sum = grads_sum[:8].reshape(2, 4, rows, half), grads_sum[8:]
    down_sum = jnp.broadcast_to(down_sum, (2, *down_sum.shape))
    shares = jnp.concatenate([conv_sum, up_sum, down_sum], axis=1)
    shares, returned = lax.optimization_barrier((shares, returned))
    own, pair = over_column(shares, y)

    def by_core(first, last):
        parts = (own[first:last], pair[first:last])
        both = jnp.where(core == 0, jnp.stack(parts), jnp.stack(parts[::-1]))
        return both.transpose(2, 1, 0, 3)

    out_conv = by_core(0, 9).reshape(rows, 9, channels)
    out_up = by_core(9, 13).reshape(rows, 4 * channels)
    out_down = jnp.where(y == core, own[13:], pair[13:])
    out_down = out_down.reshape(2, 4 * rows, half).transpose(1, 0, 2).reshape(4 * rows, channels)

    block_out = kernel_call(
        join_kernel,
        jax.ShapeDtypeStruct((4 * most, pixels, channels), F32),
        flops=0,
        moved_bytes=6 * cotangent.size,
        scratch=(pltpu.VMEM((4, 2 * most, pixels, half), F32), pltpu.SemaphoreType.DMA((4,))),
        in_specs=[SCALARS] + [WHOLE] * 4,
        out_specs=pl.BlockSpec(memory_space=pl.ANY),
    )(number, *returned)
    return (block_out.reshape(cotangent.shape), out_conv, out_down, out_up)


def solution(mesh):
    return jax.shard_map(
        per_device,
        mesh=mesh,
        in_specs=(
            P(("dp", "fsdp"), None, None, None),
            P(("dp", "fsdp"), None),
            P(("dp", "fsdp")),
            P(),
            P(),
            P("fsdp", None, None),
            P("fsdp", None),
            P("fsdp", None),
            P(),
            P(),
            P(("dp", "fsdp"), None, None, None),
        ),
        out_specs=(
            P(("dp", "fsdp"), None, None, None),
            P("fsdp", None, None),
            P("fsdp", None),
            P("fsdp", None),
        ),
        check_vma=False,
    )
```

```python
import functools
import math

import jax
import jax.numpy as jnp
from jax import lax
from jax.experimental import pallas as pl
from jax.experimental.pallas import tpu as pltpu
from jax.sharding import PartitionSpec as P

GROUPS = 32
epsilon = 1e-05
BF = jnp.bfloat16
F32 = jnp.float32
I32 = jnp.int32
AXES = ("dp", "fsdp")
FIRST = 3
VMEM_BYTES = 56 * 1024 * 1024


def moved(fn):
    pairs = []
    for index in range(128):
        dp, fsdp = index // 32, index % 32
        place = (dp // 2, dp % 2, fsdp // 8, fsdp // 4 % 2, fsdp % 4)
        h, c, z, y, x = fn(*place)
        pairs.append((index, (h * 2 + c) * 32 + z * 8 + y * 4 + x))
    return pairs


STEP = {
    "y": moved(lambda h, c, z, y, x: (h, c, z, 1 - y, x)),
    "hy": moved(lambda h, c, z, y, x: (1 - h, c, z, 1 - y, x)),
    "c": moved(lambda h, c, z, y, x: (h, 1 - c, z, y, x)),
    "h": moved(lambda h, c, z, y, x: (1 - h, c, z, y, x)),
    "hc": moved(lambda h, c, z, y, x: (1 - h, 1 - c, z, y, x)),
}
PLANES = [[z * 8 + y * 4 + x for z in range(4) for x in range(4)] for y in range(2)]


def send(value, move):
    return lax.ppermute(value, AXES, STEP[move])


def over_dp(blocks):
    own, beside, across, both = blocks
    return (own, send(beside, "c"), send(across, "h"), send(both, "hc"))


def over_column(parts, y):
    kept = lax.dynamic_index_in_dim(parts, y, axis=0, keepdims=False)
    given = lax.dynamic_index_in_dim(parts, 1 - y, axis=0, keepdims=False)
    sent = given.astype(BF)
    got = (send(sent, "y"), send(kept.astype(BF), "h"), send(sent, "hy"))
    total = kept + got[0].astype(F32) + got[1].astype(F32) + got[2].astype(F32)
    return total, send(total, "c")


def over_dp_by_chip(blocks):
    own, beside, across, both = blocks
    return (own, send(beside, "c"), send(across, "h"), send(send(both, "h"), "c"))


def over_plane(blocks):
    return lax.all_to_all(
        blocks, "fsdp", split_axis=0, concat_axis=0, axis_index_groups=PLANES, tiled=True
    )


def dot(left, right, left_dim, right_dim):
    return lax.dot_general(
        left, right, (((left_dim,), (right_dim,)), ((), ())), preferred_element_type=F32
    )


def kernel_call(body, out_shape, flops, moved_bytes, scratch=(), **more):
    return pl.pallas_call(
        body,
        out_shape=out_shape,
        scratch_shapes=list(scratch),
        compiler_params=pltpu.CompilerParams(vmem_limit_bytes=VMEM_BYTES),
        cost_estimate=pl.CostEstimate(
            flops=int(flops), bytes_accessed=int(moved_bytes), transcendentals=0
        ),
        **more,
    )


def laned(extent_rows, extent_columns, lanes):
    block = min(128, lanes)
    return pltpu.VMEM((lanes // block, extent_rows, extent_columns, block), F32)


def put_line(ref, row, first, values):
    block = ref.shape[3]
    for b in range(ref.shape[0]):
        ref[b, row, first : first + values.shape[0], :] = values[:, b * block : (b + 1) * block]


def get_line(ref, row):
    return jnp.concatenate([ref[b, row] for b in range(ref.shape[0])], axis=1)


def every_second(ref, row, first, side):
    places = [
        ref[pl.ds(b, 1), pl.ds(row, 1), pl.ds(first, side, stride=2), :].reshape(side, ref.shape[3])
        for b in range(ref.shape[0])
    ]
    return jnp.concatenate(places, axis=1)


def put_every_second(ref, row, first, values):
    side, block = values.shape[0], ref.shape[3]
    for b in range(ref.shape[0]):
        ref[pl.ds(b, 1), pl.ds(row, 1), pl.ds(first, side, stride=2), :] = values[
            :, b * block : (b + 1) * block
        ].reshape(1, 1, side, block)


WHOLE = pl.BlockSpec(memory_space=pltpu.VMEM)
SCALARS = pl.BlockSpec(memory_space=pltpu.SMEM)


def over_group(sums, width):
    lane = lax.broadcasted_iota(I32, sums.shape, 1)
    step = width // 2
    while step:
        lower = (lane & step) == 0
        lanes = sums.shape[1]
        sums = sums + jnp.where(
            lower, pltpu.roll(sums, lanes - step, 1), pltpu.roll(sums, step, 1)
        )
        step //= 2
    return sums


def norm_kernel(extent, meta, image, gain, shift, windows, residual, padded, raw):
    place = pl.program_id(0)
    channels = image.shape[2]
    half = channels // 2
    height, width = meta[place], meta[8 + place]
    core = meta[24]

    @pl.when(place == 0)
    def _():
        padded[...] = jnp.zeros_like(padded)

    inside = lax.broadcasted_iota(I32, (extent, channels), 0) < width

    def line(row):
        return image[0, row * extent : (row + 1) * extent, :].astype(F32)

    def mask(row):
        return (inside & (row < height)).astype(F32)

    group = channels // GROUPS
    counted = jnp.maximum((height * width * group).astype(F32), 1.0)
    total = jnp.zeros((extent, channels), F32)
    for row in range(extent):
        total = total + line(row) * mask(row)
    total = jnp.broadcast_to(jnp.sum(total, axis=0, keepdims=True), (8, channels))
    mean = (over_group(total, group) / counted)[:1]
    total = jnp.zeros((extent, channels), F32)
    for row in range(extent):
        centred = (line(row) - mean) * mask(row)
        total = total + centred * centred
    total = jnp.broadcast_to(jnp.sum(total, axis=0, keepdims=True), (8, channels))
    variance = (over_group(total, group) / counted)[:1]
    scale = lax.rsqrt(variance + epsilon) * gain[...]
    for row in range(extent):
        normed = (line(row) - mean) * scale + shift[...]
        put_line(padded, row + 1, 8, normed / (1.0 + jnp.exp(-normed)) * mask(row))
        residue = image[
            0, row * extent : (row + 1) * extent, pl.ds(pl.multiple_of(core * half, half), half)
        ]
        put_line(raw, row, 0, residue.astype(F32))
    side = extent // 2
    for p in range(4):
        for q in range(4):
            for i in range(0, side, 2):
                pair = [every_second(padded, 2 * n + p, 7 + q, side) for n in (i, i + 1)]
                windows[p * 4 + q, i * side : (i + 2) * side, :] = jnp.concatenate(pair).astype(BF)
    for k in range(4):
        for i in range(0, side, 2):
            pair = [every_second(raw, 2 * n + k // 2, k % 2, side) for n in (i, i + 1)]
            residual[k, i * side : (i + 2) * side, :] = jnp.concatenate(pair).astype(BF)


def normed_windows(meta, images, gain, shift):
    count, extent, _, channels = images.shape
    pixels, half = extent * extent, channels // 2
    quarter = pixels // 4
    return kernel_call(
        functools.partial(norm_kernel, extent),
        (
            jax.ShapeDtypeStruct((16, count * quarter, channels), BF),
            jax.ShapeDtypeStruct((4, count * quarter, half), BF),
        ),
        flops=40 * images.size,
        moved_bytes=12 * images.size,
        scratch=(
            laned(extent + 2, extent + 16, channels),
            laned(extent, extent, half),
        ),
        grid=(count,),
        in_specs=[
            SCALARS,
            pl.BlockSpec((1, pixels, channels), lambda g: (g, 0, 0)),
            pl.BlockSpec((1, channels), lambda g: (0, 0)),
            pl.BlockSpec((1, channels), lambda g: (0, 0)),
        ],
        out_specs=(
            pl.BlockSpec((16, quarter, channels), lambda g: (0, g, 0)),
            pl.BlockSpec((4, quarter, half), lambda g: (0, g, 0)),
        ),
    )(meta, images.reshape(count, pixels, channels), gain[None, :], shift[None, :])


def gather_up(pieces, up):
    rows = pieces.shape[2]
    for f in range(32):
        z, y, x = f // 8, f // 4 % 2, f % 4
        for k in range(4):
            up[k, f * rows : (f + 1) * rows, :] = pieces[z * 4 + x, y * 4 + k]


def gather_down(pieces, down):
    rows, half = pieces.shape[2:]
    for z in range(4):
        for x in range(4):
            for unit in range(8):
                side, step = unit // 4, unit % 4
                first = (x * 4 + step) * rows
                down[z, first : first + rows, side * half : (side + 1) * half] = pieces[
                    z * 4 + x, unit
                ]


def swapped_sum(own, got):
    middle = own.shape[0] // 2
    return jnp.concatenate(
        [own[:middle] + got[middle:], own[middle:] + got[:middle]], axis=0
    ).astype(BF)


def fold_kernel(extent, meta, cot0, cot1, cot2, cot3, folded, raw, cot, sem):
    side = extent // 2
    quarter = side * side
    half = cot.shape[2]
    slots = cot0.shape[0]
    copies = [
        pltpu.make_async_copy(ref, cot.at[pl.ds(r * slots, slots)], sem.at[r])
        for r, ref in enumerate((cot0, cot1, cot2, cot3))
    ]
    for copy in copies:
        copy.start()
    for copy in copies:
        copy.wait()
    images = folded.shape[1] // quarter
    inside = lax.broadcasted_iota(I32, (extent, half), 0)

    def one(g, carry):
        height, width, slot = meta[g], meta[8 + g], meta[16 + g]
        for row in range(extent):
            kept = ((inside < width) & (row < height)).astype(F32)
            line = cot[slot, row * extent : (row + 1) * extent, :].astype(F32)
            put_line(raw, row, 0, line * kept)
        for k in range(4):
            for i in range(0, side, 2):
                pair = [every_second(raw, 2 * n + k // 2, k % 2, side) for n in (i, i + 1)]
                first = pl.multiple_of(g * quarter + i * side, 2 * side)
                folded[k, pl.ds(first, 2 * side), :] = jnp.concatenate(pair).astype(BF)
        return carry

    lax.fori_loop(0, images, one, 0)


def glow_kernel(loss_scale, folded, pieces, part, up, held, sem):
    copy = pltpu.make_async_copy(pieces.at[:, pl.ds(0, 8)], held, sem)
    copy.start()
    copy.wait()
    gather_up(held, up)
    total = None
    for k in range(4):
        scaled = (folded[k].astype(F32) * loss_scale).astype(BF)
        term = dot(scaled, up[k], 1, 1)
        total = term if total is None else total + term
    part[...] = total


def tap_grads(taps, turned, windows, sums, grads):
    half = turned.shape[1]
    middle = turned.shape[2] // 2
    rows = grads.shape[2]
    seen = set()
    for p in range(4):
        for q in range(4):
            users = []
            for k in range(4):
                dy, dx = p - k // 2, q - k % 2
                if 0 <= dy < 3 and 0 <= dx < 3 and dy * 3 + dx in taps:
                    users.append((k, taps.index(dy * 3 + dx)))
            if not users:
                continue
            term = None
            for part in range(2):
                columns = slice(part * middle, (part + 1) * middle)
                left = jnp.concatenate([turned[k, :, columns] for k, _ in users])
                piece = dot(left, windows[part, p * 4 + q], 1, 0)
                term = piece if term is None else term + piece
            for place, (_, t) in enumerate(users):
                piece = term[place * half : (place + 1) * half]
                sums[t] = sums[t] + piece if t in seen else piece
                seen.add(t)
    for t in range(len(taps)):
        total = sums[t].T.astype(BF)
        for f in range(32):
            z, y, x = f // 8, f // 4 % 2, f % 4
            grads[z * 4 + x, y * len(taps) + t] = total[f * rows : (f + 1) * rows, :]


def window_copies(first, last, windows_own, windows_pair, windows, sem):
    part_of = pl.ds(first, last - first)
    return [
        pltpu.make_async_copy(ref.at[part_of], windows.at[part, part_of], sem.at[part])
        for part, ref in enumerate((windows_own, windows_pair))
    ]


def first_taps_kernel(
    loss_scale,
    mask,
    own,
    got_far,
    folded,
    pieces,
    windows_own,
    windows_pair,
    glow,
    turned,
    grads,
    down,
    got,
    held,
    sums,
    windows,
    sem,
):
    half = folded.shape[2]
    fetched = [
        pltpu.make_async_copy(got_far, got, sem.at[2]),
        pltpu.make_async_copy(pieces.at[:, pl.ds(8, 8)], held, sem.at[3]),
    ]
    copies = window_copies(0, 8, windows_own, windows_pair, windows, sem)
    for copy in fetched + copies:
        copy.start()
    for copy in fetched:
        copy.wait()
    gather_down(held, down)
    glow[...] = swapped_sum(own, got)
    kept = jnp.concatenate([mask[...]] * (half // mask.shape[1]), axis=1)
    for k in range(4):
        grad = folded[k].astype(F32) * loss_scale + dot(glow[...], down[k], 1, 1)
        turned[k] = (grad * kept).T.astype(BF)
    for copy in copies:
        copy.wait()
    tap_grads(list(range(FIRST)), turned, windows, sums, grads)


def other_taps_kernel(turned, windows_own, windows_pair, grads, sums, windows, sem):
    copies = window_copies(4, 16, windows_own, windows_pair, windows, sem)
    for copy in copies:
        copy.start()
    for copy in copies:
        copy.wait()
    tap_grads(list(range(FIRST, 9)), turned, windows, sums, grads)


def conv_kernel(
    mask,
    conv_pieces,
    pieces,
    windows_own,
    windows_pair,
    residual_own,
    residual_pair,
    wide,
    skip,
    part,
    conv,
    down,
    held,
    sem,
):
    half = wide.shape[2]
    rows = conv_pieces.shape[2]
    middle = wide.shape[1] // 2
    copy = pltpu.make_async_copy(pieces.at[:, pl.ds(8, 8)], held, sem)
    copy.start()
    for f in range(32):
        z, y, x = f // 8, f // 4 % 2, f % 4
        for t in range(9):
            conv[t, f * rows : (f + 1) * rows, :] = conv_pieces[z * 4 + x, y * 9 + t]
    copy.wait()
    gather_down(held, down)
    total = None
    for k in range(4):
        for first, windows, residual in (
            (0, windows_own, residual_own),
            (middle, windows_pair, residual_pair),
        ):
            convolved = None
            for t in range(9):
                v = (k // 2 + t // 3) * 4 + k % 2 + t % 3
                term = dot(windows[v], conv[t], 1, 0)
                convolved = term if convolved is None else convolved + term
            kept = mask[first : first + middle, :]
            kept = jnp.concatenate([kept] * (half // mask.shape[1]), axis=1)
            masked = (residual[k].astype(F32) + convolved) * kept
            wide[k, first : first + middle, :] = masked
            skip[k, first : first + middle, :] = masked.astype(BF)
        term = dot(skip[k], down[k], 1, 0)
        total = term if total is None else total + term
    part[...] = total


def output_kernel(
    extent,
    loss_scale,
    meta,
    mask,
    own,
    got_far,
    wide,
    skip,
    glow,
    folded,
    pieces,
    back0,
    back1,
    back2,
    back3,
    grads,
    low,
    up,
    outputs,
    raw,
    returning,
    got,
    held,
    sem,
):
    side = extent // 2
    quarter = side * side
    half = wide.shape[2]
    rows = grads.shape[2]
    images = wide.shape[1] // quarter
    copies = [
        pltpu.make_async_copy(got_far, got, sem.at[0]),
        pltpu.make_async_copy(pieces.at[:, pl.ds(0, 8)], held, sem.at[1]),
    ]
    for copy in copies:
        copy.start()
    for copy in copies:
        copy.wait()
    gather_up(held, up)
    low[...] = swapped_sum(own, got)
    kept = jnp.concatenate([mask[...]] * (half // mask.shape[1]), axis=1)
    for k in range(4):
        outputs[k] = (wide[k] + dot(low[...], up[k], 1, 0)) * kept
    returning[...] = jnp.zeros_like(returning)

    def one(g, carry):
        slot = meta[16 + g]
        for k in range(4):
            for i in range(side):
                first = pl.multiple_of(g * quarter + i * side, side)
                put_every_second(raw, 2 * i + k // 2, k % 2, outputs[k, pl.ds(first, side), :])
        for row in range(extent):
            returning[slot, row * extent : (row + 1) * extent, :] = get_line(raw, row).astype(BF)
        return carry

    lax.fori_loop(0, images, one, 0)
    slots = back0.shape[0]
    for r, back in enumerate((back0, back1, back2, back3)):
        back[...] = returning[r * slots : (r + 1) * slots]
    turned = low[...].astype(F32).T.astype(BF)
    for k in range(4):
        scaled = (folded[k].astype(F32) * loss_scale).astype(BF)
        grad = dot(turned, scaled, 1, 0).astype(BF)
        for f in range(32):
            z, y, x = f // 8, f // 4 % 2, f % 4
            grads[z * 4 + x, y * 4 + k] = grad[f * rows : (f + 1) * rows, :]
        grad = dot(skip[k].astype(F32).T.astype(BF), glow[...], 1, 0).astype(BF)
        for x in range(4):
            for unit in range(8):
                side_of, step = unit // 4, unit % 4
                first = (x * 4 + step) * rows
                grads[k * 4 + x, 8 + unit] = grad[
                    first : first + rows, side_of * half : (side_of + 1) * half
                ]


def replicas(number, half):
    for r in range(4):
        chip, core = number // 2, number % 2
        chip = 1 - chip if r // 2 else chip
        core = 1 - core if r % 2 else core
        yield r, chip, pl.ds(pl.multiple_of(core * half, half), half)


def split_kernel(number, cot, out0, out1, out2, out3):
    outs = (out0, out1, out2, out3)
    slots, _, half = out0.shape
    for r, chip, lanes in replicas(number[0], half):
        outs[r][...] = cot[pl.ds(chip * slots, slots), :, lanes]


def join_kernel(number, back0, back1, back2, back3, out, wide, sem):
    backs = (back0, back1, back2, back3)
    slots, _, half = back0.shape
    copies = []
    for r, chip, lanes in replicas(number[0], half):
        wide[r] = backs[r][...].astype(F32)
        target = out.at[pl.ds(chip * slots, slots), :, lanes]
        copies.append(pltpu.make_async_copy(wide.at[r], target, sem.at[r]))
        copies[-1].start()
    for copy in copies:
        copy.wait()


def per_device(
    images, routes, bucket, heights, widths, w_conv, w_down, w_up, norm_gain, norm_shift, cotangent
):
    count, extent, _, channels = images.shape
    half = channels // 2
    pixels = extent * extent
    quarter = pixels // 4
    most = cotangent.shape[0] // 4
    rows = w_conv.shape[0]
    low_rows = 2 * count * quarter
    loss_scale = 1.0 / math.sqrt(count * 128 * pixels)
    dp, fsdp = lax.axis_index("dp"), lax.axis_index("fsdp")
    core, y = dp % 2, fsdp // 4 % 2

    conv_own = lax.dynamic_slice_in_dim(w_conv, core * half, half, axis=2).transpose(1, 0, 2)
    up_own = lax.dynamic_slice_in_dim(
        w_up.reshape(rows, 4, channels), core * half, half, axis=2
    ).transpose(1, 0, 2)
    down_own = w_down.reshape(4 * rows, 2, half).transpose(1, 0, 2).reshape(8, rows, half)
    packed = jnp.concatenate([up_own, down_own, conv_own])
    other = send(packed, "y")

    block = jax.ShapeDtypeStruct((2 * most, pixels, half), BF)
    number = dp.astype(I32).reshape(1)
    outgoing = kernel_call(
        split_kernel,
        (block,) * 4,
        flops=0,
        moved_bytes=4 * cotangent.size,
        in_specs=[SCALARS, WHOLE],
        out_specs=(WHOLE,) * 4,
    )(number, cotangent.reshape(4 * most, pixels, channels))
    outgoing, other = lax.optimization_barrier((outgoing, other))
    arrived = over_dp(outgoing)
    first = jnp.where(y == 0, packed, other)
    second = jnp.where(y == 0, other, packed)
    down_kept = jnp.where(core == 0, first[4:12], second[4:12])
    up_down = jnp.concatenate([first[:4], second[:4], down_kept])
    conv_two = jnp.concatenate([first[12:], second[12:]])
    up_down = over_plane(jnp.broadcast_to(up_down, (16, *up_down.shape)))
    conv_two = lax.all_gather(conv_two, "fsdp", axis_index_groups=PLANES)

    images_pair = send(images, "c")
    ids = jnp.concatenate([routes, bucket[:, None]], axis=1)
    ids_pair = send(ids, "c")

    def described(table, side):
        target = table[:, 0]
        position = jnp.arange(count, dtype=I32)
        earlier = position[None, :] < position[:, None]
        same_owner = target[:, None] == target[None, :]
        order_in = jnp.sum((same_owner & earlier).astype(I32), axis=1)
        slot = (target ^ dp) * 2 * most + side * most + order_in
        chosen = table[:, 1][:, None] == jnp.arange(heights.shape[0], dtype=I32)[None, :]
        height = jnp.sum(jnp.where(chosen, heights[None, :], 0), axis=1)
        width = jnp.sum(jnp.where(chosen, widths[None, :], 0), axis=1)
        return jnp.stack([height, width, slot])

    def numbers(first, second):
        parts = jnp.concatenate([first, second], axis=1).reshape(-1)
        return jnp.concatenate([parts, jnp.broadcast_to(core, (8,)).astype(I32)])

    own_facts, pair_facts = described(ids, core), described(ids_pair, 1 - core)
    own_meta = numbers(own_facts, own_facts)
    pair_meta = numbers(pair_facts, pair_facts)
    meta = numbers(own_facts, pair_facts)
    height, width = meta[:8], meta[8:16]
    place = jnp.arange(extent // 2, dtype=I32) * 2
    mask = (place[None, :, None] < height[:, None, None]) & (
        place[None, None, :] < width[:, None, None]
    )
    mask = jnp.broadcast_to(mask.astype(F32).reshape(low_rows, 1), (low_rows, min(128, half)))

    windows_own, residual_own = normed_windows(own_meta, images, norm_gain, norm_shift)
    windows_pair, residual_pair = normed_windows(pair_meta, images_pair, norm_gain, norm_shift)

    ready, mask, windows_own, windows_pair = lax.optimization_barrier(
        (meta, mask, windows_own, windows_pair)
    )
    folded = kernel_call(
        functools.partial(fold_kernel, extent),
        jax.ShapeDtypeStruct((4, low_rows, half), BF),
        flops=0,
        moved_bytes=3 << 20,
        scratch=(
            laned(extent, extent, half),
            pltpu.VMEM((8 * most, pixels, half), BF),
            pltpu.SemaphoreType.DMA((4,)),
        ),
        in_specs=[SCALARS] + [pl.BlockSpec(memory_space=pl.ANY)] * 4,
        out_specs=WHOLE,
    )(ready, *arrived)
    glow_part = kernel_call(
        functools.partial(glow_kernel, loss_scale),
        jax.ShapeDtypeStruct((low_rows, channels), F32),
        flops=8 * low_rows * channels * half,
        moved_bytes=3 << 20,
        scratch=(
            pltpu.VMEM((4, channels, half), BF),
            pltpu.VMEM((16, 8, rows, half), BF),
            pltpu.SemaphoreType.DMA,
        ),
        in_specs=[WHOLE, pl.BlockSpec(memory_space=pl.ANY)],
        out_specs=WHOLE,
    )(folded, up_down)
    glow_got = send(glow_part, "c")

    held = pltpu.VMEM((16, 8, rows, half), BF)
    far = pl.BlockSpec(memory_space=pl.ANY)
    both_windows = pltpu.VMEM((2, *windows_own.shape), BF)
    glow, turned, first_grads = kernel_call(
        functools.partial(first_taps_kernel, loss_scale),
        (
            jax.ShapeDtypeStruct((low_rows, channels), BF),
            jax.ShapeDtypeStruct((4, half, low_rows), BF),
            jax.ShapeDtypeStruct((16, 2 * FIRST, rows, half), BF),
        ),
        flops=32 * low_rows * channels * half,
        moved_bytes=10 << 20,
        scratch=(
            pltpu.VMEM((4, half, channels), BF),
            pltpu.VMEM((low_rows, channels), F32),
            held,
            pltpu.VMEM((FIRST, half, channels), F32),
            both_windows,
            pltpu.SemaphoreType.DMA((4,)),
        ),
        in_specs=[WHOLE, WHOLE, far, WHOLE, far, far, far],
        out_specs=(WHOLE,) * 3,
    )(mask, glow_part, glow_got, folded, up_down, windows_own, windows_pair)
    first_grads = over_plane(first_grads)
    other_grads = kernel_call(
        other_taps_kernel,
        jax.ShapeDtypeStruct((16, 18 - 2 * FIRST, rows, half), BF),
        flops=48 * low_rows * channels * half,
        moved_bytes=10 << 20,
        scratch=(
            pltpu.VMEM((9 - FIRST, half, channels), F32),
            both_windows,
            pltpu.SemaphoreType.DMA((2,)),
        ),
        in_specs=[WHOLE, far, far],
        out_specs=WHOLE,
    )(turned, windows_own, windows_pair)
    other_grads, windows_own, windows_pair = lax.optimization_barrier(
        (other_grads, windows_own, windows_pair)
    )
    other_grads, first_grads = lax.optimization_barrier((other_grads, first_grads))
    other_grads = over_plane(other_grads)

    wide, skip, low_part = kernel_call(
        conv_kernel,
        (
            jax.ShapeDtypeStruct((4, low_rows, half), F32),
            jax.ShapeDtypeStruct((4, low_rows, half), BF),
            jax.ShapeDtypeStruct((low_rows, channels), F32),
        ),
        flops=80 * low_rows * channels * half,
        moved_bytes=18 << 20,
        scratch=(
            pltpu.VMEM((9, channels, half), BF),
            pltpu.VMEM((4, half, channels), BF),
            held,
            pltpu.SemaphoreType.DMA,
        ),
        in_specs=[WHOLE, WHOLE, far] + [WHOLE] * 4,
        out_specs=(WHOLE,) * 3,
    )(mask, conv_two, up_down, windows_own, windows_pair, residual_own, residual_pair)
    low_got = send(low_part, "c")

    *returning, grads = kernel_call(
        functools.partial(output_kernel, extent, loss_scale),
        (
            *(block,) * 4,
            jax.ShapeDtypeStruct((16, 16, rows, half), BF),
        ),
        flops=24 * low_rows * channels * half,
        moved_bytes=14 << 20,
        scratch=(
            pltpu.VMEM((low_rows, channels), BF),
            pltpu.VMEM((4, channels, half), BF),
            pltpu.VMEM((4, low_rows, half), F32),
            laned(extent, extent, half),
            pltpu.VMEM((8 * most, pixels, half), BF),
            pltpu.VMEM((low_rows, channels), F32),
            held,
            pltpu.SemaphoreType.DMA((2,)),
        ),
        in_specs=[SCALARS, WHOLE, WHOLE, far] + [WHOLE] * 4 + [far],
        out_specs=(WHOLE,) * 5,
    )(meta, mask, low_part, low_got, wide, skip, glow, folded, up_down)
    returned = over_dp_by_chip(returning)
    grads = over_plane(grads)

    conv_sum = jnp.concatenate(
        [
            jnp.sum(part.astype(F32), axis=0).reshape(2, -1, rows, half)
            for part in (first_grads, other_grads)
        ],
        axis=1,
    )
    conv_sum, returned = lax.optimization_barrier((conv_sum, returned))

    def by_core(own, pair):
        both = jnp.where(core == 0, jnp.stack([own, pair]), jnp.stack([pair, own]))
        return both.transpose(2, 1, 0, 3)

    out_conv = by_core(*over_column(conv_sum, y)).reshape(rows, 9, channels)
    grads_sum = jnp.sum(grads.astype(F32), axis=0)
    up_sum, down_sum = grads_sum[:8].reshape(2, 4, rows, half), grads_sum[8:]
    shares = jnp.concatenate([up_sum, jnp.broadcast_to(down_sum, (2, *down_sum.shape))], axis=1)
    shares, out_conv = lax.optimization_barrier((shares, out_conv))
    own, pair = over_column(shares, y)
    out_up = by_core(own[:4], pair[:4]).reshape(rows, 4 * channels)
    out_down = jnp.where(y == core, own[4:], pair[4:])
    out_down = out_down.reshape(2, 4 * rows, half).transpose(1, 0, 2).reshape(4 * rows, channels)

    block_out = kernel_call(
        join_kernel,
        jax.ShapeDtypeStruct((4 * most, pixels, channels), F32),
        flops=0,
        moved_bytes=6 * cotangent.size,
        scratch=(pltpu.VMEM((4, 2 * most, pixels, half), F32), pltpu.SemaphoreType.DMA((4,))),
        in_specs=[SCALARS] + [WHOLE] * 4,
        out_specs=pl.BlockSpec(memory_space=pl.ANY),
    )(number, *returned)
    return (block_out.reshape(cotangent.shape), out_conv, out_down, out_up)


def solution(mesh):
    return jax.shard_map(
        per_device,
        mesh=mesh,
        in_specs=(
            P(("dp", "fsdp"), None, None, None),
            P(("dp", "fsdp"), None),
            P(("dp", "fsdp")),
            P(),
            P(),
            P("fsdp", None, None),
            P("fsdp", None),
            P("fsdp", None),
            P(),
            P(),
            P(("dp", "fsdp"), None, None, None),
        ),
        out_specs=(
            P(("dp", "fsdp"), None, None, None),
            P("fsdp", None, None),
            P("fsdp", None),
            P("fsdp", None),
        ),
        check_vma=False,
    )
```

```python
import functools
import math

import jax
import jax.numpy as jnp
from jax import lax
from jax.experimental import pallas as pl
from jax.experimental.pallas import tpu as pltpu
from jax.sharding import PartitionSpec as P

GROUPS = 32
epsilon = 1e-05
BF = jnp.bfloat16
F32 = jnp.float32
I32 = jnp.int32
AXES = ("dp", "fsdp")
VMEM_BYTES = 56 * 1024 * 1024


def moved(fn):
    pairs = []
    for index in range(128):
        dp, fsdp = index // 32, index % 32
        place = (dp // 2, dp % 2, fsdp // 8, fsdp // 4 % 2, fsdp % 4)
        h, c, z, y, x = fn(*place)
        pairs.append((index, (h * 2 + c) * 32 + z * 8 + y * 4 + x))
    return pairs


STEP = {
    "y": moved(lambda h, c, z, y, x: (h, c, z, 1 - y, x)),
    "hy": moved(lambda h, c, z, y, x: (1 - h, c, z, 1 - y, x)),
    "c": moved(lambda h, c, z, y, x: (h, 1 - c, z, y, x)),
    "h": moved(lambda h, c, z, y, x: (1 - h, c, z, y, x)),
    "hc": moved(lambda h, c, z, y, x: (1 - h, 1 - c, z, y, x)),
}
PLANES = [[z * 8 + y * 4 + x for z in range(4) for x in range(4)] for y in range(2)]


def send(value, move):
    return lax.ppermute(value, AXES, STEP[move])


def over_dp(blocks):
    own, beside, across, both = blocks
    return (own, send(beside, "c"), send(across, "h"), send(both, "hc"))


def over_column(parts, y):
    kept = lax.dynamic_index_in_dim(parts, y, axis=0, keepdims=False)
    given = lax.dynamic_index_in_dim(parts, 1 - y, axis=0, keepdims=False)
    sent = given.astype(BF)
    got = (send(sent, "y"), send(kept.astype(BF), "h"), send(sent, "hy"))
    total = kept + got[0].astype(F32) + got[1].astype(F32) + got[2].astype(F32)
    return total, send(total, "c")


def over_plane(blocks):
    return lax.all_to_all(
        blocks, "fsdp", split_axis=0, concat_axis=0, axis_index_groups=PLANES, tiled=True
    )


def dot(left, right, left_dim, right_dim):
    return lax.dot_general(
        left, right, (((left_dim,), (right_dim,)), ((), ())), preferred_element_type=F32
    )


def kernel_call(body, out_shape, flops, moved_bytes, scratch=(), **more):
    return pl.pallas_call(
        body,
        out_shape=out_shape,
        scratch_shapes=list(scratch),
        compiler_params=pltpu.CompilerParams(vmem_limit_bytes=VMEM_BYTES),
        cost_estimate=pl.CostEstimate(
            flops=int(flops), bytes_accessed=int(moved_bytes), transcendentals=0
        ),
        **more,
    )


def laned(extent_rows, extent_columns, lanes):
    block = min(128, lanes)
    return pltpu.VMEM((lanes // block, extent_rows, extent_columns, block), F32)


def put_line(ref, row, first, values):
    block = ref.shape[3]
    for b in range(ref.shape[0]):
        ref[b, row, first : first + values.shape[0], :] = values[:, b * block : (b + 1) * block]


def get_line(ref, row):
    return jnp.concatenate([ref[b, row] for b in range(ref.shape[0])], axis=1)


def every_second(ref, row, first, side):
    places = [
        ref[pl.ds(b, 1), pl.ds(row, 1), pl.ds(first, side, stride=2), :].reshape(side, ref.shape[3])
        for b in range(ref.shape[0])
    ]
    return jnp.concatenate(places, axis=1)


def put_every_second(ref, row, first, values):
    side, block = values.shape[0], ref.shape[3]
    for b in range(ref.shape[0]):
        ref[pl.ds(b, 1), pl.ds(row, 1), pl.ds(first, side, stride=2), :] = values[
            :, b * block : (b + 1) * block
        ].reshape(1, 1, side, block)


WHOLE = pl.BlockSpec(memory_space=pltpu.VMEM)
SCALARS = pl.BlockSpec(memory_space=pltpu.SMEM)


def over_group(sums, width):
    lane = lax.broadcasted_iota(I32, sums.shape, 1)
    step = width // 2
    while step:
        lower = (lane & step) == 0
        lanes = sums.shape[1]
        sums = sums + jnp.where(
            lower, pltpu.roll(sums, lanes - step, 1), pltpu.roll(sums, step, 1)
        )
        step //= 2
    return sums


def norm_kernel(extent, meta, image, gain, shift, windows, residual, padded, raw):
    place = pl.program_id(0)
    channels = image.shape[2]
    half = channels // 2
    height, width = meta[place], meta[8 + place]
    core = meta[24]

    @pl.when(place == 0)
    def _():
        padded[...] = jnp.zeros_like(padded)

    inside = lax.broadcasted_iota(I32, (extent, channels), 0) < width

    def line(row):
        return image[0, row * extent : (row + 1) * extent, :].astype(F32)

    def mask(row):
        return (inside & (row < height)).astype(F32)

    group = channels // GROUPS
    counted = jnp.maximum((height * width * group).astype(F32), 1.0)
    total = jnp.zeros((extent, channels), F32)
    for row in range(extent):
        total = total + line(row) * mask(row)
    total = jnp.broadcast_to(jnp.sum(total, axis=0, keepdims=True), (8, channels))
    mean = (over_group(total, group) / counted)[:1]
    total = jnp.zeros((extent, channels), F32)
    for row in range(extent):
        centred = (line(row) - mean) * mask(row)
        total = total + centred * centred
    total = jnp.broadcast_to(jnp.sum(total, axis=0, keepdims=True), (8, channels))
    variance = (over_group(total, group) / counted)[:1]
    scale = lax.rsqrt(variance + epsilon) * gain[...]
    for row in range(extent):
        normed = (line(row) - mean) * scale + shift[...]
        put_line(padded, row + 1, 8, normed / (1.0 + jnp.exp(-normed)) * mask(row))
        residue = image[
            0, row * extent : (row + 1) * extent, pl.ds(pl.multiple_of(core * half, half), half)
        ]
        put_line(raw, row, 0, residue.astype(F32))
    side = extent // 2
    for p in range(4):
        for q in range(4):
            for i in range(0, side, 2):
                pair = [every_second(padded, 2 * n + p, 7 + q, side) for n in (i, i + 1)]
                windows[p * 4 + q, i * side : (i + 2) * side, :] = jnp.concatenate(pair).astype(BF)
    for k in range(4):
        for i in range(0, side, 2):
            pair = [every_second(raw, 2 * n + k // 2, k % 2, side) for n in (i, i + 1)]
            residual[k, i * side : (i + 2) * side, :] = jnp.concatenate(pair).astype(BF)


def normed_windows(meta, images, gain, shift):
    count, extent, _, channels = images.shape
    pixels, half = extent * extent, channels // 2
    quarter = pixels // 4
    return kernel_call(
        functools.partial(norm_kernel, extent),
        (
            jax.ShapeDtypeStruct((16, count * quarter, channels), BF),
            jax.ShapeDtypeStruct((4, count * quarter, half), BF),
        ),
        flops=40 * images.size,
        moved_bytes=12 * images.size,
        scratch=(
            laned(extent + 2, extent + 16, channels),
            laned(extent, extent, half),
        ),
        grid=(count,),
        in_specs=[
            SCALARS,
            pl.BlockSpec((1, pixels, channels), lambda g: (g, 0, 0)),
            pl.BlockSpec((1, channels), lambda g: (0, 0)),
            pl.BlockSpec((1, channels), lambda g: (0, 0)),
        ],
        out_specs=(
            pl.BlockSpec((16, quarter, channels), lambda g: (0, g, 0)),
            pl.BlockSpec((4, quarter, half), lambda g: (0, g, 0)),
        ),
    )(meta, images.reshape(count, pixels, channels), gain[None, :], shift[None, :])


def gather_up(pieces, up):
    rows = pieces.shape[2]
    for f in range(32):
        z, y, x = f // 8, f // 4 % 2, f % 4
        for k in range(4):
            up[k, f * rows : (f + 1) * rows, :] = pieces[z * 4 + x, y * 4 + k]


def gather_down(pieces, down):
    rows, half = pieces.shape[2:]
    for z in range(4):
        for x in range(4):
            for unit in range(8):
                side, step = unit // 4, unit % 4
                first = (x * 4 + step) * rows
                down[z, first : first + rows, side * half : (side + 1) * half] = pieces[
                    z * 4 + x, 8 + unit
                ]


def swapped_sum(own, got):
    middle = own.shape[0] // 2
    return jnp.concatenate(
        [own[:middle] + got[middle:], own[middle:] + got[:middle]], axis=0
    ).astype(BF)


def fold_kernel(extent, meta, cot0, cot1, cot2, cot3, folded, turned, raw, cot, sem):
    side = extent // 2
    quarter = side * side
    half = cot.shape[2]
    slots = cot0.shape[0]
    copies = [
        pltpu.make_async_copy(ref, cot.at[pl.ds(r * slots, slots)], sem.at[r])
        for r, ref in enumerate((cot0, cot1, cot2, cot3))
    ]
    for copy in copies:
        copy.start()
    for copy in copies:
        copy.wait()
    images = folded.shape[1] // quarter
    inside = lax.broadcasted_iota(I32, (extent, half), 0)

    def one(g, carry):
        height, width, slot = meta[g], meta[8 + g], meta[16 + g]
        for row in range(extent):
            kept = ((inside < width) & (row < height)).astype(F32)
            line = cot[slot, row * extent : (row + 1) * extent, :].astype(F32)
            put_line(raw, row, 0, line * kept)
        for k in range(4):
            for i in range(0, side, 2):
                pair = [every_second(raw, 2 * n + k // 2, k % 2, side) for n in (i, i + 1)]
                first = pl.multiple_of(g * quarter + i * side, 2 * side)
                folded[k, pl.ds(first, 2 * side), :] = jnp.concatenate(pair).astype(BF)
        return carry

    lax.fori_loop(0, images, one, 0)
    for k in range(4):
        turned[k] = folded[k].astype(F32).T.astype(BF)


def glow_kernel(loss_scale, turned, pieces, part, up, held, sem):
    copy = pltpu.make_async_copy(pieces.at[:, pl.ds(0, 8)], held, sem)
    copy.start()
    copy.wait()
    gather_up(held, up)
    total = None
    for k in range(4):
        scaled = (turned[k].astype(F32) * loss_scale).astype(BF)
        term = dot(up[k], scaled, 1, 0)
        total = term if total is None else total + term
    part[...] = total


def grad_conv_kernel(
    loss_scale,
    mask,
    own,
    got,
    folded,
    pieces,
    windows_own,
    windows_pair,
    glow,
    grads,
    down,
    turned,
    windows,
    sem,
):
    _, half, pixels = folded.shape
    rows = grads.shape[2]
    middle = pixels // 2

    def fetch(t):
        copies = []
        for k in range(4):
            v = (k // 2 + t // 3) * 4 + k % 2 + t % 3
            for part, ref in enumerate((windows_own, windows_pair)):
                place = k * 2 + part
                target = windows.at[t % 2, pl.ds(place * middle, middle)]
                copies.append(pltpu.make_async_copy(ref.at[v], target, sem.at[t % 2, place]))
        for copy in copies:
            copy.start()
        return copies

    coming = fetch(0)
    gather_down(pieces, down)
    glow[...] = jnp.concatenate(
        [own[:, :middle] + got[:, middle:], own[:, middle:] + got[:, :middle]], axis=1
    ).astype(BF)
    kept = jnp.broadcast_to(mask[:1, :], (half, pixels))
    for k in range(4):
        grad = folded[k].astype(F32) * loss_scale + dot(down[k], glow[...], 1, 0)
        turned[:, k * pixels : (k + 1) * pixels] = (grad * kept).astype(BF)
    for t in range(9):
        present, coming = coming, fetch(t + 1) if t < 8 else []
        for copy in present:
            copy.wait()
        total = dot(turned[...], windows[t % 2], 1, 0).T.astype(BF)
        for f in range(32):
            z, y, x = f // 8, f // 4 % 2, f % 4
            grads[z * 4 + x, y * 9 + t] = total[f * rows : (f + 1) * rows, :]


def conv_kernel(
    mask,
    conv_pieces,
    pieces,
    windows_own,
    windows_pair,
    residual_own,
    residual_pair,
    wide,
    skip,
    part,
    conv,
    down,
):
    half = wide.shape[2]
    rows = conv_pieces.shape[2]
    middle = wide.shape[1] // 2
    for f in range(32):
        z, y, x = f // 8, f // 4 % 2, f % 4
        for t in range(9):
            conv[t, f * rows : (f + 1) * rows, :] = conv_pieces[z * 4 + x, y * 9 + t]
    gather_down(pieces, down)
    total = None
    for k in range(4):
        for first, windows, residual in (
            (0, windows_own, residual_own),
            (middle, windows_pair, residual_pair),
        ):
            convolved = None
            for t in range(9):
                v = (k // 2 + t // 3) * 4 + k % 2 + t % 3
                term = dot(windows[v], conv[t], 1, 0)
                convolved = term if convolved is None else convolved + term
            kept = mask[first : first + middle, :]
            kept = jnp.concatenate([kept] * (half // mask.shape[1]), axis=1)
            masked = (residual[k].astype(F32) + convolved) * kept
            wide[k, first : first + middle, :] = masked
            skip[k, first : first + middle, :] = masked.astype(BF)
        term = dot(skip[k], down[k], 1, 0)
        total = term if total is None else total + term
    part[...] = total


def output_kernel(
    extent,
    loss_scale,
    meta,
    mask,
    own,
    got,
    wide,
    skip,
    glow,
    folded,
    pieces,
    back0,
    back1,
    back2,
    back3,
    grads,
    low,
    up,
    outputs,
    raw,
    returning,
):
    side = extent // 2
    quarter = side * side
    half = wide.shape[2]
    rows = grads.shape[2]
    images = wide.shape[1] // quarter
    gather_up(pieces, up)
    low[...] = swapped_sum(own, got)
    kept = jnp.concatenate([mask[...]] * (half // mask.shape[1]), axis=1)
    for k in range(4):
        outputs[k] = (wide[k] + dot(low[...], up[k], 1, 0)) * kept
    returning[...] = jnp.zeros_like(returning)

    def one(g, carry):
        slot = meta[16 + g]
        for k in range(4):
            for i in range(side):
                first = pl.multiple_of(g * quarter + i * side, side)
                put_every_second(raw, 2 * i + k // 2, k % 2, outputs[k, pl.ds(first, side), :])
        for row in range(extent):
            returning[slot, row * extent : (row + 1) * extent, :] = get_line(raw, row).astype(BF)
        return carry

    lax.fori_loop(0, images, one, 0)
    slots = back0.shape[0]
    for r, back in enumerate((back0, back1, back2, back3)):
        back[...] = returning[r * slots : (r + 1) * slots]
    turned = low[...].astype(F32).T.astype(BF)
    for k in range(4):
        scaled = (folded[k].astype(F32) * loss_scale).astype(BF)
        grad = dot(turned, scaled, 1, 0).astype(BF)
        for f in range(32):
            z, y, x = f // 8, f // 4 % 2, f % 4
            grads[z * 4 + x, y * 4 + k] = grad[f * rows : (f + 1) * rows, :]
        grad = dot(glow[...], skip[k], 1, 0).T.astype(BF)
        for x in range(4):
            for unit in range(8):
                side_of, step = unit // 4, unit % 4
                first = (x * 4 + step) * rows
                grads[k * 4 + x, 8 + unit] = grad[
                    first : first + rows, side_of * half : (side_of + 1) * half
                ]


def replicas(number, half):
    for r in range(4):
        chip, core = number // 2, number % 2
        chip = 1 - chip if r // 2 else chip
        core = 1 - core if r % 2 else core
        yield r, chip, pl.ds(pl.multiple_of(core * half, half), half)


def split_kernel(number, cot, out0, out1, out2, out3):
    outs = (out0, out1, out2, out3)
    slots, _, half = out0.shape
    for r, chip, lanes in replicas(number[0], half):
        outs[r][...] = cot[pl.ds(chip * slots, slots), :, lanes]


def join_kernel(number, back0, back1, back2, back3, out, wide, sem):
    backs = (back0, back1, back2, back3)
    slots, _, half = back0.shape
    copies = []
    for r, chip, lanes in replicas(number[0], half):
        wide[r] = backs[r][...].astype(F32)
        target = out.at[pl.ds(chip * slots, slots), :, lanes]
        copies.append(pltpu.make_async_copy(wide.at[r], target, sem.at[r]))
        copies[-1].start()
    for copy in copies:
        copy.wait()


def per_device(
    images, routes, bucket, heights, widths, w_conv, w_down, w_up, norm_gain, norm_shift, cotangent
):
    count, extent, _, channels = images.shape
    half = channels // 2
    pixels = extent * extent
    quarter = pixels // 4
    most = cotangent.shape[0] // 4
    rows = w_conv.shape[0]
    low_rows = 2 * count * quarter
    loss_scale = 1.0 / math.sqrt(count * 128 * pixels)
    dp, fsdp = lax.axis_index("dp"), lax.axis_index("fsdp")
    core, y = dp % 2, fsdp // 4 % 2

    conv_own = lax.dynamic_slice_in_dim(w_conv, core * half, half, axis=2).transpose(1, 0, 2)
    up_own = lax.dynamic_slice_in_dim(
        w_up.reshape(rows, 4, channels), core * half, half, axis=2
    ).transpose(1, 0, 2)
    down_own = w_down.reshape(4 * rows, 2, half).transpose(1, 0, 2).reshape(8, rows, half)
    packed = jnp.concatenate([up_own, down_own, conv_own])
    other = send(packed, "y")

    block = jax.ShapeDtypeStruct((2 * most, pixels, half), BF)
    number = dp.astype(I32).reshape(1)
    outgoing = kernel_call(
        split_kernel,
        (block,) * 4,
        flops=0,
        moved_bytes=4 * cotangent.size,
        in_specs=[SCALARS, WHOLE],
        out_specs=(WHOLE,) * 4,
    )(number, cotangent.reshape(4 * most, pixels, channels))
    outgoing, other = lax.optimization_barrier((outgoing, other))
    arrived = over_dp(outgoing)
    first = jnp.where(y == 0, packed, other)
    second = jnp.where(y == 0, other, packed)
    down_kept = jnp.where(core == 0, first[4:12], second[4:12])
    up_down = jnp.concatenate([first[:4], second[:4], down_kept])
    conv_two = jnp.concatenate([first[12:], second[12:]])
    up_down = over_plane(jnp.broadcast_to(up_down, (16, *up_down.shape)))
    conv_two = lax.all_gather(conv_two, "fsdp", axis_index_groups=PLANES)

    images_pair = send(images, "c")
    ids = jnp.concatenate([routes, bucket[:, None]], axis=1)
    ids_pair = send(ids, "c")

    def described(table, side):
        target = table[:, 0]
        position = jnp.arange(count, dtype=I32)
        earlier = position[None, :] < position[:, None]
        same_owner = target[:, None] == target[None, :]
        order_in = jnp.sum((same_owner & earlier).astype(I32), axis=1)
        slot = (target ^ dp) * 2 * most + side * most + order_in
        chosen = table[:, 1][:, None] == jnp.arange(heights.shape[0], dtype=I32)[None, :]
        height = jnp.sum(jnp.where(chosen, heights[None, :], 0), axis=1)
        width = jnp.sum(jnp.where(chosen, widths[None, :], 0), axis=1)
        return jnp.stack([height, width, slot])

    def numbers(first, second):
        parts = jnp.concatenate([first, second], axis=1).reshape(-1)
        return jnp.concatenate([parts, jnp.broadcast_to(core, (8,)).astype(I32)])

    own_facts, pair_facts = described(ids, core), described(ids_pair, 1 - core)
    own_meta = numbers(own_facts, own_facts)
    pair_meta = numbers(pair_facts, pair_facts)
    meta = numbers(own_facts, pair_facts)
    height, width = meta[:8], meta[8:16]
    place = jnp.arange(extent // 2, dtype=I32) * 2
    mask = (place[None, :, None] < height[:, None, None]) & (
        place[None, None, :] < width[:, None, None]
    )
    mask_lanes = jnp.broadcast_to(mask.astype(F32).reshape(1, low_rows), (8, low_rows))
    mask = jnp.broadcast_to(mask.astype(F32).reshape(low_rows, 1), (low_rows, min(128, half)))

    windows_own, residual_own = normed_windows(own_meta, images, norm_gain, norm_shift)
    windows_pair, residual_pair = normed_windows(pair_meta, images_pair, norm_gain, norm_shift)

    ready, mask, mask_lanes, windows_own, windows_pair = lax.optimization_barrier(
        (meta, mask, mask_lanes, windows_own, windows_pair)
    )
    folded, turned = kernel_call(
        functools.partial(fold_kernel, extent),
        (
            jax.ShapeDtypeStruct((4, low_rows, half), BF),
            jax.ShapeDtypeStruct((4, half, low_rows), BF),
        ),
        flops=0,
        moved_bytes=3 << 20,
        scratch=(
            laned(extent, extent, half),
            pltpu.VMEM((8 * most, pixels, half), BF),
            pltpu.SemaphoreType.DMA((4,)),
        ),
        in_specs=[SCALARS] + [pl.BlockSpec(memory_space=pl.ANY)] * 4,
        out_specs=(WHOLE, WHOLE),
    )(ready, *arrived)
    glow_part = kernel_call(
        functools.partial(glow_kernel, loss_scale),
        jax.ShapeDtypeStruct((channels, low_rows), F32),
        flops=8 * low_rows * channels * half,
        moved_bytes=3 << 20,
        scratch=(
            pltpu.VMEM((4, channels, half), BF),
            pltpu.VMEM((16, 8, rows, half), BF),
            pltpu.SemaphoreType.DMA,
        ),
        in_specs=[WHOLE, pl.BlockSpec(memory_space=pl.ANY)],
        out_specs=WHOLE,
    )(turned, up_down)
    glow_got = send(glow_part, "c")

    glow, conv_grads = kernel_call(
        functools.partial(grad_conv_kernel, loss_scale),
        (
            jax.ShapeDtypeStruct((channels, low_rows), BF),
            jax.ShapeDtypeStruct((16, 18, rows, half), BF),
        ),
        flops=80 * low_rows * channels * half,
        moved_bytes=15 << 20,
        scratch=(
            pltpu.VMEM((4, half, channels), BF),
            pltpu.VMEM((half, 4 * low_rows), BF),
            pltpu.VMEM((2, 4 * low_rows, channels), BF),
            pltpu.SemaphoreType.DMA((2, 8)),
        ),
        in_specs=[WHOLE] * 5 + [pl.BlockSpec(memory_space=pl.ANY)] * 2,
        out_specs=(WHOLE, WHOLE),
    )(mask_lanes, glow_part, glow_got, turned, up_down, windows_own, windows_pair)
    conv_grads = over_plane(conv_grads)
    glow, windows_own, windows_pair = lax.optimization_barrier((glow, windows_own, windows_pair))

    wide, skip, low_part = kernel_call(
        conv_kernel,
        (
            jax.ShapeDtypeStruct((4, low_rows, half), F32),
            jax.ShapeDtypeStruct((4, low_rows, half), BF),
            jax.ShapeDtypeStruct((low_rows, channels), F32),
        ),
        flops=80 * low_rows * channels * half,
        moved_bytes=18 << 20,
        scratch=(pltpu.VMEM((9, channels, half), BF), pltpu.VMEM((4, half, channels), BF)),
        in_specs=[WHOLE] * 7,
        out_specs=(WHOLE,) * 3,
    )(mask, conv_two, up_down, windows_own, windows_pair, residual_own, residual_pair)
    low_got = send(low_part, "c")

    *returning, grads = kernel_call(
        functools.partial(output_kernel, extent, loss_scale),
        (
            *(block,) * 4,
            jax.ShapeDtypeStruct((16, 16, rows, half), BF),
        ),
        flops=24 * low_rows * channels * half,
        moved_bytes=14 << 20,
        scratch=(
            pltpu.VMEM((low_rows, channels), BF),
            pltpu.VMEM((4, channels, half), BF),
            pltpu.VMEM((4, low_rows, half), F32),
            laned(extent, extent, half),
            pltpu.VMEM((8 * most, pixels, half), BF),
        ),
        in_specs=[SCALARS] + [WHOLE] * 8,
        out_specs=(WHOLE,) * 5,
    )(meta, mask, low_part, low_got, wide, skip, glow, folded, up_down)
    returned = over_dp(returning)
    grads = over_plane(grads)

    conv_sum = jnp.sum(conv_grads.astype(F32), axis=0).reshape(2, 9, rows, half)
    grads_sum = jnp.sum(grads.astype(F32), axis=0)
    up_sum, down_sum = grads_sum[:8].reshape(2, 4, rows, half), grads_sum[8:]
    down_sum = jnp.broadcast_to(down_sum, (2, *down_sum.shape))
    shares = jnp.concatenate([conv_sum, up_sum, down_sum], axis=1)
    shares, returned = lax.optimization_barrier((shares, returned))
    own, pair = over_column(shares, y)

    def by_core(first, last):
        parts = (own[first:last], pair[first:last])
        both = jnp.where(core == 0, jnp.stack(parts), jnp.stack(parts[::-1]))
        return both.transpose(2, 1, 0, 3)

    out_conv = by_core(0, 9).reshape(rows, 9, channels)
    out_up = by_core(9, 13).reshape(rows, 4 * channels)
    out_down = jnp.where(y == core, own[13:], pair[13:])
    out_down = out_down.reshape(2, 4 * rows, half).transpose(1, 0, 2).reshape(4 * rows, channels)

    block_out = kernel_call(
        join_kernel,
        jax.ShapeDtypeStruct((4 * most, pixels, channels), F32),
        flops=0,
        moved_bytes=6 * cotangent.size,
        scratch=(pltpu.VMEM((4, 2 * most, pixels, half), F32), pltpu.SemaphoreType.DMA((4,))),
        in_specs=[SCALARS] + [WHOLE] * 4,
        out_specs=pl.BlockSpec(memory_space=pl.ANY),
    )(number, *returned)
    return (block_out.reshape(cotangent.shape), out_conv, out_down, out_up)


def solution(mesh):
    return jax.shard_map(
        per_device,
        mesh=mesh,
        in_specs=(
            P(("dp", "fsdp"), None, None, None),
            P(("dp", "fsdp"), None),
            P(("dp", "fsdp")),
            P(),
            P(),
            P("fsdp", None, None),
            P("fsdp", None),
            P("fsdp", None),
            P(),
            P(),
            P(("dp", "fsdp"), None, None, None),
        ),
        out_specs=(
            P(("dp", "fsdp"), None, None, None),
            P("fsdp", None, None),
            P("fsdp", None),
            P("fsdp", None),
        ),
        check_vma=False,
    )
```

```python
import functools
import math

import jax
import jax.numpy as jnp
from jax import lax
from jax.experimental import pallas as pl
from jax.experimental.pallas import tpu as pltpu
from jax.sharding import PartitionSpec as P

GROUPS = 32
epsilon = 1e-05
BF = jnp.bfloat16
F32 = jnp.float32
I32 = jnp.int32
AXES = ("dp", "fsdp")
VMEM_BYTES = 56 * 1024 * 1024


def moved(fn):
    pairs = []
    for index in range(128):
        dp, fsdp = index // 32, index % 32
        place = (dp // 2, dp % 2, fsdp // 8, fsdp // 4 % 2, fsdp % 4)
        h, c, z, y, x = fn(*place)
        pairs.append((index, (h * 2 + c) * 32 + z * 8 + y * 4 + x))
    return pairs


STEP = {
    "y": moved(lambda h, c, z, y, x: (h, c, z, 1 - y, x)),
    "hy": moved(lambda h, c, z, y, x: (1 - h, c, z, 1 - y, x)),
    "c": moved(lambda h, c, z, y, x: (h, 1 - c, z, y, x)),
    "h": moved(lambda h, c, z, y, x: (1 - h, c, z, y, x)),
    "hc": moved(lambda h, c, z, y, x: (1 - h, 1 - c, z, y, x)),
}
BY_BITS = [(r >> 3 & 1) * 8 + (r >> 1 & 1) * 4 + (r >> 2 & 1) * 2 + (r & 1) for r in range(16)]
DIAGONAL = [r % 4 * 4 + (r // 4 + r) % 4 for r in range(16)]
PLANES = [[z * 8 + y * 4 + x for z in range(4) for x in range(4)] for y in range(2)]


def send(value, move):
    return lax.ppermute(value, AXES, STEP[move])


def over_dp(blocks):
    own, beside, across, both = blocks
    return (own, send(beside, "c"), send(across, "h"), send(both, "hc"))


def over_column(parts, y):
    kept = lax.dynamic_index_in_dim(parts, y, axis=0, keepdims=False)
    given = lax.dynamic_index_in_dim(parts, 1 - y, axis=0, keepdims=False)
    sent = given.astype(BF)
    got = (send(sent, "y"), send(kept.astype(BF), "h"), send(sent, "hy"))
    total = kept + got[0].astype(F32) + got[1].astype(F32) + got[2].astype(F32)
    return total, send(total, "c")


def over_plane(blocks, order=tuple(range(16))):
    groups = [[plane[place] for place in order] for plane in PLANES]
    return lax.all_to_all(
        blocks, "fsdp", split_axis=0, concat_axis=0, axis_index_groups=groups, tiled=True
    )


def dot(left, right, left_dim, right_dim):
    return lax.dot_general(
        left, right, (((left_dim,), (right_dim,)), ((), ())), preferred_element_type=F32
    )


def kernel_call(body, out_shape, flops, moved_bytes, scratch=(), **more):
    return pl.pallas_call(
        body,
        out_shape=out_shape,
        scratch_shapes=list(scratch),
        compiler_params=pltpu.CompilerParams(vmem_limit_bytes=VMEM_BYTES),
        cost_estimate=pl.CostEstimate(
            flops=int(flops), bytes_accessed=int(moved_bytes), transcendentals=0
        ),
        **more,
    )


def laned(extent_rows, extent_columns, lanes):
    block = min(128, lanes)
    return pltpu.VMEM((lanes // block, extent_rows, extent_columns, block), F32)


def put_line(ref, row, first, values):
    block = ref.shape[3]
    for b in range(ref.shape[0]):
        ref[b, row, first : first + values.shape[0], :] = values[:, b * block : (b + 1) * block]


def get_line(ref, row):
    return jnp.concatenate([ref[b, row] for b in range(ref.shape[0])], axis=1)


def every_second(ref, row, first, side):
    places = [
        ref[pl.ds(b, 1), pl.ds(row, 1), pl.ds(first, side, stride=2), :].reshape(side, ref.shape[3])
        for b in range(ref.shape[0])
    ]
    return jnp.concatenate(places, axis=1)


def put_every_second(ref, row, first, values):
    side, block = values.shape[0], ref.shape[3]
    for b in range(ref.shape[0]):
        ref[pl.ds(b, 1), pl.ds(row, 1), pl.ds(first, side, stride=2), :] = values[
            :, b * block : (b + 1) * block
        ].reshape(1, 1, side, block)


WHOLE = pl.BlockSpec(memory_space=pltpu.VMEM)
SCALARS = pl.BlockSpec(memory_space=pltpu.SMEM)


def over_group(sums, width):
    lane = lax.broadcasted_iota(I32, sums.shape, 1)
    step = width // 2
    while step:
        lower = (lane & step) == 0
        lanes = sums.shape[1]
        sums = sums + jnp.where(
            lower, pltpu.roll(sums, lanes - step, 1), pltpu.roll(sums, step, 1)
        )
        step //= 2
    return sums


def norm_kernel(extent, meta, image, gain, shift, windows, residual, padded, raw):
    place = pl.program_id(0)
    channels = image.shape[2]
    half = channels // 2
    height, width = meta[place], meta[8 + place]
    core = meta[24]

    @pl.when(place == 0)
    def _():
        padded[...] = jnp.zeros_like(padded)

    inside = lax.broadcasted_iota(I32, (extent, channels), 0) < width

    def line(row):
        return image[0, row * extent : (row + 1) * extent, :].astype(F32)

    def mask(row):
        return (inside & (row < height)).astype(F32)

    group = channels // GROUPS
    counted = jnp.maximum((height * width * group).astype(F32), 1.0)
    total = jnp.zeros((extent, channels), F32)
    for row in range(extent):
        total = total + line(row) * mask(row)
    total = jnp.broadcast_to(jnp.sum(total, axis=0, keepdims=True), (8, channels))
    mean = (over_group(total, group) / counted)[:1]
    total = jnp.zeros((extent, channels), F32)
    for row in range(extent):
        centred = (line(row) - mean) * mask(row)
        total = total + centred * centred
    total = jnp.broadcast_to(jnp.sum(total, axis=0, keepdims=True), (8, channels))
    variance = (over_group(total, group) / counted)[:1]
    scale = lax.rsqrt(variance + epsilon) * gain[...]
    for row in range(extent):
        normed = (line(row) - mean) * scale + shift[...]
        put_line(padded, row + 1, 8, normed / (1.0 + jnp.exp(-normed)) * mask(row))
        residue = image[
            0, row * extent : (row + 1) * extent, pl.ds(pl.multiple_of(core * half, half), half)
        ]
        put_line(raw, row, 0, residue.astype(F32))
    side = extent // 2
    for p in range(4):
        for q in range(4):
            for i in range(0, side, 2):
                pair = [every_second(padded, 2 * n + p, 7 + q, side) for n in (i, i + 1)]
                windows[p * 4 + q, i * side : (i + 2) * side, :] = jnp.concatenate(pair).astype(BF)
    for k in range(4):
        for i in range(0, side, 2):
            pair = [every_second(raw, 2 * n + k // 2, k % 2, side) for n in (i, i + 1)]
            residual[k, i * side : (i + 2) * side, :] = jnp.concatenate(pair).astype(BF)


def normed_windows(meta, images, gain, shift):
    count, extent, _, channels = images.shape
    pixels, half = extent * extent, channels // 2
    quarter = pixels // 4
    return kernel_call(
        functools.partial(norm_kernel, extent),
        (
            jax.ShapeDtypeStruct((16, count * quarter, channels), BF),
            jax.ShapeDtypeStruct((4, count * quarter, half), BF),
        ),
        flops=40 * images.size,
        moved_bytes=12 * images.size,
        scratch=(
            laned(extent + 2, extent + 16, channels),
            laned(extent, extent, half),
        ),
        grid=(count,),
        in_specs=[
            SCALARS,
            pl.BlockSpec((1, pixels, channels), lambda g: (g, 0, 0)),
            pl.BlockSpec((1, channels), lambda g: (0, 0)),
            pl.BlockSpec((1, channels), lambda g: (0, 0)),
        ],
        out_specs=(
            pl.BlockSpec((16, quarter, channels), lambda g: (0, g, 0)),
            pl.BlockSpec((4, quarter, half), lambda g: (0, g, 0)),
        ),
    )(meta, images.reshape(count, pixels, channels), gain[None, :], shift[None, :])


def gather_up(pieces, up):
    rows = pieces.shape[2]
    for f in range(32):
        z, y, x = f // 8, f // 4 % 2, f % 4
        for k in range(4):
            up[k, f * rows : (f + 1) * rows, :] = pieces[z * 4 + x, y * 4 + k]


def gather_down(pieces, down):
    rows, half = pieces.shape[2:]
    for z in range(4):
        for x in range(4):
            for unit in range(8):
                side, step = unit // 4, unit % 4
                first = (x * 4 + step) * rows
                down[z, first : first + rows, side * half : (side + 1) * half] = pieces[
                    z * 4 + x, 8 + unit
                ]


def swapped_sum(own, got):
    middle = own.shape[0] // 2
    return jnp.concatenate(
        [own[:middle] + got[middle:], own[middle:] + got[:middle]], axis=0
    ).astype(BF)


def fold_kernel(extent, meta, cot0, cot1, cot2, cot3, folded, raw, cot, sem):
    side = extent // 2
    quarter = side * side
    half = cot.shape[2]
    slots = cot0.shape[0]
    copies = [
        pltpu.make_async_copy(ref, cot.at[pl.ds(r * slots, slots)], sem.at[r])
        for r, ref in enumerate((cot0, cot1, cot2, cot3))
    ]
    for copy in copies:
        copy.start()
    for copy in copies:
        copy.wait()
    images = folded.shape[1] // quarter
    inside = lax.broadcasted_iota(I32, (extent, half), 0)

    def one(g, carry):
        height, width, slot = meta[g], meta[8 + g], meta[16 + g]
        for row in range(extent):
            kept = ((inside < width) & (row < height)).astype(F32)
            line = cot[slot, row * extent : (row + 1) * extent, :].astype(F32)
            put_line(raw, row, 0, line * kept)
        for k in range(4):
            for i in range(0, side, 2):
                pair = [every_second(raw, 2 * n + k // 2, k % 2, side) for n in (i, i + 1)]
                first = pl.multiple_of(g * quarter + i * side, 2 * side)
                folded[k, pl.ds(first, 2 * side), :] = jnp.concatenate(pair).astype(BF)
        return carry

    lax.fori_loop(0, images, one, 0)


def glow_kernel(loss_scale, folded, pieces, part, up, held, sem):
    copy = pltpu.make_async_copy(pieces.at[:, pl.ds(0, 8)], held, sem)
    copy.start()
    copy.wait()
    gather_up(held, up)
    total = None
    for k in range(4):
        scaled = (folded[k].astype(F32) * loss_scale).astype(BF)
        term = dot(scaled, up[k], 1, 1)
        total = term if total is None else total + term
    part[...] = total


def grad_conv_kernel(
    loss_scale, mask, own, got, folded, pieces, windows_own, windows_pair, glow, grads, down, turned
):
    half = folded.shape[2]
    rows = grads.shape[2]
    middle = folded.shape[1] // 2
    gather_down(pieces, down)
    glow[...] = swapped_sum(own, got)
    kept = jnp.concatenate([mask[...]] * (half // mask.shape[1]), axis=1)
    for k in range(4):
        grad = folded[k].astype(F32) * loss_scale + dot(glow[...], down[k], 1, 1)
        turned[k] = (grad * kept).T.astype(BF)
    for t in range(9):
        total = None
        for k in range(4):
            v = (k // 2 + t // 3) * 4 + k % 2 + t % 3
            for columns, windows in ((slice(0, middle), windows_own), (slice(middle, None), windows_pair)):
                term = dot(turned[k, :, columns], windows[v], 1, 0)
                total = term if total is None else total + term
        total = total.T.astype(BF)
        for f in range(32):
            z, y, x = f // 8, f // 4 % 2, f % 4
            grads[BY_BITS.index(z * 4 + x), y * 9 + t] = total[f * rows : (f + 1) * rows, :]


def conv_kernel(
    mask,
    conv_pieces,
    pieces,
    windows_own,
    windows_pair,
    residual_own,
    residual_pair,
    wide,
    skip,
    part,
    conv,
    down,
):
    half = wide.shape[2]
    rows = conv_pieces.shape[2]
    middle = wide.shape[1] // 2
    for f in range(32):
        z, y, x = f // 8, f // 4 % 2, f % 4
        for t in range(9):
            conv[t, f * rows : (f + 1) * rows, :] = conv_pieces[z * 4 + x, y * 9 + t]
    gather_down(pieces, down)
    total = None
    for k in range(4):
        for first, windows, residual in (
            (0, windows_own, residual_own),
            (middle, windows_pair, residual_pair),
        ):
            convolved = None
            for t in range(9):
                v = (k // 2 + t // 3) * 4 + k % 2 + t % 3
                term = dot(windows[v], conv[t], 1, 0)
                convolved = term if convolved is None else convolved + term
            kept = mask[first : first + middle, :]
            kept = jnp.concatenate([kept] * (half // mask.shape[1]), axis=1)
            masked = (residual[k].astype(F32) + convolved) * kept
            wide[k, first : first + middle, :] = masked
            skip[k, first : first + middle, :] = masked.astype(BF)
        term = dot(skip[k], down[k], 1, 0)
        total = term if total is None else total + term
    part[...] = total


def output_kernel(
    extent,
    loss_scale,
    meta,
    mask,
    own,
    got,
    wide,
    skip,
    glow,
    folded,
    pieces,
    back0,
    back1,
    back2,
    back3,
    grads,
    low,
    up,
    outputs,
    raw,
    returning,
):
    side = extent // 2
    quarter = side * side
    half = wide.shape[2]
    rows = grads.shape[2]
    images = wide.shape[1] // quarter
    gather_up(pieces, up)
    low[...] = swapped_sum(own, got)
    kept = jnp.concatenate([mask[...]] * (half // mask.shape[1]), axis=1)
    for k in range(4):
        outputs[k] = (wide[k] + dot(low[...], up[k], 1, 0)) * kept
    returning[...] = jnp.zeros_like(returning)

    def one(g, carry):
        slot = meta[16 + g]
        for k in range(4):
            for i in range(side):
                first = pl.multiple_of(g * quarter + i * side, side)
                put_every_second(raw, 2 * i + k // 2, k % 2, outputs[k, pl.ds(first, side), :])
        for row in range(extent):
            returning[slot, row * extent : (row + 1) * extent, :] = get_line(raw, row).astype(BF)
        return carry

    lax.fori_loop(0, images, one, 0)
    slots = back0.shape[0]
    for r, back in enumerate((back0, back1, back2, back3)):
        back[...] = returning[r * slots : (r + 1) * slots]
    turned = low[...].astype(F32).T.astype(BF)
    for k in range(4):
        scaled = (folded[k].astype(F32) * loss_scale).astype(BF)
        grad = dot(turned, scaled, 1, 0).astype(BF)
        for f in range(32):
            z, y, x = f // 8, f // 4 % 2, f % 4
            grads[DIAGONAL.index(z * 4 + x), y * 4 + k] = grad[f * rows : (f + 1) * rows, :]
        grad = dot(skip[k].astype(F32).T.astype(BF), glow[...], 1, 0).astype(BF)
        for x in range(4):
            for unit in range(8):
                side_of, step = unit // 4, unit % 4
                first = (x * 4 + step) * rows
                grads[DIAGONAL.index(k * 4 + x), 8 + unit] = grad[
                    first : first + rows, side_of * half : (side_of + 1) * half
                ]


def replicas(number, half):
    for r in range(4):
        chip, core = number // 2, number % 2
        chip = 1 - chip if r // 2 else chip
        core = 1 - core if r % 2 else core
        yield r, chip, pl.ds(pl.multiple_of(core * half, half), half)


def split_kernel(number, cot, out0, out1, out2, out3):
    outs = (out0, out1, out2, out3)
    slots, _, half = out0.shape
    for r, chip, lanes in replicas(number[0], half):
        outs[r][...] = cot[pl.ds(chip * slots, slots), :, lanes]


def join_kernel(number, back0, back1, back2, back3, out, wide, sem):
    backs = (back0, back1, back2, back3)
    slots, _, half = back0.shape
    copies = []
    for r, chip, lanes in replicas(number[0], half):
        wide[r] = backs[r][...].astype(F32)
        target = out.at[pl.ds(chip * slots, slots), :, lanes]
        copies.append(pltpu.make_async_copy(wide.at[r], target, sem.at[r]))
        copies[-1].start()
    for copy in copies:
        copy.wait()


def per_device(
    images, routes, bucket, heights, widths, w_conv, w_down, w_up, norm_gain, norm_shift, cotangent
):
    count, extent, _, channels = images.shape
    half = channels // 2
    pixels = extent * extent
    quarter = pixels // 4
    most = cotangent.shape[0] // 4
    rows = w_conv.shape[0]
    low_rows = 2 * count * quarter
    loss_scale = 1.0 / math.sqrt(count * 128 * pixels)
    dp, fsdp = lax.axis_index("dp"), lax.axis_index("fsdp")
    core, y = dp % 2, fsdp // 4 % 2

    conv_own = lax.dynamic_slice_in_dim(w_conv, core * half, half, axis=2).transpose(1, 0, 2)
    up_own = lax.dynamic_slice_in_dim(
        w_up.reshape(rows, 4, channels), core * half, half, axis=2
    ).transpose(1, 0, 2)
    down_own = w_down.reshape(4 * rows, 2, half).transpose(1, 0, 2).reshape(8, rows, half)
    packed = jnp.concatenate([up_own, down_own, conv_own])
    other = send(packed, "y")

    block = jax.ShapeDtypeStruct((2 * most, pixels, half), BF)
    number = dp.astype(I32).reshape(1)
    outgoing = kernel_call(
        split_kernel,
        (block,) * 4,
        flops=0,
        moved_bytes=4 * cotangent.size,
        in_specs=[SCALARS, WHOLE],
        out_specs=(WHOLE,) * 4,
    )(number, cotangent.reshape(4 * most, pixels, channels))
    outgoing, other = lax.optimization_barrier((outgoing, other))
    arrived = over_dp(outgoing)
    first = jnp.where(y == 0, packed, other)
    second = jnp.where(y == 0, other, packed)
    down_kept = jnp.where(core == 0, first[4:12], second[4:12])
    up_down = jnp.concatenate([first[:4], second[:4], down_kept])
    conv_two = jnp.concatenate([first[12:], second[12:]])
    up_down = over_plane(jnp.broadcast_to(up_down, (16, *up_down.shape)))
    conv_two = lax.all_gather(conv_two, "fsdp", axis_index_groups=PLANES)

    images_pair = send(images, "c")
    ids = jnp.concatenate([routes, bucket[:, None]], axis=1)
    ids_pair = send(ids, "c")

    def described(table, side):
        target = table[:, 0]
        position = jnp.arange(count, dtype=I32)
        earlier = position[None, :] < position[:, None]
        same_owner = target[:, None] == target[None, :]
        order_in = jnp.sum((same_owner & earlier).astype(I32), axis=1)
        slot = (target ^ dp) * 2 * most + side * most + order_in
        chosen = table[:, 1][:, None] == jnp.arange(heights.shape[0], dtype=I32)[None, :]
        height = jnp.sum(jnp.where(chosen, heights[None, :], 0), axis=1)
        width = jnp.sum(jnp.where(chosen, widths[None, :], 0), axis=1)
        return jnp.stack([height, width, slot])

    def numbers(first, second):
        parts = jnp.concatenate([first, second], axis=1).reshape(-1)
        return jnp.concatenate([parts, jnp.broadcast_to(core, (8,)).astype(I32)])

    own_facts, pair_facts = described(ids, core), described(ids_pair, 1 - core)
    own_meta = numbers(own_facts, own_facts)
    pair_meta = numbers(pair_facts, pair_facts)
    meta = numbers(own_facts, pair_facts)
    height, width = meta[:8], meta[8:16]
    place = jnp.arange(extent // 2, dtype=I32) * 2
    mask = (place[None, :, None] < height[:, None, None]) & (
        place[None, None, :] < width[:, None, None]
    )
    mask = jnp.broadcast_to(mask.astype(F32).reshape(low_rows, 1), (low_rows, min(128, half)))

    windows_own, residual_own = normed_windows(own_meta, images, norm_gain, norm_shift)
    windows_pair, residual_pair = normed_windows(pair_meta, images_pair, norm_gain, norm_shift)

    ready, mask, windows_own, windows_pair = lax.optimization_barrier(
        (meta, mask, windows_own, windows_pair)
    )
    folded = kernel_call(
        functools.partial(fold_kernel, extent),
        jax.ShapeDtypeStruct((4, low_rows, half), BF),
        flops=0,
        moved_bytes=3 << 20,
        scratch=(
            laned(extent, extent, half),
            pltpu.VMEM((8 * most, pixels, half), BF),
            pltpu.SemaphoreType.DMA((4,)),
        ),
        in_specs=[SCALARS] + [pl.BlockSpec(memory_space=pl.ANY)] * 4,
        out_specs=WHOLE,
    )(ready, *arrived)
    glow_part = kernel_call(
        functools.partial(glow_kernel, loss_scale),
        jax.ShapeDtypeStruct((low_rows, channels), F32),
        flops=8 * low_rows * channels * half,
        moved_bytes=3 << 20,
        scratch=(
            pltpu.VMEM((4, channels, half), BF),
            pltpu.VMEM((16, 8, rows, half), BF),
            pltpu.SemaphoreType.DMA,
        ),
        in_specs=[WHOLE, pl.BlockSpec(memory_space=pl.ANY)],
        out_specs=WHOLE,
    )(folded, up_down)
    glow_got = send(glow_part, "c")

    glow, conv_grads = kernel_call(
        functools.partial(grad_conv_kernel, loss_scale),
        (
            jax.ShapeDtypeStruct((low_rows, channels), BF),
            jax.ShapeDtypeStruct((16, 18, rows, half), BF),
        ),
        flops=80 * low_rows * channels * half,
        moved_bytes=15 << 20,
        scratch=(pltpu.VMEM((4, half, channels), BF), pltpu.VMEM((4, half, low_rows), BF)),
        in_specs=[WHOLE] * 7,
        out_specs=(WHOLE, WHOLE),
    )(mask, glow_part, glow_got, folded, up_down, windows_own, windows_pair)
    conv_grads = over_plane(conv_grads, BY_BITS)
    glow, windows_own, windows_pair = lax.optimization_barrier((glow, windows_own, windows_pair))

    wide, skip, low_part = kernel_call(
        conv_kernel,
        (
            jax.ShapeDtypeStruct((4, low_rows, half), F32),
            jax.ShapeDtypeStruct((4, low_rows, half), BF),
            jax.ShapeDtypeStruct((low_rows, channels), F32),
        ),
        flops=80 * low_rows * channels * half,
        moved_bytes=18 << 20,
        scratch=(pltpu.VMEM((9, channels, half), BF), pltpu.VMEM((4, half, channels), BF)),
        in_specs=[WHOLE] * 7,
        out_specs=(WHOLE,) * 3,
    )(mask, conv_two, up_down, windows_own, windows_pair, residual_own, residual_pair)
    low_got = send(low_part, "c")

    *returning, grads = kernel_call(
        functools.partial(output_kernel, extent, loss_scale),
        (
            *(block,) * 4,
            jax.ShapeDtypeStruct((16, 16, rows, half), BF),
        ),
        flops=24 * low_rows * channels * half,
        moved_bytes=14 << 20,
        scratch=(
            pltpu.VMEM((low_rows, channels), BF),
            pltpu.VMEM((4, channels, half), BF),
            pltpu.VMEM((4, low_rows, half), F32),
            laned(extent, extent, half),
            pltpu.VMEM((8 * most, pixels, half), BF),
        ),
        in_specs=[SCALARS] + [WHOLE] * 8,
        out_specs=(WHOLE,) * 5,
    )(meta, mask, low_part, low_got, wide, skip, glow, folded, up_down)
    returned = over_dp(returning)
    grads = over_plane(grads, DIAGONAL)

    conv_sum = jnp.sum(conv_grads.astype(F32), axis=0).reshape(2, 9, rows, half)
    grads_sum = jnp.sum(grads.astype(F32), axis=0)
    up_sum, down_sum = grads_sum[:8].reshape(2, 4, rows, half), grads_sum[8:]
    down_sum = jnp.broadcast_to(down_sum, (2, *down_sum.shape))
    shares = jnp.concatenate([conv_sum, up_sum, down_sum], axis=1)
    shares, returned = lax.optimization_barrier((shares, returned))
    own, pair = over_column(shares, y)

    def by_core(first, last):
        parts = (own[first:last], pair[first:last])
        both = jnp.where(core == 0, jnp.stack(parts), jnp.stack(parts[::-1]))
        return both.transpose(2, 1, 0, 3)

    out_conv = by_core(0, 9).reshape(rows, 9, channels)
    out_up = by_core(9, 13).reshape(rows, 4 * channels)
    out_down = jnp.where(y == core, own[13:], pair[13:])
    out_down = out_down.reshape(2, 4 * rows, half).transpose(1, 0, 2).reshape(4 * rows, channels)

    block_out = kernel_call(
        join_kernel,
        jax.ShapeDtypeStruct((4 * most, pixels, channels), F32),
        flops=0,
        moved_bytes=6 * cotangent.size,
        scratch=(pltpu.VMEM((4, 2 * most, pixels, half), F32), pltpu.SemaphoreType.DMA((4,))),
        in_specs=[SCALARS] + [WHOLE] * 4,
        out_specs=pl.BlockSpec(memory_space=pl.ANY),
    )(number, *returned)
    return (block_out.reshape(cotangent.shape), out_conv, out_down, out_up)


def solution(mesh):
    return jax.shard_map(
        per_device,
        mesh=mesh,
        in_specs=(
            P(("dp", "fsdp"), None, None, None),
            P(("dp", "fsdp"), None),
            P(("dp", "fsdp")),
            P(),
            P(),
            P("fsdp", None, None),
            P("fsdp", None),
            P("fsdp", None),
            P(),
            P(),
            P(("dp", "fsdp"), None, None, None),
        ),
        out_specs=(
            P(("dp", "fsdp"), None, None, None),
            P("fsdp", None, None),
            P("fsdp", None),
            P("fsdp", None),
        ),
        check_vma=False,
    )
```

```python
import functools
import math

import jax
import jax.numpy as jnp
from jax import lax
from jax.experimental import pallas as pl
from jax.experimental.pallas import tpu as pltpu
from jax.sharding import PartitionSpec as P

GROUPS = 32
epsilon = 1e-05
BF = jnp.bfloat16
F32 = jnp.float32
I32 = jnp.int32
AXES = ("dp", "fsdp")
VMEM_BYTES = 56 * 1024 * 1024


def moved(fn):
    pairs = []
    for index in range(128):
        dp, fsdp = index // 32, index % 32
        place = (dp // 2, dp % 2, fsdp // 8, fsdp // 4 % 2, fsdp % 4)
        h, c, z, y, x = fn(*place)
        pairs.append((index, (h * 2 + c) * 32 + z * 8 + y * 4 + x))
    return pairs


STEP = {
    "y": moved(lambda h, c, z, y, x: (h, c, z, 1 - y, x)),
    "hy": moved(lambda h, c, z, y, x: (1 - h, c, z, 1 - y, x)),
    "c": moved(lambda h, c, z, y, x: (h, 1 - c, z, y, x)),
    "h": moved(lambda h, c, z, y, x: (1 - h, c, z, y, x)),
    "hc": moved(lambda h, c, z, y, x: (1 - h, 1 - c, z, y, x)),
}
BY_BITS = [(r >> 3 & 1) * 8 + (r >> 1 & 1) * 4 + (r >> 2 & 1) * 2 + (r & 1) for r in range(16)]
DIAGONAL = [r % 4 * 4 + (r // 4 + r) % 4 for r in range(16)]
PLANES = [[z * 8 + y * 4 + x for z in range(4) for x in range(4)] for y in range(2)]


def send(value, move):
    return lax.ppermute(value, AXES, STEP[move])


def over_dp(blocks):
    own, beside, across, both = blocks
    return (own, send(beside, "c"), send(across, "h"), send(both, "hc"))


def over_column(parts, y):
    kept = lax.dynamic_index_in_dim(parts, y, axis=0, keepdims=False)
    given = lax.dynamic_index_in_dim(parts, 1 - y, axis=0, keepdims=False)
    sent = given.astype(BF)
    got = (send(sent, "y"), send(kept.astype(BF), "h"), send(sent, "hy"))
    total = kept + got[0].astype(F32) + got[1].astype(F32) + got[2].astype(F32)
    return total, send(total, "c")


def over_plane(blocks, order=tuple(range(16))):
    groups = [[plane[place] for place in order] for plane in PLANES]
    return lax.all_to_all(
        blocks, "fsdp", split_axis=0, concat_axis=0, axis_index_groups=groups, tiled=True
    )


def dot(left, right, left_dim, right_dim):
    return lax.dot_general(
        left, right, (((left_dim,), (right_dim,)), ((), ())), preferred_element_type=F32
    )


def kernel_call(body, out_shape, flops, moved_bytes, scratch=(), **more):
    return pl.pallas_call(
        body,
        out_shape=out_shape,
        scratch_shapes=list(scratch),
        compiler_params=pltpu.CompilerParams(vmem_limit_bytes=VMEM_BYTES),
        cost_estimate=pl.CostEstimate(
            flops=int(flops), bytes_accessed=int(moved_bytes), transcendentals=0
        ),
        **more,
    )


def laned(extent_rows, extent_columns, lanes):
    block = min(128, lanes)
    return pltpu.VMEM((lanes // block, extent_rows, extent_columns, block), F32)


def put_line(ref, row, first, values):
    block = ref.shape[3]
    for b in range(ref.shape[0]):
        ref[b, row, first : first + values.shape[0], :] = values[:, b * block : (b + 1) * block]


def get_line(ref, row):
    return jnp.concatenate([ref[b, row] for b in range(ref.shape[0])], axis=1)


def every_second(ref, row, first, side):
    places = [
        ref[pl.ds(b, 1), pl.ds(row, 1), pl.ds(first, side, stride=2), :].reshape(side, ref.shape[3])
        for b in range(ref.shape[0])
    ]
    return jnp.concatenate(places, axis=1)


def put_every_second(ref, row, first, values):
    side, block = values.shape[0], ref.shape[3]
    for b in range(ref.shape[0]):
        ref[pl.ds(b, 1), pl.ds(row, 1), pl.ds(first, side, stride=2), :] = values[
            :, b * block : (b + 1) * block
        ].reshape(1, 1, side, block)


WHOLE = pl.BlockSpec(memory_space=pltpu.VMEM)
SCALARS = pl.BlockSpec(memory_space=pltpu.SMEM)


def over_group(sums, width):
    lane = lax.broadcasted_iota(I32, sums.shape, 1)
    step = width // 2
    while step:
        lower = (lane & step) == 0
        lanes = sums.shape[1]
        sums = sums + jnp.where(
            lower, pltpu.roll(sums, lanes - step, 1), pltpu.roll(sums, step, 1)
        )
        step //= 2
    return sums


def norm_kernel(extent, meta, image, gain, shift, windows, residual, padded, raw):
    place = pl.program_id(0)
    channels = image.shape[2]
    half = channels // 2
    height, width = meta[place], meta[8 + place]
    core = meta[24]

    @pl.when(place == 0)
    def _():
        padded[...] = jnp.zeros_like(padded)

    inside = lax.broadcasted_iota(I32, (extent, channels), 0) < width

    def line(row):
        return image[0, row * extent : (row + 1) * extent, :].astype(F32)

    def mask(row):
        return (inside & (row < height)).astype(F32)

    group = channels // GROUPS
    counted = jnp.maximum((height * width * group).astype(F32), 1.0)
    total = jnp.zeros((extent, channels), F32)
    for row in range(extent):
        total = total + line(row) * mask(row)
    total = jnp.broadcast_to(jnp.sum(total, axis=0, keepdims=True), (8, channels))
    mean = (over_group(total, group) / counted)[:1]
    total = jnp.zeros((extent, channels), F32)
    for row in range(extent):
        centred = (line(row) - mean) * mask(row)
        total = total + centred * centred
    total = jnp.broadcast_to(jnp.sum(total, axis=0, keepdims=True), (8, channels))
    variance = (over_group(total, group) / counted)[:1]
    scale = lax.rsqrt(variance + epsilon) * gain[...]
    for row in range(extent):
        normed = (line(row) - mean) * scale + shift[...]
        put_line(padded, row + 1, 8, normed / (1.0 + jnp.exp(-normed)) * mask(row))
        residue = image[
            0, row * extent : (row + 1) * extent, pl.ds(pl.multiple_of(core * half, half), half)
        ]
        put_line(raw, row, 0, residue.astype(F32))
    side = extent // 2
    for p in range(4):
        for q in range(4):
            for i in range(0, side, 2):
                pair = [every_second(padded, 2 * n + p, 7 + q, side) for n in (i, i + 1)]
                windows[p * 4 + q, i * side : (i + 2) * side, :] = jnp.concatenate(pair).astype(BF)
    for k in range(4):
        for i in range(0, side, 2):
            pair = [every_second(raw, 2 * n + k // 2, k % 2, side) for n in (i, i + 1)]
            residual[k, i * side : (i + 2) * side, :] = jnp.concatenate(pair).astype(BF)


def normed_windows(meta, images, gain, shift):
    count, extent, _, channels = images.shape
    pixels, half = extent * extent, channels // 2
    quarter = pixels // 4
    return kernel_call(
        functools.partial(norm_kernel, extent),
        (
            jax.ShapeDtypeStruct((16, count * quarter, channels), BF),
            jax.ShapeDtypeStruct((4, count * quarter, half), BF),
        ),
        flops=40 * images.size,
        moved_bytes=12 * images.size,
        scratch=(
            laned(extent + 2, extent + 16, channels),
            laned(extent, extent, half),
        ),
        grid=(count,),
        in_specs=[
            SCALARS,
            pl.BlockSpec((1, pixels, channels), lambda g: (g, 0, 0)),
            pl.BlockSpec((1, channels), lambda g: (0, 0)),
            pl.BlockSpec((1, channels), lambda g: (0, 0)),
        ],
        out_specs=(
            pl.BlockSpec((16, quarter, channels), lambda g: (0, g, 0)),
            pl.BlockSpec((4, quarter, half), lambda g: (0, g, 0)),
        ),
    )(meta, images.reshape(count, pixels, channels), gain[None, :], shift[None, :])


def gather_up(pieces, up):
    rows = pieces.shape[2]
    for f in range(32):
        z, y, x = f // 8, f // 4 % 2, f % 4
        for k in range(4):
            up[k, f * rows : (f + 1) * rows, :] = pieces[BY_BITS.index(z * 4 + x), y * 4 + k]


def gather_down(pieces, down):
    rows, half = pieces.shape[2:]
    for z in range(4):
        for x in range(4):
            for unit in range(8):
                side, step = unit // 4, unit % 4
                first = (x * 4 + step) * rows
                down[z, first : first + rows, side * half : (side + 1) * half] = pieces[
                    BY_BITS.index(z * 4 + x), 8 + unit
                ]


def swapped_sum(own, got):
    middle = own.shape[0] // 2
    return jnp.concatenate(
        [own[:middle] + got[middle:], own[middle:] + got[:middle]], axis=0
    ).astype(BF)


def glow_kernel(
    extent, loss_scale, meta, cot0, cot1, cot2, cot3, pieces, folded, part, raw, up, cot, sem
):
    side = extent // 2
    quarter = side * side
    half = cot.shape[2]
    slots = cot0.shape[0]
    copies = [
        pltpu.make_async_copy(ref, cot.at[pl.ds(r * slots, slots)], sem.at[r])
        for r, ref in enumerate((cot0, cot1, cot2, cot3))
    ]
    for copy in copies:
        copy.start()
    gather_up(pieces, up)
    for copy in copies:
        copy.wait()
    images = folded.shape[1] // quarter
    inside = lax.broadcasted_iota(I32, (extent, half), 0)

    def one(g, carry):
        height, width, slot = meta[g], meta[8 + g], meta[16 + g]
        for row in range(extent):
            kept = ((inside < width) & (row < height)).astype(F32)
            line = cot[slot, row * extent : (row + 1) * extent, :].astype(F32)
            put_line(raw, row, 0, line * kept)
        for k in range(4):
            for i in range(0, side, 2):
                pair = [every_second(raw, 2 * n + k // 2, k % 2, side) for n in (i, i + 1)]
                first = pl.multiple_of(g * quarter + i * side, 2 * side)
                folded[k, pl.ds(first, 2 * side), :] = jnp.concatenate(pair).astype(BF)
        return carry

    lax.fori_loop(0, images, one, 0)
    total = None
    for k in range(4):
        scaled = (folded[k].astype(F32) * loss_scale).astype(BF)
        term = dot(scaled, up[k], 1, 1)
        total = term if total is None else total + term
    part[...] = total


def grad_conv_kernel(
    loss_scale, mask, own, got, folded, pieces, windows_own, windows_pair, glow, grads, down, turned
):
    half = folded.shape[2]
    rows = grads.shape[2]
    middle = folded.shape[1] // 2
    gather_down(pieces, down)
    glow[...] = swapped_sum(own, got)
    kept = jnp.concatenate([mask[...]] * (half // mask.shape[1]), axis=1)
    for k in range(4):
        grad = folded[k].astype(F32) * loss_scale + dot(glow[...], down[k], 1, 1)
        turned[k] = (grad * kept).T.astype(BF)
    for t in range(9):
        total = None
        for k in range(4):
            v = (k // 2 + t // 3) * 4 + k % 2 + t % 3
            for columns, windows in ((slice(0, middle), windows_own), (slice(middle, None), windows_pair)):
                term = dot(turned[k, :, columns], windows[v], 1, 0)
                total = term if total is None else total + term
        total = total.T.astype(BF)
        for f in range(32):
            z, y, x = f // 8, f // 4 % 2, f % 4
            grads[BY_BITS.index(z * 4 + x), y * 9 + t] = total[f * rows : (f + 1) * rows, :]


def conv_kernel(
    mask,
    conv_pieces,
    pieces,
    windows_own,
    windows_pair,
    residual_own,
    residual_pair,
    wide,
    skip,
    part,
    conv,
    down,
):
    half = wide.shape[2]
    rows = conv_pieces.shape[2]
    middle = wide.shape[1] // 2
    for f in range(32):
        z, y, x = f // 8, f // 4 % 2, f % 4
        for t in range(9):
            conv[t, f * rows : (f + 1) * rows, :] = conv_pieces[z * 4 + x, y * 9 + t]
    gather_down(pieces, down)
    total = None
    for k in range(4):
        for first, windows, residual in (
            (0, windows_own, residual_own),
            (middle, windows_pair, residual_pair),
        ):
            convolved = None
            for t in range(9):
                v = (k // 2 + t // 3) * 4 + k % 2 + t % 3
                term = dot(windows[v], conv[t], 1, 0)
                convolved = term if convolved is None else convolved + term
            kept = mask[first : first + middle, :]
            kept = jnp.concatenate([kept] * (half // mask.shape[1]), axis=1)
            masked = (residual[k].astype(F32) + convolved) * kept
            wide[k, first : first + middle, :] = masked
            skip[k, first : first + middle, :] = masked.astype(BF)
        term = dot(skip[k], down[k], 1, 0)
        total = term if total is None else total + term
    part[...] = total


def output_kernel(
    extent,
    loss_scale,
    meta,
    mask,
    own,
    got,
    wide,
    skip,
    glow,
    folded,
    pieces,
    back0,
    back1,
    back2,
    back3,
    grads,
    low,
    up,
    outputs,
    raw,
    returning,
):
    side = extent // 2
    quarter = side * side
    half = wide.shape[2]
    rows = grads.shape[2]
    images = wide.shape[1] // quarter
    gather_up(pieces, up)
    low[...] = swapped_sum(own, got)
    kept = jnp.concatenate([mask[...]] * (half // mask.shape[1]), axis=1)
    for k in range(4):
        outputs[k] = (wide[k] + dot(low[...], up[k], 1, 0)) * kept
    returning[...] = jnp.zeros_like(returning)

    def one(g, carry):
        slot = meta[16 + g]
        for k in range(4):
            for i in range(side):
                first = pl.multiple_of(g * quarter + i * side, side)
                put_every_second(raw, 2 * i + k // 2, k % 2, outputs[k, pl.ds(first, side), :])
        for row in range(extent):
            returning[slot, row * extent : (row + 1) * extent, :] = get_line(raw, row).astype(BF)
        return carry

    lax.fori_loop(0, images, one, 0)
    slots = back0.shape[0]
    for r, back in enumerate((back0, back1, back2, back3)):
        back[...] = returning[r * slots : (r + 1) * slots]
    turned = low[...].astype(F32).T.astype(BF)
    for k in range(4):
        scaled = (folded[k].astype(F32) * loss_scale).astype(BF)
        grad = dot(turned, scaled, 1, 0).astype(BF)
        for f in range(32):
            z, y, x = f // 8, f // 4 % 2, f % 4
            grads[DIAGONAL.index(z * 4 + x), y * 4 + k] = grad[f * rows : (f + 1) * rows, :]
        grad = dot(skip[k].astype(F32).T.astype(BF), glow[...], 1, 0).astype(BF)
        for x in range(4):
            for unit in range(8):
                side_of, step = unit // 4, unit % 4
                first = (x * 4 + step) * rows
                grads[DIAGONAL.index(k * 4 + x), 8 + unit] = grad[
                    first : first + rows, side_of * half : (side_of + 1) * half
                ]


def replicas(number, half):
    for r in range(4):
        chip, core = number // 2, number % 2
        chip = 1 - chip if r // 2 else chip
        core = 1 - core if r % 2 else core
        yield r, chip, pl.ds(pl.multiple_of(core * half, half), half)


def split_kernel(number, cot, out0, out1, out2, out3):
    outs = (out0, out1, out2, out3)
    slots, _, half = out0.shape
    for r, chip, lanes in replicas(number[0], half):
        outs[r][...] = cot[pl.ds(chip * slots, slots), :, lanes]


def join_kernel(number, back0, back1, back2, back3, out, wide, sem):
    backs = (back0, back1, back2, back3)
    slots, _, half = back0.shape
    copies = []
    for r, chip, lanes in replicas(number[0], half):
        wide[r] = backs[r][...].astype(F32)
        target = out.at[pl.ds(chip * slots, slots), :, lanes]
        copies.append(pltpu.make_async_copy(wide.at[r], target, sem.at[r]))
        copies[-1].start()
    for copy in copies:
        copy.wait()


def per_device(
    images, routes, bucket, heights, widths, w_conv, w_down, w_up, norm_gain, norm_shift, cotangent
):
    count, extent, _, channels = images.shape
    half = channels // 2
    pixels = extent * extent
    quarter = pixels // 4
    most = cotangent.shape[0] // 4
    rows = w_conv.shape[0]
    low_rows = 2 * count * quarter
    loss_scale = 1.0 / math.sqrt(count * 128 * pixels)
    dp, fsdp = lax.axis_index("dp"), lax.axis_index("fsdp")
    core, y = dp % 2, fsdp // 4 % 2

    conv_own = lax.dynamic_slice_in_dim(w_conv, core * half, half, axis=2).transpose(1, 0, 2)
    up_own = lax.dynamic_slice_in_dim(
        w_up.reshape(rows, 4, channels), core * half, half, axis=2
    ).transpose(1, 0, 2)
    down_own = w_down.reshape(4 * rows, 2, half).transpose(1, 0, 2).reshape(8, rows, half)
    packed = jnp.concatenate([up_own, down_own, conv_own])
    other = send(packed, "y")

    block = jax.ShapeDtypeStruct((2 * most, pixels, half), BF)
    number = dp.astype(I32).reshape(1)
    outgoing = kernel_call(
        split_kernel,
        (block,) * 4,
        flops=0,
        moved_bytes=4 * cotangent.size,
        in_specs=[SCALARS, WHOLE],
        out_specs=(WHOLE,) * 4,
    )(number, cotangent.reshape(4 * most, pixels, channels))
    outgoing, other = lax.optimization_barrier((outgoing, other))
    arrived = over_dp(outgoing)
    first = jnp.where(y == 0, packed, other)
    second = jnp.where(y == 0, other, packed)
    down_kept = jnp.where(core == 0, first[4:12], second[4:12])
    up_down = jnp.concatenate([first[:4], second[:4], down_kept])
    conv_two = jnp.concatenate([first[12:], second[12:]])
    up_down = over_plane(jnp.broadcast_to(up_down, (16, *up_down.shape)), BY_BITS)
    conv_two = lax.all_gather(conv_two, "fsdp", axis_index_groups=PLANES)

    images_pair = send(images, "c")
    ids = jnp.concatenate([routes, bucket[:, None]], axis=1)
    ids_pair = send(ids, "c")

    def described(table, side):
        target = table[:, 0]
        position = jnp.arange(count, dtype=I32)
        earlier = position[None, :] < position[:, None]
        same_owner = target[:, None] == target[None, :]
        order_in = jnp.sum((same_owner & earlier).astype(I32), axis=1)
        slot = (target ^ dp) * 2 * most + side * most + order_in
        chosen = table[:, 1][:, None] == jnp.arange(heights.shape[0], dtype=I32)[None, :]
        height = jnp.sum(jnp.where(chosen, heights[None, :], 0), axis=1)
        width = jnp.sum(jnp.where(chosen, widths[None, :], 0), axis=1)
        return jnp.stack([height, width, slot])

    def numbers(first, second):
        parts = jnp.concatenate([first, second], axis=1).reshape(-1)
        return jnp.concatenate([parts, jnp.broadcast_to(core, (8,)).astype(I32)])

    own_facts, pair_facts = described(ids, core), described(ids_pair, 1 - core)
    own_meta = numbers(own_facts, own_facts)
    pair_meta = numbers(pair_facts, pair_facts)
    meta = numbers(own_facts, pair_facts)
    height, width = meta[:8], meta[8:16]
    place = jnp.arange(extent // 2, dtype=I32) * 2
    mask = (place[None, :, None] < height[:, None, None]) & (
        place[None, None, :] < width[:, None, None]
    )
    mask = jnp.broadcast_to(mask.astype(F32).reshape(low_rows, 1), (low_rows, min(128, half)))

    windows_own, residual_own = normed_windows(own_meta, images, norm_gain, norm_shift)
    windows_pair, residual_pair = normed_windows(pair_meta, images_pair, norm_gain, norm_shift)

    ready, mask, windows_own, windows_pair = lax.optimization_barrier(
        (meta, mask, windows_own, windows_pair)
    )
    folded, glow_part = kernel_call(
        functools.partial(glow_kernel, extent, loss_scale),
        (
            jax.ShapeDtypeStruct((4, low_rows, half), BF),
            jax.ShapeDtypeStruct((low_rows, channels), F32),
        ),
        flops=8 * low_rows * channels * half,
        moved_bytes=5 << 20,
        scratch=(
            laned(extent, extent, half),
            pltpu.VMEM((4, channels, half), BF),
            pltpu.VMEM((8 * most, pixels, half), BF),
            pltpu.SemaphoreType.DMA((4,)),
        ),
        in_specs=[SCALARS] + [pl.BlockSpec(memory_space=pl.ANY)] * 4 + [WHOLE],
        out_specs=(WHOLE, WHOLE),
    )(ready, *arrived, up_down)
    glow_got = send(glow_part, "c")

    glow, conv_grads = kernel_call(
        functools.partial(grad_conv_kernel, loss_scale),
        (
            jax.ShapeDtypeStruct((low_rows, channels), BF),
            jax.ShapeDtypeStruct((16, 18, rows, half), BF),
        ),
        flops=80 * low_rows * channels * half,
        moved_bytes=15 << 20,
        scratch=(pltpu.VMEM((4, half, channels), BF), pltpu.VMEM((4, half, low_rows), BF)),
        in_specs=[WHOLE] * 7,
        out_specs=(WHOLE, WHOLE),
    )(mask, glow_part, glow_got, folded, up_down, windows_own, windows_pair)
    conv_grads = over_plane(conv_grads, BY_BITS)
    glow, windows_own, windows_pair = lax.optimization_barrier((glow, windows_own, windows_pair))

    wide, skip, low_part = kernel_call(
        conv_kernel,
        (
            jax.ShapeDtypeStruct((4, low_rows, half), F32),
            jax.ShapeDtypeStruct((4, low_rows, half), BF),
            jax.ShapeDtypeStruct((low_rows, channels), F32),
        ),
        flops=80 * low_rows * channels * half,
        moved_bytes=18 << 20,
        scratch=(pltpu.VMEM((9, channels, half), BF), pltpu.VMEM((4, half, channels), BF)),
        in_specs=[WHOLE] * 7,
        out_specs=(WHOLE,) * 3,
    )(mask, conv_two, up_down, windows_own, windows_pair, residual_own, residual_pair)
    low_got = send(low_part, "c")

    *returning, grads = kernel_call(
        functools.partial(output_kernel, extent, loss_scale),
        (
            *(block,) * 4,
            jax.ShapeDtypeStruct((16, 16, rows, half), BF),
        ),
        flops=24 * low_rows * channels * half,
        moved_bytes=14 << 20,
        scratch=(
            pltpu.VMEM((low_rows, channels), BF),
            pltpu.VMEM((4, channels, half), BF),
            pltpu.VMEM((4, low_rows, half), F32),
            laned(extent, extent, half),
            pltpu.VMEM((8 * most, pixels, half), BF),
        ),
        in_specs=[SCALARS] + [WHOLE] * 8,
        out_specs=(WHOLE,) * 5,
    )(meta, mask, low_part, low_got, wide, skip, glow, folded, up_down)
    returned = over_dp(returning)
    grads = over_plane(grads, DIAGONAL)

    conv_sum = jnp.sum(conv_grads.astype(F32), axis=0).reshape(2, 9, rows, half)
    grads_sum = jnp.sum(grads.astype(F32), axis=0)
    up_sum, down_sum = grads_sum[:8].reshape(2, 4, rows, half), grads_sum[8:]
    down_sum = jnp.broadcast_to(down_sum, (2, *down_sum.shape))
    shares = jnp.concatenate([conv_sum, up_sum, down_sum], axis=1)
    shares, returned = lax.optimization_barrier((shares, returned))
    own, pair = over_column(shares, y)

    def by_core(first, last):
        parts = (own[first:last], pair[first:last])
        both = jnp.where(core == 0, jnp.stack(parts), jnp.stack(parts[::-1]))
        return both.transpose(2, 1, 0, 3)

    out_conv = by_core(0, 9).reshape(rows, 9, channels)
    out_up = by_core(9, 13).reshape(rows, 4 * channels)
    out_down = jnp.where(y == core, own[13:], pair[13:])
    out_down = out_down.reshape(2, 4 * rows, half).transpose(1, 0, 2).reshape(4 * rows, channels)

    block_out = kernel_call(
        join_kernel,
        jax.ShapeDtypeStruct((4 * most, pixels, channels), F32),
        flops=0,
        moved_bytes=6 * cotangent.size,
        scratch=(pltpu.VMEM((4, 2 * most, pixels, half), F32), pltpu.SemaphoreType.DMA((4,))),
        in_specs=[SCALARS] + [WHOLE] * 4,
        out_specs=pl.BlockSpec(memory_space=pl.ANY),
    )(number, *returned)
    return (block_out.reshape(cotangent.shape), out_conv, out_down, out_up)


def solution(mesh):
    return jax.shard_map(
        per_device,
        mesh=mesh,
        in_specs=(
            P(("dp", "fsdp"), None, None, None),
            P(("dp", "fsdp"), None),
            P(("dp", "fsdp")),
            P(),
            P(),
            P("fsdp", None, None),
            P("fsdp", None),
            P("fsdp", None),
            P(),
            P(),
            P(("dp", "fsdp"), None, None, None),
        ),
        out_specs=(
            P(("dp", "fsdp"), None, None, None),
            P("fsdp", None, None),
            P("fsdp", None),
            P("fsdp", None),
        ),
        check_vma=False,
    )
```

```python
import functools
import math

import jax
import jax.numpy as jnp
from jax import lax
from jax.experimental import pallas as pl
from jax.experimental.pallas import tpu as pltpu
from jax.sharding import PartitionSpec as P

GROUPS = 32
epsilon = 1e-05
BF = jnp.bfloat16
F32 = jnp.float32
I32 = jnp.int32
AXES = ("dp", "fsdp")
VMEM_BYTES = 56 * 1024 * 1024


def moved(fn):
    pairs = []
    for index in range(128):
        dp, fsdp = index // 32, index % 32
        place = (dp // 2, dp % 2, fsdp // 8, fsdp // 4 % 2, fsdp % 4)
        h, c, z, y, x = fn(*place)
        pairs.append((index, (h * 2 + c) * 32 + z * 8 + y * 4 + x))
    return pairs


STEP = {
    "y": moved(lambda h, c, z, y, x: (h, c, z, 1 - y, x)),
    "hy": moved(lambda h, c, z, y, x: (1 - h, c, z, 1 - y, x)),
    "c": moved(lambda h, c, z, y, x: (h, 1 - c, z, y, x)),
    "h": moved(lambda h, c, z, y, x: (1 - h, c, z, y, x)),
    "hc": moved(lambda h, c, z, y, x: (1 - h, 1 - c, z, y, x)),
}
BY_BITS = [(r >> 3 & 1) * 8 + (r >> 1 & 1) * 4 + (r >> 2 & 1) * 2 + (r & 1) for r in range(16)]
DIAGONAL = [r % 4 * 4 + (r // 4 + r) % 4 for r in range(16)]
PLANES = [[z * 8 + y * 4 + x for z in range(4) for x in range(4)] for y in range(2)]


def send(value, move):
    return lax.ppermute(value, AXES, STEP[move])


def over_dp(blocks):
    own, beside, across, both = blocks
    return (own, send(beside, "c"), send(across, "h"), send(both, "hc"))


def over_column(parts, y):
    kept = lax.dynamic_index_in_dim(parts, y, axis=0, keepdims=False)
    given = lax.dynamic_index_in_dim(parts, 1 - y, axis=0, keepdims=False)
    sent = given.astype(BF)
    got = (send(sent, "y"), send(kept.astype(BF), "h"), send(sent, "hy"))
    total = kept + got[0].astype(F32) + got[1].astype(F32) + got[2].astype(F32)
    return total, send(total, "c")


def over_plane(blocks, order=tuple(range(16))):
    groups = [[plane[place] for place in order] for plane in PLANES]
    return lax.all_to_all(
        blocks, "fsdp", split_axis=0, concat_axis=0, axis_index_groups=groups, tiled=True
    )


def dot(left, right, left_dim, right_dim):
    return lax.dot_general(
        left, right, (((left_dim,), (right_dim,)), ((), ())), preferred_element_type=F32
    )


def kernel_call(body, out_shape, flops, moved_bytes, scratch=(), **more):
    return pl.pallas_call(
        body,
        out_shape=out_shape,
        scratch_shapes=list(scratch),
        compiler_params=pltpu.CompilerParams(vmem_limit_bytes=VMEM_BYTES),
        cost_estimate=pl.CostEstimate(
            flops=int(flops), bytes_accessed=int(moved_bytes), transcendentals=0
        ),
        **more,
    )


def laned(extent_rows, extent_columns, lanes):
    block = min(128, lanes)
    return pltpu.VMEM((lanes // block, extent_rows, extent_columns, block), F32)


def put_line(ref, row, first, values):
    block = ref.shape[3]
    for b in range(ref.shape[0]):
        ref[b, row, first : first + values.shape[0], :] = values[:, b * block : (b + 1) * block]


def get_line(ref, row):
    return jnp.concatenate([ref[b, row] for b in range(ref.shape[0])], axis=1)


def every_second(ref, row, first, side):
    places = [
        ref[pl.ds(b, 1), pl.ds(row, 1), pl.ds(first, side, stride=2), :].reshape(side, ref.shape[3])
        for b in range(ref.shape[0])
    ]
    return jnp.concatenate(places, axis=1)


def put_every_second(ref, row, first, values):
    side, block = values.shape[0], ref.shape[3]
    for b in range(ref.shape[0]):
        ref[pl.ds(b, 1), pl.ds(row, 1), pl.ds(first, side, stride=2), :] = values[
            :, b * block : (b + 1) * block
        ].reshape(1, 1, side, block)


WHOLE = pl.BlockSpec(memory_space=pltpu.VMEM)
SCALARS = pl.BlockSpec(memory_space=pltpu.SMEM)


def over_group(sums, width):
    lane = lax.broadcasted_iota(I32, sums.shape, 1)
    step = width // 2
    while step:
        lower = (lane & step) == 0
        lanes = sums.shape[1]
        sums = sums + jnp.where(
            lower, pltpu.roll(sums, lanes - step, 1), pltpu.roll(sums, step, 1)
        )
        step //= 2
    return sums


def norm_kernel(extent, meta, image, gain, shift, windows, residual, padded, raw):
    place = pl.program_id(0)
    channels = image.shape[2]
    half = channels // 2
    height, width = meta[place], meta[8 + place]
    core = meta[24]

    @pl.when(place == 0)
    def _():
        padded[...] = jnp.zeros_like(padded)

    inside = lax.broadcasted_iota(I32, (extent, channels), 0) < width

    def line(row):
        return image[0, row * extent : (row + 1) * extent, :].astype(F32)

    def mask(row):
        return (inside & (row < height)).astype(F32)

    group = channels // GROUPS
    counted = jnp.maximum((height * width * group).astype(F32), 1.0)
    total = jnp.zeros((extent, channels), F32)
    for row in range(extent):
        total = total + line(row) * mask(row)
    total = jnp.broadcast_to(jnp.sum(total, axis=0, keepdims=True), (8, channels))
    mean = (over_group(total, group) / counted)[:1]
    total = jnp.zeros((extent, channels), F32)
    for row in range(extent):
        centred = (line(row) - mean) * mask(row)
        total = total + centred * centred
    total = jnp.broadcast_to(jnp.sum(total, axis=0, keepdims=True), (8, channels))
    variance = (over_group(total, group) / counted)[:1]
    scale = lax.rsqrt(variance + epsilon) * gain[...]
    for row in range(extent):
        normed = (line(row) - mean) * scale + shift[...]
        put_line(padded, row + 1, 8, normed / (1.0 + jnp.exp(-normed)) * mask(row))
        residue = image[
            0, row * extent : (row + 1) * extent, pl.ds(pl.multiple_of(core * half, half), half)
        ]
        put_line(raw, row, 0, residue.astype(F32))
    side = extent // 2
    for p in range(4):
        for q in range(4):
            for i in range(0, side, 2):
                pair = [every_second(padded, 2 * n + p, 7 + q, side) for n in (i, i + 1)]
                windows[p * 4 + q, i * side : (i + 2) * side, :] = jnp.concatenate(pair).astype(BF)
    for k in range(4):
        for i in range(0, side, 2):
            pair = [every_second(raw, 2 * n + k // 2, k % 2, side) for n in (i, i + 1)]
            residual[k, i * side : (i + 2) * side, :] = jnp.concatenate(pair).astype(BF)


def normed_windows(meta, images, gain, shift):
    count, extent, _, channels = images.shape
    pixels, half = extent * extent, channels // 2
    quarter = pixels // 4
    return kernel_call(
        functools.partial(norm_kernel, extent),
        (
            jax.ShapeDtypeStruct((16, count * quarter, channels), BF),
            jax.ShapeDtypeStruct((4, count * quarter, half), BF),
        ),
        flops=40 * images.size,
        moved_bytes=12 * images.size,
        scratch=(
            laned(extent + 2, extent + 16, channels),
            laned(extent, extent, half),
        ),
        grid=(count,),
        in_specs=[
            SCALARS,
            pl.BlockSpec((1, pixels, channels), lambda g: (g, 0, 0)),
            pl.BlockSpec((1, channels), lambda g: (0, 0)),
            pl.BlockSpec((1, channels), lambda g: (0, 0)),
        ],
        out_specs=(
            pl.BlockSpec((16, quarter, channels), lambda g: (0, g, 0)),
            pl.BlockSpec((4, quarter, half), lambda g: (0, g, 0)),
        ),
    )(meta, images.reshape(count, pixels, channels), gain[None, :], shift[None, :])


def gather_up(pieces, up):
    rows = pieces.shape[2]
    for f in range(32):
        z, y, x = f // 8, f // 4 % 2, f % 4
        for k in range(4):
            up[k, f * rows : (f + 1) * rows, :] = pieces[DIAGONAL.index(z * 4 + x), y * 4 + k]


def gather_down(pieces, down):
    rows, half = pieces.shape[2:]
    for z in range(4):
        for x in range(4):
            for unit in range(8):
                side, step = unit // 4, unit % 4
                first = (x * 4 + step) * rows
                down[z, first : first + rows, side * half : (side + 1) * half] = pieces[
                    DIAGONAL.index(z * 4 + x), 8 + unit
                ]


def swapped_sum(own, got):
    middle = own.shape[0] // 2
    return jnp.concatenate(
        [own[:middle] + got[middle:], own[middle:] + got[:middle]], axis=0
    ).astype(BF)


def glow_kernel(
    extent, loss_scale, meta, cot0, cot1, cot2, cot3, pieces, folded, part, raw, up, cot, sem
):
    side = extent // 2
    quarter = side * side
    half = cot.shape[2]
    slots = cot0.shape[0]
    copies = [
        pltpu.make_async_copy(ref, cot.at[pl.ds(r * slots, slots)], sem.at[r])
        for r, ref in enumerate((cot0, cot1, cot2, cot3))
    ]
    for copy in copies:
        copy.start()
    gather_up(pieces, up)
    for copy in copies:
        copy.wait()
    images = folded.shape[1] // quarter
    inside = lax.broadcasted_iota(I32, (extent, half), 0)

    def one(g, carry):
        height, width, slot = meta[g], meta[8 + g], meta[16 + g]
        for row in range(extent):
            kept = ((inside < width) & (row < height)).astype(F32)
            line = cot[slot, row * extent : (row + 1) * extent, :].astype(F32)
            put_line(raw, row, 0, line * kept)
        for k in range(4):
            for i in range(0, side, 2):
                pair = [every_second(raw, 2 * n + k // 2, k % 2, side) for n in (i, i + 1)]
                first = pl.multiple_of(g * quarter + i * side, 2 * side)
                folded[k, pl.ds(first, 2 * side), :] = jnp.concatenate(pair).astype(BF)
        return carry

    lax.fori_loop(0, images, one, 0)
    total = None
    for k in range(4):
        scaled = (folded[k].astype(F32) * loss_scale).astype(BF)
        term = dot(scaled, up[k], 1, 1)
        total = term if total is None else total + term
    part[...] = total


def grad_conv_kernel(
    loss_scale, mask, own, got, folded, pieces, windows_own, windows_pair, glow, grads, down, turned
):
    half = folded.shape[2]
    rows = grads.shape[2]
    middle = folded.shape[1] // 2
    gather_down(pieces, down)
    glow[...] = swapped_sum(own, got)
    kept = jnp.concatenate([mask[...]] * (half // mask.shape[1]), axis=1)
    for k in range(4):
        grad = folded[k].astype(F32) * loss_scale + dot(glow[...], down[k], 1, 1)
        turned[k] = (grad * kept).T.astype(BF)
    for t in range(9):
        total = None
        for k in range(4):
            v = (k // 2 + t // 3) * 4 + k % 2 + t % 3
            for columns, windows in ((slice(0, middle), windows_own), (slice(middle, None), windows_pair)):
                term = dot(turned[k, :, columns], windows[v], 1, 0)
                total = term if total is None else total + term
        total = total.T.astype(BF)
        for f in range(32):
            z, y, x = f // 8, f // 4 % 2, f % 4
            grads[BY_BITS.index(z * 4 + x), y * 9 + t] = total[f * rows : (f + 1) * rows, :]


def conv_kernel(
    mask,
    conv_pieces,
    pieces,
    windows_own,
    windows_pair,
    residual_own,
    residual_pair,
    wide,
    skip,
    part,
    conv,
    down,
):
    half = wide.shape[2]
    rows = conv_pieces.shape[2]
    middle = wide.shape[1] // 2
    for f in range(32):
        z, y, x = f // 8, f // 4 % 2, f % 4
        for t in range(9):
            conv[t, f * rows : (f + 1) * rows, :] = conv_pieces[z * 4 + x, y * 9 + t]
    gather_down(pieces, down)
    total = None
    for k in range(4):
        for first, windows, residual in (
            (0, windows_own, residual_own),
            (middle, windows_pair, residual_pair),
        ):
            convolved = None
            for t in range(9):
                v = (k // 2 + t // 3) * 4 + k % 2 + t % 3
                term = dot(windows[v], conv[t], 1, 0)
                convolved = term if convolved is None else convolved + term
            kept = mask[first : first + middle, :]
            kept = jnp.concatenate([kept] * (half // mask.shape[1]), axis=1)
            masked = (residual[k].astype(F32) + convolved) * kept
            wide[k, first : first + middle, :] = masked
            skip[k, first : first + middle, :] = masked.astype(BF)
        term = dot(skip[k], down[k], 1, 0)
        total = term if total is None else total + term
    part[...] = total


def output_kernel(
    extent,
    loss_scale,
    meta,
    mask,
    own,
    got,
    wide,
    skip,
    glow,
    folded,
    pieces,
    back0,
    back1,
    back2,
    back3,
    grads,
    low,
    up,
    outputs,
    raw,
    returning,
):
    side = extent // 2
    quarter = side * side
    half = wide.shape[2]
    rows = grads.shape[2]
    images = wide.shape[1] // quarter
    gather_up(pieces, up)
    low[...] = swapped_sum(own, got)
    kept = jnp.concatenate([mask[...]] * (half // mask.shape[1]), axis=1)
    for k in range(4):
        outputs[k] = (wide[k] + dot(low[...], up[k], 1, 0)) * kept
    returning[...] = jnp.zeros_like(returning)

    def one(g, carry):
        slot = meta[16 + g]
        for k in range(4):
            for i in range(side):
                first = pl.multiple_of(g * quarter + i * side, side)
                put_every_second(raw, 2 * i + k // 2, k % 2, outputs[k, pl.ds(first, side), :])
        for row in range(extent):
            returning[slot, row * extent : (row + 1) * extent, :] = get_line(raw, row).astype(BF)
        return carry

    lax.fori_loop(0, images, one, 0)
    slots = back0.shape[0]
    for r, back in enumerate((back0, back1, back2, back3)):
        back[...] = returning[r * slots : (r + 1) * slots]
    turned = low[...].astype(F32).T.astype(BF)
    for k in range(4):
        scaled = (folded[k].astype(F32) * loss_scale).astype(BF)
        grad = dot(turned, scaled, 1, 0).astype(BF)
        for f in range(32):
            z, y, x = f // 8, f // 4 % 2, f % 4
            grads[DIAGONAL.index(z * 4 + x), y * 4 + k] = grad[f * rows : (f + 1) * rows, :]
        grad = dot(skip[k].astype(F32).T.astype(BF), glow[...], 1, 0).astype(BF)
        for x in range(4):
            for unit in range(8):
                side_of, step = unit // 4, unit % 4
                first = (x * 4 + step) * rows
                grads[DIAGONAL.index(k * 4 + x), 8 + unit] = grad[
                    first : first + rows, side_of * half : (side_of + 1) * half
                ]


def replicas(number, half):
    for r in range(4):
        chip, core = number // 2, number % 2
        chip = 1 - chip if r // 2 else chip
        core = 1 - core if r % 2 else core
        yield r, chip, pl.ds(pl.multiple_of(core * half, half), half)


def split_kernel(number, cot, out0, out1, out2, out3):
    outs = (out0, out1, out2, out3)
    slots, _, half = out0.shape
    for r, chip, lanes in replicas(number[0], half):
        outs[r][...] = cot[pl.ds(chip * slots, slots), :, lanes]


def join_kernel(number, back0, back1, back2, back3, out, wide, sem):
    backs = (back0, back1, back2, back3)
    slots, _, half = back0.shape
    copies = []
    for r, chip, lanes in replicas(number[0], half):
        wide[r] = backs[r][...].astype(F32)
        target = out.at[pl.ds(chip * slots, slots), :, lanes]
        copies.append(pltpu.make_async_copy(wide.at[r], target, sem.at[r]))
        copies[-1].start()
    for copy in copies:
        copy.wait()


def per_device(
    images, routes, bucket, heights, widths, w_conv, w_down, w_up, norm_gain, norm_shift, cotangent
):
    count, extent, _, channels = images.shape
    half = channels // 2
    pixels = extent * extent
    quarter = pixels // 4
    most = cotangent.shape[0] // 4
    rows = w_conv.shape[0]
    low_rows = 2 * count * quarter
    loss_scale = 1.0 / math.sqrt(count * 128 * pixels)
    dp, fsdp = lax.axis_index("dp"), lax.axis_index("fsdp")
    core, y = dp % 2, fsdp // 4 % 2

    conv_own = lax.dynamic_slice_in_dim(w_conv, core * half, half, axis=2).transpose(1, 0, 2)
    up_own = lax.dynamic_slice_in_dim(
        w_up.reshape(rows, 4, channels), core * half, half, axis=2
    ).transpose(1, 0, 2)
    down_own = w_down.reshape(4 * rows, 2, half).transpose(1, 0, 2).reshape(8, rows, half)
    packed = jnp.concatenate([up_own, down_own, conv_own])
    other = send(packed, "y")

    block = jax.ShapeDtypeStruct((2 * most, pixels, half), BF)
    number = dp.astype(I32).reshape(1)
    outgoing = kernel_call(
        split_kernel,
        (block,) * 4,
        flops=0,
        moved_bytes=4 * cotangent.size,
        in_specs=[SCALARS, WHOLE],
        out_specs=(WHOLE,) * 4,
    )(number, cotangent.reshape(4 * most, pixels, channels))
    outgoing, other = lax.optimization_barrier((outgoing, other))
    arrived = over_dp(outgoing)
    first = jnp.where(y == 0, packed, other)
    second = jnp.where(y == 0, other, packed)
    down_kept = jnp.where(core == 0, first[4:12], second[4:12])
    up_down = jnp.concatenate([first[:4], second[:4], down_kept])
    conv_two = jnp.concatenate([first[12:], second[12:]])
    up_down = over_plane(jnp.broadcast_to(up_down, (16, *up_down.shape)), DIAGONAL)
    conv_two = lax.all_gather(conv_two, "fsdp", axis_index_groups=PLANES)

    images_pair = send(images, "c")
    ids = jnp.concatenate([routes, bucket[:, None]], axis=1)
    ids_pair = send(ids, "c")

    def described(table, side):
        target = table[:, 0]
        position = jnp.arange(count, dtype=I32)
        earlier = position[None, :] < position[:, None]
        same_owner = target[:, None] == target[None, :]
        order_in = jnp.sum((same_owner & earlier).astype(I32), axis=1)
        slot = (target ^ dp) * 2 * most + side * most + order_in
        chosen = table[:, 1][:, None] == jnp.arange(heights.shape[0], dtype=I32)[None, :]
        height = jnp.sum(jnp.where(chosen, heights[None, :], 0), axis=1)
        width = jnp.sum(jnp.where(chosen, widths[None, :], 0), axis=1)
        return jnp.stack([height, width, slot])

    def numbers(first, second):
        parts = jnp.concatenate([first, second], axis=1).reshape(-1)
        return jnp.concatenate([parts, jnp.broadcast_to(core, (8,)).astype(I32)])

    own_facts, pair_facts = described(ids, core), described(ids_pair, 1 - core)
    own_meta = numbers(own_facts, own_facts)
    pair_meta = numbers(pair_facts, pair_facts)
    meta = numbers(own_facts, pair_facts)
    height, width = meta[:8], meta[8:16]
    place = jnp.arange(extent // 2, dtype=I32) * 2
    mask = (place[None, :, None] < height[:, None, None]) & (
        place[None, None, :] < width[:, None, None]
    )
    mask = jnp.broadcast_to(mask.astype(F32).reshape(low_rows, 1), (low_rows, min(128, half)))

    windows_own, residual_own = normed_windows(own_meta, images, norm_gain, norm_shift)
    windows_pair, residual_pair = normed_windows(pair_meta, images_pair, norm_gain, norm_shift)

    ready, mask, windows_own, windows_pair = lax.optimization_barrier(
        (meta, mask, windows_own, windows_pair)
    )
    folded, glow_part = kernel_call(
        functools.partial(glow_kernel, extent, loss_scale),
        (
            jax.ShapeDtypeStruct((4, low_rows, half), BF),
            jax.ShapeDtypeStruct((low_rows, channels), F32),
        ),
        flops=8 * low_rows * channels * half,
        moved_bytes=5 << 20,
        scratch=(
            laned(extent, extent, half),
            pltpu.VMEM((4, channels, half), BF),
            pltpu.VMEM((8 * most, pixels, half), BF),
            pltpu.SemaphoreType.DMA((4,)),
        ),
        in_specs=[SCALARS] + [pl.BlockSpec(memory_space=pl.ANY)] * 4 + [WHOLE],
        out_specs=(WHOLE, WHOLE),
    )(ready, *arrived, up_down)
    glow_got = send(glow_part, "c")

    glow, conv_grads = kernel_call(
        functools.partial(grad_conv_kernel, loss_scale),
        (
            jax.ShapeDtypeStruct((low_rows, channels), BF),
            jax.ShapeDtypeStruct((16, 18, rows, half), BF),
        ),
        flops=80 * low_rows * channels * half,
        moved_bytes=15 << 20,
        scratch=(pltpu.VMEM((4, half, channels), BF), pltpu.VMEM((4, half, low_rows), BF)),
        in_specs=[WHOLE] * 7,
        out_specs=(WHOLE, WHOLE),
    )(mask, glow_part, glow_got, folded, up_down, windows_own, windows_pair)
    conv_grads = over_plane(conv_grads, BY_BITS)
    glow, windows_own, windows_pair = lax.optimization_barrier((glow, windows_own, windows_pair))

    wide, skip, low_part = kernel_call(
        conv_kernel,
        (
            jax.ShapeDtypeStruct((4, low_rows, half), F32),
            jax.ShapeDtypeStruct((4, low_rows, half), BF),
            jax.ShapeDtypeStruct((low_rows, channels), F32),
        ),
        flops=80 * low_rows * channels * half,
        moved_bytes=18 << 20,
        scratch=(pltpu.VMEM((9, channels, half), BF), pltpu.VMEM((4, half, channels), BF)),
        in_specs=[WHOLE] * 7,
        out_specs=(WHOLE,) * 3,
    )(mask, conv_two, up_down, windows_own, windows_pair, residual_own, residual_pair)
    low_got = send(low_part, "c")

    *returning, grads = kernel_call(
        functools.partial(output_kernel, extent, loss_scale),
        (
            *(block,) * 4,
            jax.ShapeDtypeStruct((16, 16, rows, half), BF),
        ),
        flops=24 * low_rows * channels * half,
        moved_bytes=14 << 20,
        scratch=(
            pltpu.VMEM((low_rows, channels), BF),
            pltpu.VMEM((4, channels, half), BF),
            pltpu.VMEM((4, low_rows, half), F32),
            laned(extent, extent, half),
            pltpu.VMEM((8 * most, pixels, half), BF),
        ),
        in_specs=[SCALARS] + [WHOLE] * 8,
        out_specs=(WHOLE,) * 5,
    )(meta, mask, low_part, low_got, wide, skip, glow, folded, up_down)
    returned = over_dp(returning)
    grads = over_plane(grads, DIAGONAL)

    conv_sum = jnp.sum(conv_grads.astype(F32), axis=0).reshape(2, 9, rows, half)
    grads_sum = jnp.sum(grads.astype(F32), axis=0)
    up_sum, down_sum = grads_sum[:8].reshape(2, 4, rows, half), grads_sum[8:]
    down_sum = jnp.broadcast_to(down_sum, (2, *down_sum.shape))
    shares = jnp.concatenate([conv_sum, up_sum, down_sum], axis=1)
    shares, returned = lax.optimization_barrier((shares, returned))
    own, pair = over_column(shares, y)

    def by_core(first, last):
        parts = (own[first:last], pair[first:last])
        both = jnp.where(core == 0, jnp.stack(parts), jnp.stack(parts[::-1]))
        return both.transpose(2, 1, 0, 3)

    out_conv = by_core(0, 9).reshape(rows, 9, channels)
    out_up = by_core(9, 13).reshape(rows, 4 * channels)
    out_down = jnp.where(y == core, own[13:], pair[13:])
    out_down = out_down.reshape(2, 4 * rows, half).transpose(1, 0, 2).reshape(4 * rows, channels)

    block_out = kernel_call(
        join_kernel,
        jax.ShapeDtypeStruct((4 * most, pixels, channels), F32),
        flops=0,
        moved_bytes=6 * cotangent.size,
        scratch=(pltpu.VMEM((4, 2 * most, pixels, half), F32), pltpu.SemaphoreType.DMA((4,))),
        in_specs=[SCALARS] + [WHOLE] * 4,
        out_specs=pl.BlockSpec(memory_space=pl.ANY),
    )(number, *returned)
    return (block_out.reshape(cotangent.shape), out_conv, out_down, out_up)


def solution(mesh):
    return jax.shard_map(
        per_device,
        mesh=mesh,
        in_specs=(
            P(("dp", "fsdp"), None, None, None),
            P(("dp", "fsdp"), None),
            P(("dp", "fsdp")),
            P(),
            P(),
            P("fsdp", None, None),
            P("fsdp", None),
            P("fsdp", None),
            P(),
            P(),
            P(("dp", "fsdp"), None, None, None),
        ),
        out_specs=(
            P(("dp", "fsdp"), None, None, None),
            P("fsdp", None, None),
            P("fsdp", None),
            P("fsdp", None),
        ),
        check_vma=False,
    )
```
